32 devices in a mesh: row: 8 (over z, core), col: 4 (over y, x).
Axes of the slice: x: 2, y: 2, z: 4, core: 2. Of those that a mesh axis runs over, the one named last changes fastest.
Arguments:
- vectors: float32 [12288, 128], P(('row', 'col')), may hold values from -6 to 6
- energies: float32 [12288], P(('row', 'col')), may hold values from 1 to 3
- intersections: bfloat16 [96, 512, 128], P(('row', 'col')), may hold values from -0.25 to 0.25
- coarse: bfloat16 [8, 8, 512, 512], P('col', 'row'), may hold values from -0.15625 to 0.15625
- fine_coarse: int32 [96], replicated, may hold values from 0 to 7, as said below
- coarse_slot: int32 [8], replicated, may hold values from 0 to 7, each once
- tile_codes: int32 [32, 96], P(('row', 'col')), may hold values from 0 to 287, as said below
- tile_count: int32 [32], P(('row', 'col')), may hold values from 12 to 96, as said below
Outputs:
- first_step: float32 [12288, 128], P(('row', 'col'))
- second_step: float32 [12288, 128], P(('row', 'col'))
The draws below stay inside these ranges and needn't reach their ends.
Inputs may be any that keep to these rules, and one draw needn't show every extreme that they name: `fine_coarse`: fine block k lies on device d = k // 3; with c = d % (4) its coarse k-point lies in c * 2 to (c + 1) * 2 - 1. `coarse_slot`: each coarse k-point has its own position. `tile_codes`: each row lists distinct codes; a code e stands for output position e // (C 3) and input position e % (C 3) of the device's lists, with C = 4. Only the first tile_count[d] codes of row d are used; some device uses all 96.
All inputs are finite; a program needn't handle non-finite values.
Results may differ from the reference program's by a relative error of at most 0.0044.
Values may be sent and summed in bfloat16 or wider, within the bound.
No kernel may reach another device: no remote copies, remote signals or barrier semaphores. Data moves between devices by JAX's collectives and lax.ppermute only.
A program may use at most 128 MiB of HBM per device.

```python
import jax
import jax.numpy as jnp
from jax import lax

TILE = 128
CP = 512
NV = 128
CKC = 2
BLK_DEV = 3
NB = 96
ORDER = 12288
NCK = 8
TILE_MAX = 96
N_ROW = 8
N_COL = 4
DEVICES = 32


def draw_fine_coarse(key, part):
    block_ids = jnp.arange(NB, dtype=jnp.int32)
    column = block_ids // BLK_DEV % (NCK // CKC)
    offsets = jax.random.randint(jax.random.fold_in(key, 7), (NB,), 0, CKC, dtype=jnp.int32)
    return (column * CKC + offsets).astype(jnp.int32)


def draw_tile_codes(key, part):
    device_keys = jax.random.split(jax.random.fold_in(key, 11), DEVICES)

    def draw_row(row_key):
        return jax.random.permutation(row_key, DEVICES * BLK_DEV * BLK_DEV)[:TILE_MAX].astype(jnp.int32)
    return jax.vmap(draw_row)(device_keys)


def draw_tile_count(key, part):
    count_key, pick_key = jax.random.split(jax.random.fold_in(key, 23))
    base = TILE_MAX // 8 + jax.random.randint(count_key, (DEVICES,), 0, TILE_MAX // 2 + 1, dtype=jnp.int32)
    busiest = jax.random.randint(pick_key, (), 0, DEVICES, dtype=jnp.int32)
    return jnp.where(jnp.arange(DEVICES, dtype=jnp.int32) == busiest, TILE_MAX, base).astype(jnp.int32)


def block_scale(own_key, dims, cuts, smallest, largest):
    loudness, own = 1.0, jax.random.fold_in(own_key, 6)
    for axis_at, parts in cuts:
        draws = jnp.exp(jax.random.uniform(jax.random.fold_in(own, axis_at), (parts,), jnp.float32, smallest / len(cuts), largest / len(cuts)))
        loudness = loudness * jnp.repeat(draws, dims[axis_at] // parts).reshape([-1 if axis == axis_at else 1 for axis in range(len(dims))])
    return loudness


def scatter_about(own_key, extent, deviation, reach, pieces=(), kind=jnp.bfloat16):
    level = block_scale(own_key, extent, pieces, -0.22, 0.18) if pieces else 1.0
    values = jax.random.normal(own_key, extent, jnp.float32) * deviation * level
    return jnp.minimum(jnp.maximum(values, -reach), reach).astype(kind)


def setup_inputs(seed: int = 0) -> dict:
    seeds = jax.random.split(jax.random.key(seed), 9)
    return {
        "vectors": scatter_about(seeds[0], (ORDER, NV), 1.0, 6.0, ((0, 32),), jnp.float32),
        "energies": jnp.clip(1.0 + 2.0 * jax.random.uniform(seeds[1], (ORDER,), jnp.float32) ** block_scale(seeds[1], (ORDER,), ((0, 32),), -0.2, 0.2), 1.0, 3.0),
        "intersections": scatter_about(seeds[2], (NB, CP, TILE), CP ** -0.5, 0.25, ((0, 32),)),
        "coarse": scatter_about(seeds[3], (NCK, NCK, CP, CP), (TILE * NB // 8) ** -0.5, 0.15625, ((0, 4), (1, 8))),
        "fine_coarse": draw_fine_coarse(jax.random.fold_in(seeds[8], 71), 0),
        "coarse_slot": jax.random.permutation(seeds[5], NCK).astype(jnp.int32),
        "tile_codes": draw_tile_codes(jax.random.fold_in(seeds[8], 71), 0),
        "tile_count": draw_tile_count(jax.random.fold_in(seeds[8], 71), 0),
    }


spectrum_center = 2.0
spectrum_half = 3.0


def device_part(device, rounded, intersections, coarse, fine_coarse, coarse_slot, tile_codes, tile_count):
    row_id = device // N_COL
    col_id = device % N_COL
    spread = N_COL * BLK_DEV
    index_out = jnp.arange(N_ROW * BLK_DEV, dtype=jnp.int32)
    index_in = jnp.arange(spread, dtype=jnp.int32)
    out_blocks = (((index_out // BLK_DEV) * N_COL + col_id) * BLK_DEV + index_out % BLK_DEV).astype(jnp.int32)
    in_blocks = ((row_id * N_COL + index_in // BLK_DEV) * BLK_DEV + index_in % BLK_DEV).astype(jnp.int32)
    own_points = (col_id * CKC + jnp.arange(CKC, dtype=jnp.int32)).astype(jnp.int32)
    in_slots = coarse_slot[fine_coarse[in_blocks]].astype(jnp.int32)
    blocks = coarse[own_points[:, None], in_slots[None, :]]
    over_in = intersections[in_blocks]
    projected = jnp.einsum("aicd,idt->aict", blocks.astype(jnp.float32), over_in.astype(jnp.float32)).astype(jnp.bfloat16)
    tile_list = tile_codes[device]
    out_idx = (tile_list // spread).astype(jnp.int32)
    in_idx = (tile_list % spread).astype(jnp.int32)
    out_block = out_blocks[out_idx]
    local_point = (fine_coarse[out_block] - col_id * CKC).astype(jnp.int32)
    right_sel = projected[local_point, in_idx]
    left_over = intersections[out_block]
    fine_tiles = jnp.einsum("kct,kcu->ktu", left_over.astype(jnp.float32), right_sel.astype(jnp.float32)).astype(jnp.bfloat16)
    live_mask = jnp.arange(TILE_MAX, dtype=jnp.int32) < tile_count[device]
    fine_tiles = jnp.where(live_mask[:, None, None], fine_tiles, jnp.zeros_like(fine_tiles))
    inputs = rounded[in_blocks[in_idx]]
    product = jnp.einsum("ktu,kun->ktn", fine_tiles.astype(jnp.float32), inputs.astype(jnp.float32))
    device_sum = jnp.zeros((N_ROW * BLK_DEV, TILE, NV), jnp.float32).at[out_idx].add(product)
    return out_blocks, device_sum


def apply_kernel(field, intersections, coarse, fine_coarse, coarse_slot, tile_codes, tile_count):
    rounded = field.astype(jnp.bfloat16)

    def visit(running, device):
        out_blocks, device_sum = device_part(device, rounded, intersections, coarse, fine_coarse, coarse_slot, tile_codes, tile_count)
        return running.at[out_blocks].add(device_sum), None

    result, _ = lax.scan(visit, jnp.zeros((NB, TILE, NV), jnp.float32), jnp.arange(DEVICES, dtype=jnp.int32))
    return result


def reference(vectors, energies, intersections, coarse, fine_coarse, coarse_slot, tile_codes, tile_count):
    start_vec = vectors.reshape(NB, TILE, NV)
    pair_energy = energies.reshape(NB, TILE, 1)

    def apply_shifted(field):
        kernel_part = apply_kernel(field, intersections, coarse, fine_coarse, coarse_slot, tile_codes, tile_count)
        return (pair_energy * field + kernel_part - spectrum_center * field) / spectrum_half

    first_step = apply_shifted(start_vec)
    second_step = 2.0 * apply_shifted(first_step) - start_vec
    return first_step.reshape(ORDER, NV), second_step.reshape(ORDER, NV)
```

```python
import functools

import jax
import jax.numpy as jnp
from jax import lax
from jax.experimental import pallas as pl
from jax.experimental.pallas import tpu as pltpu
from jax.sharding import PartitionSpec as P

spectrum_center = 2.0
spectrum_half = 3.0
axes = ("row", "col")
chunk_groups = 8
mib = 1 << 20


class Layout:
    def __init__(self, rows, cols, blocks, pairs, side, width, points, slots_dev, tile_max, unroll):
        self.rows, self.cols, self.blocks = rows, cols, blocks
        self.pairs, self.side, self.width = pairs, side, width
        self.points, self.slots_dev, self.tile_max = points, slots_dev, tile_max
        self.places = rows // 2
        self.near = max(self.places // 2, 1)
        self.owners = 2 if self.places > 1 else 1
        self.spread = cols * blocks
        self.inputs = self.owners * self.spread
        self.outputs = rows * blocks
        self.slots = 2 * self.near * slots_dev
        self.unroll = unroll
        most = self.owners * tile_max + self.inputs * (unroll - 1)
        self.groups = -(-most // (unroll * chunk_groups)) * chunk_groups


def plan_kernel(lay, ids, codes, counts, fine, stored, group_start, slot_of, entries, fill):
    place, core, col = ids[0], ids[1], ids[2]
    half = lax.div(place, lay.near)

    def clear(p, carry):
        owner = lax.div(p, lay.spread)
        rest = lax.rem(p, lay.spread)
        from_col = lax.bitwise_xor(lax.div(rest, lay.blocks), col)
        from_place = lax.bitwise_xor(place, owner * lay.near)
        block = ((from_place * 2 + core) * lay.cols + from_col) * lay.blocks + lax.rem(rest, lay.blocks)
        position = stored[fine[block]]
        at_row = lax.div(position, lay.slots_dev)
        at_place, at_core = lax.div(at_row, 2), lax.rem(at_row, 2)
        slot = (lax.bitwise_xor(at_place, place) * 2 + lax.bitwise_xor(at_core, core)) * lay.slots_dev
        slot = slot + lax.rem(position, lay.slots_dev)
        slot_of[p] = jnp.where(lax.div(at_place, lay.near) == half, slot, -1)
        fill[p] = 0
        return carry

    lax.fori_loop(0, lay.inputs, clear, 0)

    def input_of(owner, code):
        j = lax.rem(code, lay.spread)
        from_col = lax.bitwise_xor(lax.div(j, lay.blocks), col)
        return owner * lay.spread + from_col * lay.blocks + lax.rem(j, lay.blocks)

    for owner in range(lay.owners):

        def count(i, carry):
            p = input_of(owner, codes[owner, i])
            fill[p] = fill[p] + 1
            return carry

        lax.fori_loop(0, counts[owner], count, 0)

    def place_groups(p, start):
        group_start[p] = start
        used = jnp.where(slot_of[p] >= 0, fill[p], 0)
        fill[p] = start * lay.unroll
        return start + lax.div(used + (lay.unroll - 1), lay.unroll)

    total = lax.fori_loop(0, lay.inputs, place_groups, 0)
    group_start[lay.inputs] = total

    def blank(i, carry):
        entries[i] = lay.outputs * lay.points
        return carry

    lax.fori_loop(0, total * lay.unroll, blank, 0)

    for owner in range(lay.owners):

        def put(i, carry):
            code = codes[owner, i]
            p = input_of(owner, code)

            @pl.when(slot_of[p] >= 0)
            def _():
                out = lax.div(code, lay.spread)
                at_row = lax.div(out, lay.blocks)
                within = lax.rem(out, lay.blocks)
                far = lax.bitwise_xor(lax.div(at_row, 2), place)
                other = lax.bitwise_xor(lax.rem(at_row, 2), core)
                q = (other * lay.places + far) * lay.blocks + within
                a = fine[(at_row * lay.cols + col) * lay.blocks + within] - col * lay.points
                spot = fill[p]
                entries[spot] = q * lay.points + a
                fill[p] = spot + 1

            return carry

        lax.fori_loop(0, counts[owner], put, 0)


def make_plan(lay, ids, codes, counts, fine, stored):
    smem = pl.BlockSpec(memory_space=pltpu.SMEM)
    return pl.pallas_call(
        functools.partial(plan_kernel, lay),
        out_shape=(
            jax.ShapeDtypeStruct((lay.inputs + 1,), jnp.int32),
            jax.ShapeDtypeStruct((lay.inputs,), jnp.int32),
            jax.ShapeDtypeStruct((lay.groups * lay.unroll,), jnp.int32),
        ),
        in_specs=[smem] * 5,
        out_specs=(smem,) * 3,
        scratch_shapes=[pltpu.SMEM((lay.inputs,), jnp.int32)],
    )(ids, codes, counts, fine, stored)


def add_products(lay, group, entries, tiles, rounded_block, total):
    products = [
        jnp.dot(tiles[i], rounded_block, preferred_element_type=jnp.float32) for i in range(lay.unroll)
    ]
    for i in range(lay.unroll):
        q = lax.div(entries[group * lay.unroll + i], lay.points)
        total[q] = total[q] + products[i]


def tiles_kernel(lay, group_start, slot_of, entries, *refs):
    n_in = lay.owners * lay.cols
    n_out = 2 * lay.places
    n_coarse = 2 * lay.near
    refs = list(refs)
    given_in = [refs.pop(0) for _ in range(n_in)]
    given_out = [refs.pop(0) for _ in range(n_out)]
    given_coarse = [refs.pop(0) for _ in range(n_coarse)]
    given_vec = [refs.pop(0) for _ in range(lay.cols)]
    own_sum, other_sum, tiles_out = refs[:3]
    right, left, blocks, rounded, tiles, projected, total, sems, out_sems = refs[3:]
    copies = []

    def fetch(source, target):
        copies.append(pltpu.make_async_copy(source, target, sems.at[len(copies)]))
        copies[-1].start()

    for i in range(n_coarse):
        for a in range(lay.points):
            fetch(given_coarse[i].at[a], blocks.at[a, pl.ds(i * lay.slots_dev, lay.slots_dev)])
    for i in range(n_in):
        fetch(given_in[i], right.at[pl.ds(i * lay.blocks, lay.blocks)])
    for d in range(lay.cols):
        for g in range(lay.owners):
            fetch(given_vec[d].at[g], rounded.at[pl.ds((g * lay.cols + d) * lay.blocks, lay.blocks)])
    for i in range(n_out):
        fetch(given_out[i], left.at[pl.ds(i * lay.blocks, lay.blocks)])
    total[...] = jnp.zeros_like(total)
    for copy in copies:
        copy.wait()

    def visit(p, carry):
        first, last = group_start[p], group_start[p + 1]

        @pl.when(last > first)
        def _():
            slot = slot_of[p]
            for a in range(lay.points):
                projected[:, a * lay.side : (a + 1) * lay.side] = jnp.dot(
                    blocks[a, slot], right[p], preferred_element_type=jnp.float32
                ).astype(jnp.bfloat16)

            def group_step(group, inner):
                fresh = []
                for i in range(lay.unroll):
                    entry = entries[group * lay.unroll + i]
                    q = jnp.minimum(lax.div(entry, lay.points), lay.outputs - 1)
                    a = lax.rem(entry, lay.points)
                    both = jnp.dot(left[q], projected[...], preferred_element_type=jnp.float32)
                    tile = both[:, : lay.side]
                    for b in range(1, lay.points):
                        tile = jnp.where(a == b, both[:, b * lay.side : (b + 1) * lay.side], tile)
                    fresh.append(tile.astype(jnp.bfloat16))
                for i in range(lay.unroll):
                    tiles[group * lay.unroll + i] = fresh[i]
                add_products(lay, group, entries, fresh, rounded[p], total)
                return inner

            lax.fori_loop(first, last, group_step, 0)

        return carry

    lax.fori_loop(0, lay.inputs, visit, 0)
    used = group_start[lay.inputs]
    span = chunk_groups * lay.unroll

    def store(chunk):
        part = pl.ds(chunk * span, span)
        return pltpu.make_async_copy(tiles.at[part], tiles_out.at[part], out_sems.at[chunk])

    for chunk in range(lay.groups // chunk_groups):

        @pl.when(used > chunk * chunk_groups)
        def _():
            store(chunk).start()

    own = lay.places * lay.blocks
    own_sum[...] = total[0:own]
    other_sum[...] = total[own : 2 * own]
    for chunk in range(lay.groups // chunk_groups):

        @pl.when(used > chunk * chunk_groups)
        def _():
            store(chunk).wait()


def make_tiles(lay, plan, inputs, outputs, coarse, rounded):
    smem = pl.BlockSpec(memory_space=pltpu.SMEM)
    hbm = pl.BlockSpec(memory_space=pl.ANY)
    vmem = pl.BlockSpec(memory_space=pltpu.VMEM)
    own = lay.places * lay.blocks
    sums = jax.ShapeDtypeStruct((own, lay.side, lay.width), jnp.float32)
    n_copies = len(inputs) + len(outputs) + len(coarse) * lay.points + len(rounded) * lay.owners
    tiles = (lay.groups * lay.unroll, lay.side, lay.side)
    return pl.pallas_call(
        functools.partial(tiles_kernel, lay),
        out_shape=(sums, sums, jax.ShapeDtypeStruct(tiles, jnp.bfloat16)),
        in_specs=[smem] * 3 + [hbm] * (len(inputs) + len(outputs) + len(coarse) + len(rounded)),
        out_specs=(vmem, vmem, hbm),
        scratch_shapes=[
            pltpu.VMEM((lay.inputs, lay.pairs, lay.side), jnp.bfloat16),
            pltpu.VMEM((lay.outputs, lay.side, lay.pairs), jnp.bfloat16),
            pltpu.VMEM((lay.points, lay.slots, lay.pairs, lay.pairs), jnp.bfloat16),
            pltpu.VMEM((lay.inputs, lay.side, lay.width), jnp.bfloat16),
            pltpu.VMEM(tiles, jnp.bfloat16),
            pltpu.VMEM((lay.pairs, lay.points * lay.side), jnp.bfloat16),
            pltpu.VMEM((lay.outputs + 1, lay.side, lay.width), jnp.float32),
            pltpu.SemaphoreType.DMA((n_copies,)),
            pltpu.SemaphoreType.DMA((lay.groups // chunk_groups,)),
        ],
        compiler_params=pltpu.CompilerParams(vmem_limit_bytes=60 * mib),
        cost_estimate=pl.CostEstimate(flops=4_000_000_000, bytes_accessed=16_000_000, transcendentals=0),
    )(*plan, *inputs, *outputs, *coarse, *rounded)


def apply_kernel(lay, group_start, slot_of, entries, tiles_in, *refs):
    given_vec = refs[: lay.cols]
    own_sum, other_sum = refs[lay.cols : lay.cols + 2]
    rounded, tiles, total, sems, out_sems = refs[lay.cols + 2 :]
    used = group_start[lay.inputs]
    span = chunk_groups * lay.unroll

    def load(chunk):
        part = pl.ds(chunk * span, span)
        return pltpu.make_async_copy(tiles_in.at[part], tiles.at[part], out_sems.at[chunk])

    for chunk in range(lay.groups // chunk_groups):

        @pl.when(used > chunk * chunk_groups)
        def _():
            load(chunk).start()

    copies = []
    for d in range(lay.cols):
        for g in range(lay.owners):
            target = rounded.at[pl.ds((g * lay.cols + d) * lay.blocks, lay.blocks)]
            copies.append(pltpu.make_async_copy(given_vec[d].at[g], target, sems.at[len(copies)]))
            copies[-1].start()
    total[...] = jnp.zeros_like(total)
    for copy in copies:
        copy.wait()
    for chunk in range(lay.groups // chunk_groups):

        @pl.when(used > chunk * chunk_groups)
        def _():
            load(chunk).wait()

    def visit(p, carry):
        def group_step(group, inner):
            held = [tiles[group * lay.unroll + i] for i in range(lay.unroll)]
            add_products(lay, group, entries, held, rounded[p], total)
            return inner

        lax.fori_loop(group_start[p], group_start[p + 1], group_step, 0)
        return carry

    lax.fori_loop(0, lay.inputs, visit, 0)
    own = lay.places * lay.blocks
    own_sum[...] = total[0:own]
    other_sum[...] = total[own : 2 * own]


def apply_tiles(lay, plan, tiles, rounded):
    smem = pl.BlockSpec(memory_space=pltpu.SMEM)
    hbm = pl.BlockSpec(memory_space=pl.ANY)
    vmem = pl.BlockSpec(memory_space=pltpu.VMEM)
    own = lay.places * lay.blocks
    sums = jax.ShapeDtypeStruct((own, lay.side, lay.width), jnp.float32)
    return pl.pallas_call(
        functools.partial(apply_kernel, lay),
        out_shape=(sums, sums),
        in_specs=[smem] * 3 + [hbm] * (1 + len(rounded)),
        out_specs=(vmem, vmem),
        scratch_shapes=[
            pltpu.VMEM((lay.inputs, lay.side, lay.width), jnp.bfloat16),
            pltpu.VMEM(tiles.shape, jnp.bfloat16),
            pltpu.VMEM((lay.outputs + 1, lay.side, lay.width), jnp.float32),
            pltpu.SemaphoreType.DMA((len(rounded) * lay.owners,)),
            pltpu.SemaphoreType.DMA((lay.groups // chunk_groups,)),
        ],
        compiler_params=pltpu.CompilerParams(vmem_limit_bytes=50 * mib),
        cost_estimate=pl.CostEstimate(flops=400_000_000, bytes_accessed=4_000_000, transcendentals=0),
    )(*plan, tiles, *rounded)


def on_device(
    vectors, energies, intersections, coarse, fine_coarse, coarse_slot, tile_codes, tile_count
):
    rows = lax.axis_size("row")
    cols = lax.axis_size("col")
    row_id = lax.axis_index("row")
    col_id = lax.axis_index("col")
    blocks, pairs, side = intersections.shape
    width = vectors.shape[1]
    points, slots_dev = coarse.shape[:2]
    lay = Layout(rows, cols, blocks, pairs, side, width, points, slots_dev, tile_codes.shape[1], 4)
    if lay.groups * lay.unroll * side * side * 2 > 16 * mib:
        lay = Layout(rows, cols, blocks, pairs, side, width, points, slots_dev, tile_codes.shape[1], 1)
    near = lay.near

    def move(array, row_step, col_step):
        pairs_list = [
            (r * cols + c, (r ^ row_step) * cols + (c ^ col_step)) for r in range(rows) for c in range(cols)
        ]
        return lax.ppermute(array, axes, pairs_list)

    def along(array, step):
        return move(array, 2 * step, 0)

    def to_core(array):
        return move(array, 1, 0)

    def in_plane(array):
        return [array] + [move(array, 0, d) for d in range(1, cols)]

    start = vectors.reshape(blocks, side, width)
    energy = energies.reshape(blocks, side, 1)
    two_owners = lay.owners == 2
    codes, counts = tile_codes, tile_count
    if two_owners:
        codes = jnp.concatenate([tile_codes, along(tile_codes, near)], axis=0)
        counts = jnp.concatenate([tile_count, along(tile_count, near)], axis=0)
        starts = jnp.stack([start, along(start, near)])
        energies_both = jnp.stack([energy, along(energies, near).reshape(blocks, side, 1)])
    else:
        starts, energies_both = start[None], energy[None]
    ids = jnp.stack([row_id // 2, row_id % 2, col_id]).astype(jnp.int32)
    plan = make_plan(lay, ids, codes, counts, fine_coarse, coarse_slot)

    over_line = [intersections] + [along(intersections, d) for d in range(1, lay.places)]
    near_coarse = [coarse] + [along(coarse, e) for e in range(1, near)]
    blocks_coarse = []
    for part in near_coarse:
        blocks_coarse += [part, to_core(part)]
    inputs = in_plane(intersections)
    if two_owners:
        inputs = inputs + in_plane(over_line[near])
    lefts = [jnp.swapaxes(part, 1, 2) for part in over_line]
    lefts = lefts + [to_core(part) for part in lefts]
    rounded = in_plane(starts.astype(jnp.bfloat16))

    own_sum, other_sum, tiles = make_tiles(lay, plan, inputs, lefts, blocks_coarse, rounded)

    def over_core(own_part, other_part):
        return (own_part + to_core(other_part)).reshape(lay.places, blocks, side, width)

    merged = over_core(own_sum, other_sum)
    if two_owners:
        sums = jnp.stack([merged[0], merged[near]])
        for e in range(1, near):
            sent = jnp.stack([merged[e], merged[e ^ near]]).astype(jnp.bfloat16)
            sums = sums + along(sent, e).astype(jnp.float32)
        sums = sums + along(sums.astype(jnp.bfloat16), near)[::-1].astype(jnp.float32)
    else:
        sums = merged

    firsts = (energies_both * starts + sums - spectrum_center * starts) / spectrum_half
    own_sum, other_sum = apply_tiles(lay, plan, tiles, in_plane(firsts.astype(jnp.bfloat16)))
    merged = over_core(own_sum, other_sum)
    last = merged[0]
    for d in range(1, lay.places):
        last = last + along(merged[d].astype(jnp.bfloat16), d).astype(jnp.float32)
    first = firsts[0]
    second = 2.0 * ((energy * first + last - spectrum_center * first) / spectrum_half) - start
    return first.reshape(vectors.shape), second.reshape(vectors.shape)


def solution(mesh):
    in_specs = (
        P(axes, None),
        P(axes),
        P(axes, None, None),
        P("col", "row", None, None),
        P(),
        P(),
        P(axes, None),
        P(axes),
    )
    out_specs = (P(axes, None), P(axes, None))
    return jax.shard_map(
        on_device, mesh=mesh, in_specs=in_specs, out_specs=out_specs, check_vma=False
    )
```

```python
import functools

import jax
import jax.numpy as jnp
from jax import lax
from jax.experimental import pallas as pl
from jax.experimental.pallas import tpu as pltpu
from jax.sharding import PartitionSpec as P

spectrum_center = 2.0
spectrum_half = 3.0
axes = ("row", "col")
chunk_groups = 8
mib = 1 << 20


class Layout:
    def __init__(self, rows, cols, blocks, pairs, side, width, points, slots_dev, tile_max, unroll):
        self.rows, self.cols, self.blocks = rows, cols, blocks
        self.pairs, self.side, self.width = pairs, side, width
        self.points, self.slots_dev, self.tile_max = points, slots_dev, tile_max
        self.places = rows // 2
        self.near = max(self.places // 2, 1)
        self.owners = 2 if self.places > 1 else 1
        self.spread = cols * blocks
        self.inputs = self.owners * self.spread
        self.outputs = rows * blocks
        self.slots = 2 * self.near * slots_dev
        self.unroll = unroll
        most = self.owners * tile_max + self.inputs * (unroll - 1)
        self.groups = -(-most // (unroll * chunk_groups)) * chunk_groups

    def line_steps(self):
        return [d for d in range(1, self.places) if d != self.near]


def plan_kernel(lay, ids, codes, counts, fine, stored, group_start, slot_of, entries, fill):
    place, core, col = ids[0], ids[1], ids[2]
    half = lax.div(place, lay.near)

    def clear(p, carry):
        owner = lax.div(p, lay.spread)
        rest = lax.rem(p, lay.spread)
        from_col = lax.bitwise_xor(lax.div(rest, lay.blocks), col)
        from_place = lax.bitwise_xor(place, owner * lay.near)
        block = ((from_place * 2 + core) * lay.cols + from_col) * lay.blocks + lax.rem(rest, lay.blocks)
        position = stored[fine[block]]
        at_row = lax.div(position, lay.slots_dev)
        at_place, at_core = lax.div(at_row, 2), lax.rem(at_row, 2)
        slot = (lax.bitwise_xor(at_place, place) * 2 + lax.bitwise_xor(at_core, core)) * lay.slots_dev
        slot = slot + lax.rem(position, lay.slots_dev)
        slot_of[p] = jnp.where(lax.div(at_place, lay.near) == half, slot, -1)
        fill[p] = 0
        return carry

    lax.fori_loop(0, lay.inputs, clear, 0)

    def input_of(owner, code):
        j = lax.rem(code, lay.spread)
        from_col = lax.bitwise_xor(lax.div(j, lay.blocks), col)
        return owner * lay.spread + from_col * lay.blocks + lax.rem(j, lay.blocks)

    for owner in range(lay.owners):

        def count(i, carry):
            p = input_of(owner, codes[owner, i])
            fill[p] = fill[p] + 1
            return carry

        lax.fori_loop(0, counts[owner], count, 0)

    def place_groups(p, start):
        group_start[p] = start
        used = jnp.where(slot_of[p] >= 0, fill[p], 0)
        fill[p] = start * lay.unroll
        return start + lax.div(used + (lay.unroll - 1), lay.unroll)

    total = lax.fori_loop(0, lay.inputs, place_groups, 0)
    group_start[lay.inputs] = total

    def blank(i, carry):
        entries[i] = lay.outputs * lay.points
        return carry

    lax.fori_loop(0, total * lay.unroll, blank, 0)

    for owner in range(lay.owners):

        def put(i, carry):
            code = codes[owner, i]
            p = input_of(owner, code)

            @pl.when(slot_of[p] >= 0)
            def _():
                out = lax.div(code, lay.spread)
                at_row = lax.div(out, lay.blocks)
                within = lax.rem(out, lay.blocks)
                far = lax.bitwise_xor(lax.div(at_row, 2), place)
                other = lax.bitwise_xor(lax.rem(at_row, 2), core)
                q = (other * lay.places + far) * lay.blocks + within
                a = fine[(at_row * lay.cols + col) * lay.blocks + within] - col * lay.points
                spot = fill[p]
                entries[spot] = q * lay.points + a
                fill[p] = spot + 1

            return carry

        lax.fori_loop(0, counts[owner], put, 0)


def make_plan(lay, ids, codes, counts, fine, stored):
    smem = pl.BlockSpec(memory_space=pltpu.SMEM)
    return pl.pallas_call(
        functools.partial(plan_kernel, lay),
        out_shape=(
            jax.ShapeDtypeStruct((lay.inputs + 1,), jnp.int32),
            jax.ShapeDtypeStruct((lay.inputs,), jnp.int32),
            jax.ShapeDtypeStruct((lay.groups * lay.unroll,), jnp.int32),
        ),
        in_specs=[smem] * 5,
        out_specs=(smem,) * 3,
        scratch_shapes=[pltpu.SMEM((lay.inputs,), jnp.int32)],
        cost_estimate=pl.CostEstimate(flops=0, bytes_accessed=20_000_000, transcendentals=0),
    )(ids, codes, counts, fine, stored)


def add_products(lay, group, entries, tiles, rounded_block, total):
    products = [
        jnp.dot(tiles[i], rounded_block, preferred_element_type=jnp.float32) for i in range(lay.unroll)
    ]
    for i in range(lay.unroll):
        q = lax.div(entries[group * lay.unroll + i], lay.points)
        total[q] = total[q] + products[i]


def turn_kernel(lay, *refs):
    given, outs = refs[: lay.owners], refs[lay.owners :]
    for g in range(lay.owners):
        for t in range(lay.blocks):
            turned = given[g][t, 0 : lay.pairs, :].T
            outs[0][g * lay.blocks + t] = turned
            if g == 0:
                outs[1][t] = turned


def turn(lay, *given):
    vmem = pl.BlockSpec(memory_space=pltpu.VMEM)
    return pl.pallas_call(
        functools.partial(turn_kernel, lay),
        out_shape=(
            jax.ShapeDtypeStruct((lay.owners * lay.blocks, lay.side, lay.pairs), jnp.bfloat16),
            jax.ShapeDtypeStruct((lay.blocks, lay.side, lay.pairs), jnp.bfloat16),
        ),
        in_specs=[vmem] * lay.owners,
        out_specs=(vmem, vmem),
        compiler_params=pltpu.CompilerParams(vmem_limit_bytes=16 * mib),
        cost_estimate=pl.CostEstimate(flops=1_000_000, bytes_accessed=3_000_000, transcendentals=0),
    )(*given)


def tiles_kernel(lay, group_start, slot_of, entries, *refs):
    n_in = lay.owners * lay.cols
    n_coarse = 2 * lay.near
    lines = lay.line_steps()
    refs = list(refs)
    given_in = [refs.pop(0) for _ in range(n_in)]
    given_out = [refs.pop(0) for _ in range(2 * (1 + len(lines)))]
    given_coarse = [refs.pop(0) for _ in range(n_coarse)]
    own_sum, other_sum, tiles_out = refs[:3]
    right, left, blocks, rounded, tiles, projected, total, sems, out_sems = refs[3:]
    copies = []

    def fetch(source, target):
        copies.append(pltpu.make_async_copy(source, target, sems.at[len(copies)]))
        copies[-1].start()

    for i in range(n_coarse):
        for a in range(lay.points):
            fetch(given_coarse[i].at[a], blocks.at[a, pl.ds(i * lay.slots_dev, lay.slots_dev)])
    for i in range(n_in):
        part = pl.ds(i * lay.blocks, lay.blocks)
        fetch(given_in[i].at[:, pl.ds(0, lay.pairs)], right.at[part])
        fetch(given_in[i].at[:, pl.ds(lay.pairs, lay.side)], rounded.at[part])
    for k in range(2):
        held = given_out[k * (1 + len(lines)) :]
        for g in range(lay.owners):
            spot = (k * lay.places + g * lay.near) * lay.blocks
            fetch(held[0].at[pl.ds(g * lay.blocks, lay.blocks)], left.at[pl.ds(spot, lay.blocks)])
        for i, d in enumerate(lines):
            fetch(held[1 + i], left.at[pl.ds((k * lay.places + d) * lay.blocks, lay.blocks)])
    total[...] = jnp.zeros_like(total)
    for copy in copies:
        copy.wait()

    def visit(p, carry):
        first, last = group_start[p], group_start[p + 1]

        @pl.when(last > first)
        def _():
            slot = slot_of[p]
            for a in range(lay.points):
                projected[:, a * lay.side : (a + 1) * lay.side] = jnp.dot(
                    blocks[a, slot], right[p], preferred_element_type=jnp.float32
                ).astype(jnp.bfloat16)

            def group_step(group, inner):
                fresh = []
                for i in range(lay.unroll):
                    entry = entries[group * lay.unroll + i]
                    q = jnp.minimum(lax.div(entry, lay.points), lay.outputs - 1)
                    a = lax.rem(entry, lay.points)
                    both = jnp.dot(left[q], projected[...], preferred_element_type=jnp.float32)
                    tile = both[:, : lay.side]
                    for b in range(1, lay.points):
                        tile = jnp.where(a == b, both[:, b * lay.side : (b + 1) * lay.side], tile)
                    fresh.append(tile.astype(jnp.bfloat16))
                for i in range(lay.unroll):
                    tiles[group * lay.unroll + i] = fresh[i]
                add_products(lay, group, entries, fresh, rounded[p], total)
                return inner

            lax.fori_loop(first, last, group_step, 0)

        return carry

    lax.fori_loop(0, lay.inputs, visit, 0)
    used = group_start[lay.inputs]
    span = chunk_groups * lay.unroll

    def store(chunk):
        part = pl.ds(chunk * span, span)
        return pltpu.make_async_copy(tiles.at[part], tiles_out.at[part], out_sems.at[chunk])

    for chunk in range(lay.groups // chunk_groups):

        @pl.when(used > chunk * chunk_groups)
        def _():
            store(chunk).start()

    own = lay.places * lay.blocks
    own_sum[...] = total[0:own]
    other_sum[...] = total[own : 2 * own]
    for chunk in range(lay.groups // chunk_groups):

        @pl.when(used > chunk * chunk_groups)
        def _():
            store(chunk).wait()


def make_tiles(lay, plan, inputs, outputs, coarse):
    smem = pl.BlockSpec(memory_space=pltpu.SMEM)
    hbm = pl.BlockSpec(memory_space=pl.ANY)
    vmem = pl.BlockSpec(memory_space=pltpu.VMEM)
    own = lay.places * lay.blocks
    sums = jax.ShapeDtypeStruct((own, lay.side, lay.width), jnp.float32)
    n_copies = 2 * len(inputs) + 2 * lay.places + len(coarse) * lay.points
    tiles = (lay.groups * lay.unroll, lay.side, lay.side)
    return pl.pallas_call(
        functools.partial(tiles_kernel, lay),
        out_shape=(sums, sums, jax.ShapeDtypeStruct(tiles, jnp.bfloat16)),
        in_specs=[smem] * 3 + [hbm] * (len(inputs) + len(outputs) + len(coarse)),
        out_specs=(vmem, vmem, hbm),
        scratch_shapes=[
            pltpu.VMEM((lay.inputs, lay.pairs, lay.side), jnp.bfloat16),
            pltpu.VMEM((lay.outputs, lay.side, lay.pairs), jnp.bfloat16),
            pltpu.VMEM((lay.points, lay.slots, lay.pairs, lay.pairs), jnp.bfloat16),
            pltpu.VMEM((lay.inputs, lay.side, lay.width), jnp.bfloat16),
            pltpu.VMEM(tiles, jnp.bfloat16),
            pltpu.VMEM((lay.pairs, lay.points * lay.side), jnp.bfloat16),
            pltpu.VMEM((lay.outputs + 1, lay.side, lay.width), jnp.float32),
            pltpu.SemaphoreType.DMA((n_copies,)),
            pltpu.SemaphoreType.DMA((lay.groups // chunk_groups,)),
        ],
        compiler_params=pltpu.CompilerParams(vmem_limit_bytes=60 * mib),
        cost_estimate=pl.CostEstimate(flops=4_000_000_000, bytes_accessed=50_000_000, transcendentals=0),
    )(*plan, *inputs, *outputs, *coarse)


def apply_kernel(lay, group_start, slot_of, entries, tiles_in, *refs):
    given_vec = refs[: lay.cols]
    own_sum, other_sum = refs[lay.cols : lay.cols + 2]
    rounded, tiles, total, sems, out_sems = refs[lay.cols + 2 :]
    used = group_start[lay.inputs]
    span = chunk_groups * lay.unroll

    def load(chunk):
        part = pl.ds(chunk * span, span)
        return pltpu.make_async_copy(tiles_in.at[part], tiles.at[part], out_sems.at[chunk])

    for chunk in range(lay.groups // chunk_groups):

        @pl.when(used > chunk * chunk_groups)
        def _():
            load(chunk).start()

    copies = []
    for d in range(lay.cols):
        for g in range(lay.owners):
            target = rounded.at[pl.ds((g * lay.cols + d) * lay.blocks, lay.blocks)]
            copies.append(pltpu.make_async_copy(given_vec[d].at[g], target, sems.at[len(copies)]))
            copies[-1].start()
    total[...] = jnp.zeros_like(total)
    for copy in copies:
        copy.wait()
    for chunk in range(lay.groups // chunk_groups):

        @pl.when(used > chunk * chunk_groups)
        def _():
            load(chunk).wait()

    def visit(p, carry):
        def group_step(group, inner):
            held = [tiles[group * lay.unroll + i] for i in range(lay.unroll)]
            add_products(lay, group, entries, held, rounded[p], total)
            return inner

        lax.fori_loop(group_start[p], group_start[p + 1], group_step, 0)
        return carry

    lax.fori_loop(0, lay.inputs, visit, 0)
    own = lay.places * lay.blocks
    own_sum[...] = total[0:own]
    other_sum[...] = total[own : 2 * own]


def apply_tiles(lay, plan, tiles, rounded):
    smem = pl.BlockSpec(memory_space=pltpu.SMEM)
    hbm = pl.BlockSpec(memory_space=pl.ANY)
    vmem = pl.BlockSpec(memory_space=pltpu.VMEM)
    own = lay.places * lay.blocks
    sums = jax.ShapeDtypeStruct((own, lay.side, lay.width), jnp.float32)
    return pl.pallas_call(
        functools.partial(apply_kernel, lay),
        out_shape=(sums, sums),
        in_specs=[smem] * 3 + [hbm] * (1 + len(rounded)),
        out_specs=(vmem, vmem),
        scratch_shapes=[
            pltpu.VMEM((lay.inputs, lay.side, lay.width), jnp.bfloat16),
            pltpu.VMEM(tiles.shape, jnp.bfloat16),
            pltpu.VMEM((lay.outputs + 1, lay.side, lay.width), jnp.float32),
            pltpu.SemaphoreType.DMA((len(rounded) * lay.owners,)),
            pltpu.SemaphoreType.DMA((lay.groups // chunk_groups,)),
        ],
        compiler_params=pltpu.CompilerParams(vmem_limit_bytes=50 * mib),
        cost_estimate=pl.CostEstimate(flops=400_000_000, bytes_accessed=4_000_000, transcendentals=0),
    )(*plan, tiles, *rounded)


def on_device(
    vectors, energies, intersections, coarse, fine_coarse, coarse_slot, tile_codes, tile_count
):
    rows = lax.axis_size("row")
    cols = lax.axis_size("col")
    row_id = lax.axis_index("row")
    col_id = lax.axis_index("col")
    blocks, pairs, side = intersections.shape
    width = vectors.shape[1]
    points, slots_dev = coarse.shape[:2]
    lay = Layout(rows, cols, blocks, pairs, side, width, points, slots_dev, tile_codes.shape[1], 4)
    if lay.groups * lay.unroll * side * side * 2 > 16 * mib:
        lay = Layout(rows, cols, blocks, pairs, side, width, points, slots_dev, tile_codes.shape[1], 1)
    near = lay.near

    def move(array, row_step, col_step):
        pairs_list = [
            (r * cols + c, (r ^ row_step) * cols + (c ^ col_step)) for r in range(rows) for c in range(cols)
        ]
        return lax.ppermute(array, axes, pairs_list)

    def along(array, step):
        return move(array, 2 * step, 0)

    def to_core(array):
        return move(array, 1, 0)

    def in_plane(array):
        return [array] + [move(array, 0, d) for d in range(1, cols)]

    start = vectors.reshape(blocks, side, width)
    energy = energies.reshape(blocks, side, 1)
    two_owners = lay.owners == 2
    n_codes = tile_codes.shape[1]
    listed = jnp.concatenate([tile_codes, tile_count[:, None]], axis=1)
    if two_owners:
        listed = jnp.concatenate([listed, along(listed, near)], axis=0)
    ids = jnp.stack([row_id // 2, row_id % 2, col_id]).astype(jnp.int32)
    plan = make_plan(lay, ids, listed[:, :n_codes], listed[:, n_codes], fine_coarse, coarse_slot)
    joined = jnp.concatenate([intersections, start.astype(jnp.bfloat16)], axis=1)

    partner = [along(joined, near)] if two_owners else []
    inputs = in_plane(joined)
    late_coarse, plan = lax.optimization_barrier((coarse, plan))
    near_coarse = [coarse] + [along(late_coarse, e) for e in range(1, near)]
    turned, turned_own = turn(lay, joined, *partner)
    partner, inputs = lax.optimization_barrier((partner, inputs))
    for part in partner:
        inputs = inputs + in_plane(part)
    lines = [along(turned_own, d) for d in lay.line_steps()]
    held = (inputs, turned, near_coarse, lines)
    inputs, turned, near_coarse, lines = lax.optimization_barrier(held)
    blocks_coarse = []
    for part in near_coarse:
        blocks_coarse += [part, to_core(part)]
    lefts = [turned] + lines
    lefts = lefts + [to_core(part) for part in lefts]

    own_sum, other_sum, tiles = make_tiles(lay, plan, inputs, lefts, blocks_coarse)

    def over_core(own_part, other_part):
        return (own_part + to_core(other_part)).reshape(lay.places, blocks, side, width)

    def shifted_part(field):
        return energy * field - spectrum_center * field

    merged = over_core(own_sum, other_sum)
    if two_owners:
        sums = jnp.stack([merged[0] + shifted_part(start), merged[near]])
        for e in range(1, near):
            sent = jnp.stack([merged[e], merged[e ^ near]]).astype(jnp.bfloat16)
            sums = sums + along(sent, e).astype(jnp.float32)
        sums = sums + along(sums.astype(jnp.bfloat16), near)[::-1].astype(jnp.float32)
    else:
        sums = merged + shifted_part(start)[None]

    firsts = sums / spectrum_half
    first = firsts[0]
    own_sum, other_sum = apply_tiles(lay, plan, tiles, in_plane(firsts.astype(jnp.bfloat16)))
    merged = over_core(own_sum, other_sum)
    last = merged[0]
    for d in range(1, lay.places):
        last = last + along(merged[d].astype(jnp.bfloat16), d).astype(jnp.float32)
    second = 2.0 * ((shifted_part(first) + last) / spectrum_half) - start
    return first.reshape(vectors.shape), second.reshape(vectors.shape)


def solution(mesh):
    in_specs = (
        P(axes, None),
        P(axes),
        P(axes, None, None),
        P("col", "row", None, None),
        P(),
        P(),
        P(axes, None),
        P(axes),
    )
    out_specs = (P(axes, None), P(axes, None))
    return jax.shard_map(
        on_device, mesh=mesh, in_specs=in_specs, out_specs=out_specs, check_vma=False
    )
```

```python
import functools

import jax
import jax.numpy as jnp
from jax import lax
from jax.experimental import pallas as pl
from jax.experimental.pallas import tpu as pltpu
from jax.sharding import PartitionSpec as P

spectrum_center = 2.0
spectrum_half = 3.0
axes = ("row", "col")
chunk_groups = 8
mib = 1 << 20


class Layout:
    def __init__(self, rows, cols, blocks, pairs, side, width, points, slots_dev, tile_max, unroll):
        self.rows, self.cols, self.blocks = rows, cols, blocks
        self.pairs, self.side, self.width = pairs, side, width
        self.points, self.slots_dev, self.tile_max = points, slots_dev, tile_max
        self.places = rows // 2
        self.near = max(self.places // 2, 1)
        self.owners = 2 if self.places > 1 else 1
        self.spread = cols * blocks
        self.inputs = self.owners * self.spread
        self.outputs = rows * blocks
        self.slots = 2 * self.near * slots_dev
        self.unroll = unroll
        self.vmem = (32 if unroll > 1 else 60) * mib
        most = self.owners * tile_max + self.inputs * (unroll - 1) + unroll
        self.groups = -(-most // (unroll * chunk_groups)) * chunk_groups

    def line_steps(self):
        return [d for d in range(1, self.places) if d != self.near]


def plan_kernel(lay, ids, listed, fine, stored, slot_of, valid, sizes, group_input, entries, fill):
    place, core, col = ids[0], ids[1], ids[2]
    half = lax.div(place, lay.near)
    blank = lay.outputs * lay.points

    for owner in range(lay.owners):

        def examine(i, found):
            p = owner * lay.spread + i
            from_col = lax.bitwise_xor(lax.div(i, lay.blocks), col)
            from_place = lax.bitwise_xor(place, owner * lay.near)
            block = ((from_place * 2 + core) * lay.cols + from_col) * lay.blocks + lax.rem(i, lay.blocks)
            position = stored[fine[block]]
            at_row = lax.div(position, lay.slots_dev)
            at_place, at_core = lax.div(at_row, 2), lax.rem(at_row, 2)
            slot = (lax.bitwise_xor(at_place, place) * 2 + lax.bitwise_xor(at_core, core)) * lay.slots_dev
            slot = slot + lax.rem(position, lay.slots_dev)
            here = lax.div(at_place, lay.near) == half
            slot_of[p] = jnp.where(here, slot, -1)
            valid[owner * (lay.spread + 1) + found] = i
            fill[p] = 0
            return found + here.astype(jnp.int32)

        sizes[1 + owner] = lax.fori_loop(0, lay.spread, examine, 0)

    def input_of(owner, code):
        j = lax.rem(code, lay.spread)
        from_col = lax.bitwise_xor(lax.div(j, lay.blocks), col)
        return owner * lay.spread + from_col * lay.blocks + lax.rem(j, lay.blocks)

    for owner in range(lay.owners):

        def count(i, carry):
            p = input_of(owner, listed[owner, i])
            fill[p] = fill[p] + 1
            return carry

        lax.fori_loop(0, listed[owner, lay.tile_max], count, 0)

    group_input[0] = 0

    def place_groups(p, start):
        used = jnp.where(slot_of[p] >= 0, fill[p], 0)
        fill[p] = start * lay.unroll
        end = start + lax.div(used + (lay.unroll - 1), lay.unroll)

        def name(group, carry):
            group_input[group] = p
            return carry

        lax.fori_loop(start, end, name, 0)
        return end

    total = lax.fori_loop(0, lay.inputs, place_groups, 1)
    sizes[0] = total

    def clear(i, carry):
        entries[i] = blank
        return carry

    lax.fori_loop(0, total * lay.unroll, clear, 0)

    for owner in range(lay.owners):

        def put(i, carry):
            code = listed[owner, i]
            p = input_of(owner, code)

            @pl.when(slot_of[p] >= 0)
            def _():
                out = lax.div(code, lay.spread)
                at_row = lax.div(out, lay.blocks)
                within = lax.rem(out, lay.blocks)
                far = lax.bitwise_xor(lax.div(at_row, 2), place)
                other = lax.bitwise_xor(lax.rem(at_row, 2), core)
                q = (other * lay.places + far) * lay.blocks + within
                a = fine[(at_row * lay.cols + col) * lay.blocks + within] - col * lay.points
                spot = fill[p]
                entries[spot] = q * lay.points + a
                fill[p] = spot + 1

            return carry

        lax.fori_loop(0, listed[owner, lay.tile_max], put, 0)


def make_plan(lay, ids, listed, fine, stored):
    smem = pl.BlockSpec(memory_space=pltpu.SMEM)
    lengths = (
        lay.inputs,
        lay.owners * (lay.spread + 1),
        1 + lay.owners,
        lay.groups,
        lay.groups * lay.unroll,
    )
    return pl.pallas_call(
        functools.partial(plan_kernel, lay),
        out_shape=tuple(jax.ShapeDtypeStruct((n,), jnp.int32) for n in lengths),
        in_specs=[smem] * 4,
        out_specs=(smem,) * 5,
        scratch_shapes=[pltpu.SMEM((lay.inputs,), jnp.int32)],
        cost_estimate=pl.CostEstimate(flops=0, bytes_accessed=20_000_000, transcendentals=0),
    )(ids, listed, fine, stored)


def project_kernel(lay, owner, slot_of, valid, sizes, *refs):
    n_coarse = 2 * (2 * lay.near - 1)
    given_in, given_coarse = refs[: lay.cols], list(refs[lay.cols : lay.cols + n_coarse])
    out, right, blocks, sems = refs[lay.cols + n_coarse :]
    copies = []

    def fetch(source, target):
        copies.append(pltpu.make_async_copy(source, target, sems.at[len(copies)]))
        copies[-1].start()

    for i in range(lay.cols):
        fetch(given_in[i].at[:, pl.ds(0, lay.pairs)], right.at[pl.ds(i * lay.blocks, lay.blocks)])
    for i in range(2 * lay.near):
        first = given_coarse.pop(0)
        for a in range(first.shape[0]):
            fetch(first.at[a], blocks.at[a, pl.ds(i * lay.slots_dev, lay.slots_dev)])
        if i < 2:
            continue
        rest = given_coarse.pop(0)
        for a in range(1, lay.points):
            for at in range(lay.slots_dev):
                row = lay.blocks * lay.side + ((a - 1) * lay.slots_dev + at) * lay.pairs
                fetch(rest.at[pl.ds(row, lay.pairs)], blocks.at[a, i * lay.slots_dev + at])
    for copy in copies:
        copy.wait()
    found = sizes[1 + owner]

    def visit(step, carry):
        for lane in range(2):
            i = valid[owner * (lay.spread + 1) + jnp.minimum(2 * step + lane, found - 1)]
            slot = slot_of[owner * lay.spread + i]
            for a in range(lay.points):
                out[i, :, a * lay.side : (a + 1) * lay.side] = jnp.dot(
                    blocks[a, slot], right[i], preferred_element_type=jnp.float32
                ).astype(jnp.bfloat16)
        return carry

    lax.fori_loop(0, lax.div(found + 1, 2), visit, 0)


def project(lay, owner, plan, inputs, coarse):
    smem = pl.BlockSpec(memory_space=pltpu.SMEM)
    hbm = pl.BlockSpec(memory_space=pl.ANY)
    shape = (lay.spread, lay.pairs, lay.points * lay.side)
    return pl.pallas_call(
        functools.partial(project_kernel, lay, owner),
        out_shape=jax.ShapeDtypeStruct(shape, jnp.bfloat16),
        in_specs=[smem] * 3 + [hbm] * (len(inputs) + len(coarse)),
        out_specs=pl.BlockSpec(memory_space=pltpu.VMEM),
        scratch_shapes=[
            pltpu.VMEM((lay.spread, lay.pairs, lay.side), jnp.bfloat16),
            pltpu.VMEM((lay.points, lay.slots, lay.pairs, lay.pairs), jnp.bfloat16),
            pltpu.SemaphoreType.DMA((len(inputs) + lay.slots * lay.points,)),
        ],
        compiler_params=pltpu.CompilerParams(vmem_limit_bytes=32 * mib),
        cost_estimate=pl.CostEstimate(flops=1_000_000_000, bytes_accessed=20_000_000, transcendentals=0),
    )(*plan[:3], *inputs, *coarse)


def add_products(lay, group, group_input, entries, tiles, rounded, total):
    vector = rounded[group_input[group]]
    products = [
        jnp.dot(tiles[group * lay.unroll + i], vector, preferred_element_type=jnp.float32)
        for i in range(lay.unroll)
    ]
    for i in range(lay.unroll):
        q = lax.div(entries[group * lay.unroll + i], lay.points)
        total[q] = total[q] + products[i]


def turn_kernel(lay, *refs):
    given, rest, outs = refs[: lay.owners], refs[lay.owners], refs[lay.owners + 1 :]
    for g in range(lay.owners):
        for t in range(lay.blocks):
            turned = given[g][t, 0 : lay.pairs, :].T
            outs[0][g * lay.blocks + t] = turned
            if g == 0:
                outs[1][t] = turned
                outs[2][t * lay.side : (t + 1) * lay.side, :] = turned
    outs[2][lay.blocks * lay.side :, :] = rest[...]


def turn(lay, rest, *given):
    vmem = pl.BlockSpec(memory_space=pltpu.VMEM)
    return pl.pallas_call(
        functools.partial(turn_kernel, lay),
        out_shape=(
            jax.ShapeDtypeStruct((lay.owners * lay.blocks, lay.side, lay.pairs), jnp.bfloat16),
            jax.ShapeDtypeStruct((lay.blocks, lay.side, lay.pairs), jnp.bfloat16),
            jax.ShapeDtypeStruct((lay.blocks * lay.side + rest.shape[0], lay.pairs), jnp.bfloat16),
        ),
        in_specs=[vmem] * (lay.owners + 1),
        out_specs=(vmem,) * 3,
        compiler_params=pltpu.CompilerParams(vmem_limit_bytes=16 * mib),
        cost_estimate=pl.CostEstimate(flops=1_000_000, bytes_accessed=3_000_000, transcendentals=0),
    )(*given, rest)


def tiles_kernel(lay, sizes, group_input, entries, *refs):
    n_in = lay.owners * lay.cols
    lines = lay.line_steps()
    refs = list(refs)
    given_in = [refs.pop(0) for _ in range(n_in)]
    given_out = [refs.pop(0) for _ in range(2 * (1 + len(lines)))]
    given_projected = [refs.pop(0) for _ in range(lay.owners)]
    own_sum, other_sum, tiles_out = refs[:3]
    left, projected, rounded, tiles, total, sems, out_sems = refs[3:]
    copies = []

    def fetch(source, target):
        copies.append(pltpu.make_async_copy(source, target, sems.at[len(copies)]))
        copies[-1].start()

    for k in range(2):
        held = given_out[k * (1 + len(lines)) :]
        for g in range(lay.owners):
            spot = (k * lay.places + g * lay.near) * lay.blocks
            fetch(held[0].at[pl.ds(g * lay.blocks, lay.blocks)], left.at[pl.ds(spot, lay.blocks)])
        for i, d in enumerate(lines):
            spot = (k * lay.places + d) * lay.blocks
            if d > lay.near:
                fetch(held[1 + i], left.at[pl.ds(spot, lay.blocks)])
            else:
                for t in range(lay.blocks):
                    fetch(held[1 + i].at[pl.ds(t * lay.side, lay.side)], left.at[spot + t])
    for g in range(lay.owners):
        fetch(given_projected[g], projected.at[pl.ds(g * lay.spread, lay.spread)])
    for i in range(n_in):
        part = pl.ds(i * lay.blocks, lay.blocks)
        fetch(given_in[i].at[:, pl.ds(lay.pairs, lay.side)], rounded.at[part])
    total[...] = jnp.zeros_like(total)
    for copy in copies:
        copy.wait()
    used = sizes[0]

    def group_step(group, carry):
        p = group_input[group]
        for i in range(lay.unroll):
            entry = entries[group * lay.unroll + i]
            q = jnp.minimum(lax.div(entry, lay.points), lay.outputs - 1)
            a = lax.rem(entry, lay.points)
            both = jnp.dot(left[q], projected[p], preferred_element_type=jnp.float32)
            tile = both[:, : lay.side]
            for b in range(1, lay.points):
                tile = jnp.where(a == b, both[:, b * lay.side : (b + 1) * lay.side], tile)
            tiles[group * lay.unroll + i] = tile.astype(jnp.bfloat16)
        add_products(lay, group - 1, group_input, entries, tiles, rounded, total)
        return carry

    lax.fori_loop(1, used, group_step, 0)
    span = chunk_groups * lay.unroll

    def store(chunk):
        part = pl.ds(chunk * span, span)
        return pltpu.make_async_copy(tiles.at[part], tiles_out.at[part], out_sems.at[chunk])

    for chunk in range(lay.groups // chunk_groups):

        @pl.when(used > chunk * chunk_groups)
        def _():
            store(chunk).start()

    add_products(lay, used - 1, group_input, entries, tiles, rounded, total)
    own = lay.places * lay.blocks
    own_sum[...] = total[0:own]
    other_sum[...] = total[own : 2 * own]
    for chunk in range(lay.groups // chunk_groups):

        @pl.when(used > chunk * chunk_groups)
        def _():
            store(chunk).wait()


def make_tiles(lay, plan, inputs, outputs, projected):
    smem = pl.BlockSpec(memory_space=pltpu.SMEM)
    hbm = pl.BlockSpec(memory_space=pl.ANY)
    vmem = pl.BlockSpec(memory_space=pltpu.VMEM)
    own = lay.places * lay.blocks
    sums = jax.ShapeDtypeStruct((own, lay.side, lay.width), jnp.float32)
    n_copies = len(inputs) + 2 * lay.places * lay.blocks + len(projected)
    tiles = (lay.groups * lay.unroll, lay.side, lay.side)
    return pl.pallas_call(
        functools.partial(tiles_kernel, lay),
        out_shape=(sums, sums, jax.ShapeDtypeStruct(tiles, jnp.bfloat16)),
        in_specs=[smem] * 3 + [hbm] * (len(inputs) + len(outputs) + len(projected)),
        out_specs=(vmem, vmem, hbm),
        scratch_shapes=[
            pltpu.VMEM((lay.outputs, lay.side, lay.pairs), jnp.bfloat16),
            pltpu.VMEM((lay.inputs, lay.pairs, lay.points * lay.side), jnp.bfloat16),
            pltpu.VMEM((lay.inputs, lay.side, lay.width), jnp.bfloat16),
            pltpu.VMEM(tiles, jnp.bfloat16),
            pltpu.VMEM((lay.outputs + 1, lay.side, lay.width), jnp.float32),
            pltpu.SemaphoreType.DMA((n_copies,)),
            pltpu.SemaphoreType.DMA((lay.groups // chunk_groups,)),
        ],
        compiler_params=pltpu.CompilerParams(vmem_limit_bytes=lay.vmem),
        cost_estimate=pl.CostEstimate(flops=4_000_000_000, bytes_accessed=30_000_000, transcendentals=0),
    )(plan[2], *plan[3:], *inputs, *outputs, *projected)


def apply_kernel(lay, sizes, group_input, entries, tiles_in, *refs):
    given_vec = refs[: lay.cols]
    own_sum, other_sum = refs[lay.cols : lay.cols + 2]
    rounded, tiles, total, sems, out_sems = refs[lay.cols + 2 :]
    used = sizes[0]
    span = chunk_groups * lay.unroll

    def load(chunk):
        part = pl.ds(chunk * span, span)
        return pltpu.make_async_copy(tiles_in.at[part], tiles.at[part], out_sems.at[chunk])

    for chunk in range(lay.groups // chunk_groups):

        @pl.when(used > chunk * chunk_groups)
        def _():
            load(chunk).start()

    copies = []
    for d in range(lay.cols):
        for g in range(lay.owners):
            target = rounded.at[pl.ds((g * lay.cols + d) * lay.blocks, lay.blocks)]
            copies.append(pltpu.make_async_copy(given_vec[d].at[g], target, sems.at[len(copies)]))
            copies[-1].start()
    total[...] = jnp.zeros_like(total)
    for copy in copies:
        copy.wait()
    for chunk in range(lay.groups // chunk_groups):

        @pl.when(used > chunk * chunk_groups)
        def _():
            load(chunk).wait()

    def group_step(group, carry):
        add_products(lay, group, group_input, entries, tiles, rounded, total)
        return carry

    lax.fori_loop(1, used, group_step, 0)
    own = lay.places * lay.blocks
    own_sum[...] = total[0:own]
    other_sum[...] = total[own : 2 * own]


def apply_tiles(lay, plan, tiles, rounded):
    smem = pl.BlockSpec(memory_space=pltpu.SMEM)
    hbm = pl.BlockSpec(memory_space=pl.ANY)
    vmem = pl.BlockSpec(memory_space=pltpu.VMEM)
    own = lay.places * lay.blocks
    sums = jax.ShapeDtypeStruct((own, lay.side, lay.width), jnp.float32)
    return pl.pallas_call(
        functools.partial(apply_kernel, lay),
        out_shape=(sums, sums),
        in_specs=[smem] * 3 + [hbm] * (1 + len(rounded)),
        out_specs=(vmem, vmem),
        scratch_shapes=[
            pltpu.VMEM((lay.inputs, lay.side, lay.width), jnp.bfloat16),
            pltpu.VMEM(tiles.shape, jnp.bfloat16),
            pltpu.VMEM((lay.outputs + 1, lay.side, lay.width), jnp.float32),
            pltpu.SemaphoreType.DMA((len(rounded) * lay.owners,)),
            pltpu.SemaphoreType.DMA((lay.groups // chunk_groups,)),
        ],
        compiler_params=pltpu.CompilerParams(vmem_limit_bytes=lay.vmem),
        cost_estimate=pl.CostEstimate(flops=400_000_000, bytes_accessed=4_000_000, transcendentals=0),
    )(plan[2], *plan[3:], tiles, *rounded)


def on_device(
    vectors, energies, intersections, coarse, fine_coarse, coarse_slot, tile_codes, tile_count
):
    rows = lax.axis_size("row")
    cols = lax.axis_size("col")
    row_id = lax.axis_index("row")
    col_id = lax.axis_index("col")
    blocks, pairs, side = intersections.shape
    width = vectors.shape[1]
    points, slots_dev = coarse.shape[:2]
    lay = Layout(rows, cols, blocks, pairs, side, width, points, slots_dev, tile_codes.shape[1], 4)
    if lay.groups * lay.unroll * side * side * 2 > 16 * mib:
        lay = Layout(rows, cols, blocks, pairs, side, width, points, slots_dev, tile_codes.shape[1], 1)
    near = lay.near

    def move(array, row_step, col_step):
        pairs_list = [
            (r * cols + c, (r ^ row_step) * cols + (c ^ col_step)) for r in range(rows) for c in range(cols)
        ]
        return lax.ppermute(array, axes, pairs_list)

    def along(array, step):
        return move(array, 2 * step, 0)

    def to_core(array):
        return move(array, 1, 0)

    def in_plane(array):
        return [array] + [move(array, 0, d) for d in range(1, cols)]

    start = vectors.reshape(blocks, side, width)
    energy = energies.reshape(blocks, side, 1)
    two_owners = lay.owners == 2
    ids = jnp.stack([row_id // 2, row_id % 2, col_id]).astype(jnp.int32)
    listed = jnp.concatenate([tile_codes, tile_count[:, None]], axis=1)
    n_listed = listed.shape[1]
    digits = jnp.concatenate([listed[0] >> 8, listed[0] & 255]).astype(jnp.bfloat16)
    depth = 16 * -(-2 * n_listed // (16 * width * blocks))
    digits = jnp.pad(digits, (0, blocks * depth * width - 2 * n_listed)).reshape(blocks, depth, width)
    joined = jnp.concatenate([intersections, start.astype(jnp.bfloat16), digits], axis=1)

    partner = [along(joined, near)] if two_owners else []
    inputs = in_plane(joined)
    near_coarse = [along(coarse[:1], e) for e in range(1, near)]
    rest = coarse[1:].reshape(-1, pairs)
    partner, inputs, near_coarse, rest = lax.optimization_barrier((partner, inputs, near_coarse, rest))
    if two_owners:
        sent = partner[0][:, pairs + side :].reshape(-1)[: 2 * n_listed].astype(jnp.int32)
        listed = jnp.concatenate([listed, ((sent[:n_listed] << 8) + sent[n_listed:])[None]], axis=0)
    plan = make_plan(lay, ids, listed, fine_coarse, coarse_slot)
    turned, turned_own, mixed = turn(lay, rest, joined, *partner)
    for part in partner:
        inputs = inputs + in_plane(part)
    lines = [along(mixed if d < near else turned_own, d) for d in lay.line_steps()]
    held = (inputs, turned, lines, near_coarse, plan)
    inputs, turned, lines, near_coarse, plan = lax.optimization_barrier(held)
    blocks_coarse = [coarse, to_core(coarse)]
    lefts = [turned] + lines
    lefts_core = [to_core(part) for part in lefts]
    for e in range(1, near):
        first_rows = near_coarse[e - 1]
        blocks_coarse += [first_rows, lefts[e], to_core(first_rows), lefts_core[e]]
    lefts = lefts + lefts_core
    projected = [
        project(lay, g, plan, inputs[g * cols : (g + 1) * cols], blocks_coarse) for g in range(lay.owners)
    ]
    own_sum, other_sum, tiles = make_tiles(lay, plan, inputs, lefts, projected)

    def over_core(own_part, other_part):
        return (own_part + to_core(other_part)).reshape(lay.places, blocks, side, width)

    def shifted_part(field):
        return energy * field - spectrum_center * field

    merged = over_core(own_sum, other_sum)
    if two_owners:
        sums = jnp.stack([merged[0] + shifted_part(start), merged[near]])
        for e in range(1, near):
            sent = jnp.stack([merged[e], merged[e ^ near]]).astype(jnp.bfloat16)
            sums = sums + along(sent, e).astype(jnp.float32)
        sums = sums + along(sums.astype(jnp.bfloat16), near)[::-1].astype(jnp.float32)
    else:
        sums = merged + shifted_part(start)[None]

    firsts = sums / spectrum_half
    first = firsts[0]
    own_sum, other_sum = apply_tiles(lay, plan, tiles, in_plane(firsts.astype(jnp.bfloat16)))
    merged = over_core(own_sum, other_sum)
    last = merged[0]
    for d in range(1, lay.places):
        last = last + along(merged[d].astype(jnp.bfloat16), d).astype(jnp.float32)
    second = 2.0 * ((shifted_part(first) + last) / spectrum_half) - start
    return first.reshape(vectors.shape), second.reshape(vectors.shape)


def solution(mesh):
    in_specs = (
        P(axes, None),
        P(axes),
        P(axes, None, None),
        P("col", "row", None, None),
        P(),
        P(),
        P(axes, None),
        P(axes),
    )
    out_specs = (P(axes, None), P(axes, None))
    return jax.shard_map(
        on_device, mesh=mesh, in_specs=in_specs, out_specs=out_specs, check_vma=False
    )
```

```python
import functools

import jax
import jax.numpy as jnp
from jax import lax
from jax.experimental import pallas as pl
from jax.experimental.pallas import tpu as pltpu
from jax.sharding import PartitionSpec as P

spectrum_center = 2.0
spectrum_half = 3.0
axes = ("row", "col")
chunk_groups = 8
mib = 1 << 20


class Layout:
    def __init__(self, rows, cols, blocks, pairs, side, width, points, slots_dev, tile_max, unroll):
        self.rows, self.cols, self.blocks = rows, cols, blocks
        self.pairs, self.side, self.width = pairs, side, width
        self.points, self.slots_dev, self.tile_max = points, slots_dev, tile_max
        self.places = rows // 2
        self.near = max(self.places // 2, 1)
        self.owners = 2 if self.places > 1 else 1
        self.spread = cols * blocks
        self.inputs = self.owners * self.spread
        self.outputs = rows * blocks
        self.slots = 2 * self.near * slots_dev
        self.unroll = unroll
        self.vmem = 60 * mib
        most = self.owners * tile_max + self.inputs * (unroll - 1) + unroll
        self.groups = -(-most // (unroll * chunk_groups)) * chunk_groups

    def line_steps(self):
        return [d for d in range(1, self.places) if d != self.near]


def plan_kernel(lay, ids, listed, fine, stored, slot_of, valid, sizes, group_input, entries, fill):
    place, core, col = ids[0], ids[1], ids[2]
    half = lax.div(place, lay.near)
    blank = lay.outputs * lay.points

    for owner in range(lay.owners):

        def examine(i, found):
            p = owner * lay.spread + i
            from_col = lax.bitwise_xor(lax.div(i, lay.blocks), col)
            from_place = lax.bitwise_xor(place, owner * lay.near)
            block = ((from_place * 2 + core) * lay.cols + from_col) * lay.blocks + lax.rem(i, lay.blocks)
            position = stored[fine[block]]
            at_row = lax.div(position, lay.slots_dev)
            at_place, at_core = lax.div(at_row, 2), lax.rem(at_row, 2)
            slot = (lax.bitwise_xor(at_place, place) * 2 + lax.bitwise_xor(at_core, core)) * lay.slots_dev
            slot = slot + lax.rem(position, lay.slots_dev)
            here = lax.div(at_place, lay.near) == half
            slot_of[p] = jnp.where(here, slot, -1)
            valid[owner * (lay.spread + 1) + found] = i
            fill[p] = 0
            return found + here.astype(jnp.int32)

        sizes[1 + owner] = lax.fori_loop(0, lay.spread, examine, 0)

    def input_of(owner, code):
        j = lax.rem(code, lay.spread)
        from_col = lax.bitwise_xor(lax.div(j, lay.blocks), col)
        return owner * lay.spread + from_col * lay.blocks + lax.rem(j, lay.blocks)

    for owner in range(lay.owners):

        def count(i, carry):
            p = input_of(owner, listed[owner, i])
            fill[p] = fill[p] + 1
            return carry

        lax.fori_loop(0, listed[owner, lay.tile_max], count, 0)

    group_input[0] = 0

    def place_groups(p, start):
        used = jnp.where(slot_of[p] >= 0, fill[p], 0)
        fill[p] = start * lay.unroll
        end = start + lax.div(used + (lay.unroll - 1), lay.unroll)

        def name(group, carry):
            group_input[group] = p
            return carry

        lax.fori_loop(start, end, name, 0)
        return end

    total = 1
    for owner in range(lay.owners):
        if owner > 0:
            sizes[lay.owners + owner] = total
        total = lax.fori_loop(owner * lay.spread, (owner + 1) * lay.spread, place_groups, total)
    sizes[0] = total

    def clear(i, carry):
        entries[i] = blank
        return carry

    lax.fori_loop(0, total * lay.unroll, clear, 0)

    for owner in range(lay.owners):

        def put(i, carry):
            code = listed[owner, i]
            p = input_of(owner, code)

            @pl.when(slot_of[p] >= 0)
            def _():
                out = lax.div(code, lay.spread)
                at_row = lax.div(out, lay.blocks)
                within = lax.rem(out, lay.blocks)
                far = lax.bitwise_xor(lax.div(at_row, 2), place)
                other = lax.bitwise_xor(lax.rem(at_row, 2), core)
                q = (other * lay.places + far) * lay.blocks + within
                a = fine[(at_row * lay.cols + col) * lay.blocks + within] - col * lay.points
                spot = fill[p]
                entries[spot] = q * lay.points + a
                fill[p] = spot + 1

            return carry

        lax.fori_loop(0, listed[owner, lay.tile_max], put, 0)


def make_plan(lay, ids, listed, fine, stored):
    smem = pl.BlockSpec(memory_space=pltpu.SMEM)
    lengths = (
        lay.inputs,
        lay.owners * (lay.spread + 1),
        2 * lay.owners,
        lay.groups,
        lay.groups * lay.unroll,
    )
    return pl.pallas_call(
        functools.partial(plan_kernel, lay),
        out_shape=tuple(jax.ShapeDtypeStruct((n,), jnp.int32) for n in lengths),
        in_specs=[smem] * 4,
        out_specs=(smem,) * 5,
        scratch_shapes=[pltpu.SMEM((lay.inputs,), jnp.int32)],
        cost_estimate=pl.CostEstimate(flops=0, bytes_accessed=20_000_000, transcendentals=0),
    )(ids, listed, fine, stored)


def project_kernel(lay, owner, slot_of, valid, sizes, *refs):
    n_coarse = 2 * (2 * lay.near - 1)
    given_in, given_coarse = refs[: lay.cols], list(refs[lay.cols : lay.cols + n_coarse])
    out, right, blocks, sems = refs[lay.cols + n_coarse :]
    copies = []

    def fetch(source, target):
        copies.append(pltpu.make_async_copy(source, target, sems.at[len(copies)]))
        copies[-1].start()

    for i in range(lay.cols):
        fetch(given_in[i].at[:, pl.ds(0, lay.pairs)], right.at[pl.ds(i * lay.blocks, lay.blocks)])
    for i in range(2 * lay.near):
        first = given_coarse.pop(0)
        for a in range(first.shape[0]):
            fetch(first.at[a], blocks.at[a, pl.ds(i * lay.slots_dev, lay.slots_dev)])
        if i < 2:
            continue
        rest = given_coarse.pop(0)
        for a in range(1, lay.points):
            for at in range(lay.slots_dev):
                row = lay.blocks * lay.side + ((a - 1) * lay.slots_dev + at) * lay.pairs
                fetch(rest.at[pl.ds(row, lay.pairs)], blocks.at[a, i * lay.slots_dev + at])
    for copy in copies:
        copy.wait()
    found = sizes[1 + owner]

    def visit(step, carry):
        for lane in range(2):
            i = valid[owner * (lay.spread + 1) + jnp.minimum(2 * step + lane, found - 1)]
            slot = slot_of[owner * lay.spread + i]
            for a in range(lay.points):
                out[i, :, a * lay.side : (a + 1) * lay.side] = jnp.dot(
                    blocks[a, slot], right[i], preferred_element_type=jnp.float32
                ).astype(jnp.bfloat16)
        return carry

    lax.fori_loop(0, lax.div(found + 1, 2), visit, 0)


def project(lay, owner, plan, inputs, coarse):
    smem = pl.BlockSpec(memory_space=pltpu.SMEM)
    hbm = pl.BlockSpec(memory_space=pl.ANY)
    shape = (lay.spread, lay.pairs, lay.points * lay.side)
    return pl.pallas_call(
        functools.partial(project_kernel, lay, owner),
        out_shape=jax.ShapeDtypeStruct(shape, jnp.bfloat16),
        in_specs=[smem] * 3 + [hbm] * (len(inputs) + len(coarse)),
        out_specs=pl.BlockSpec(memory_space=pltpu.VMEM),
        scratch_shapes=[
            pltpu.VMEM((lay.spread, lay.pairs, lay.side), jnp.bfloat16),
            pltpu.VMEM((lay.points, lay.slots, lay.pairs, lay.pairs), jnp.bfloat16),
            pltpu.SemaphoreType.DMA((len(inputs) + lay.slots * lay.points,)),
        ],
        compiler_params=pltpu.CompilerParams(vmem_limit_bytes=lay.vmem),
        cost_estimate=pl.CostEstimate(flops=1_000_000_000, bytes_accessed=20_000_000, transcendentals=0),
    )(*plan[:3], *inputs, *coarse)


def add_products(lay, group, group_input, entries, tiles, rounded, total):
    held = tiles[pl.ds(group * lay.unroll, lay.unroll)].reshape(lay.unroll * lay.side, lay.side)
    products = jnp.dot(held, rounded[group_input[group]], preferred_element_type=jnp.float32)
    for i in range(lay.unroll):
        q = lax.div(entries[group * lay.unroll + i], lay.points)
        total[q] = total[q] + products[i * lay.side : (i + 1) * lay.side]


def turn_own_kernel(lay, given, coarse, turned, mixed):
    for t in range(lay.blocks):
        block = given[t, 0 : lay.pairs, :].T
        turned[t] = block
        mixed[t * lay.side : (t + 1) * lay.side, :] = block
    row = lay.blocks * lay.side
    for a in range(1, lay.points):
        for at in range(lay.slots_dev):
            mixed[row : row + lay.pairs, :] = coarse[a, at]
            row += lay.pairs


def turn_own(lay, joined, coarse):
    vmem = pl.BlockSpec(memory_space=pltpu.VMEM)
    rows = lay.blocks * lay.side + (lay.points - 1) * lay.slots_dev * lay.pairs
    return pl.pallas_call(
        functools.partial(turn_own_kernel, lay),
        out_shape=(
            jax.ShapeDtypeStruct((lay.blocks, lay.side, lay.pairs), jnp.bfloat16),
            jax.ShapeDtypeStruct((rows, lay.pairs), jnp.bfloat16),
        ),
        in_specs=[vmem] * 2,
        out_specs=(vmem,) * 2,
        compiler_params=pltpu.CompilerParams(vmem_limit_bytes=16 * mib),
        cost_estimate=pl.CostEstimate(flops=1_000_000, bytes_accessed=5_000_000, transcendentals=0),
    )(joined, coarse)


def turn_both_kernel(lay, given, own, out):
    out[0 : lay.blocks] = own[...]
    for t in range(lay.blocks):
        out[lay.blocks + t] = given[t, 0 : lay.pairs, :].T


def turn_both(lay, partner, own):
    vmem = pl.BlockSpec(memory_space=pltpu.VMEM)
    return pl.pallas_call(
        functools.partial(turn_both_kernel, lay),
        out_shape=jax.ShapeDtypeStruct((2 * lay.blocks, lay.side, lay.pairs), jnp.bfloat16),
        in_specs=[vmem] * 2,
        out_specs=vmem,
        compiler_params=pltpu.CompilerParams(vmem_limit_bytes=16 * mib),
        cost_estimate=pl.CostEstimate(flops=1_000_000, bytes_accessed=5_000_000, transcendentals=0),
    )(partner, own)


def tiles_kernel(lay, sizes, group_input, entries, *refs):
    n_in = lay.owners * lay.cols
    lines = lay.line_steps()
    refs = list(refs)
    given_in = [refs.pop(0) for _ in range(n_in)]
    given_out = [refs.pop(0) for _ in range(2 * (1 + len(lines)))]
    given_projected = [refs.pop(0) for _ in range(lay.owners)]
    own_sum, other_sum, tiles_out = refs[:3]
    left, rounded, tiles, total, sems, out_sems = refs[3:]
    copies = []

    def fetch(source, target):
        copies.append(pltpu.make_async_copy(source, target, sems.at[len(copies)]))
        copies[-1].start()

    for k in range(2):
        held = given_out[k * (1 + len(lines)) :]
        for g in range(lay.owners):
            spot = (k * lay.places + g * lay.near) * lay.blocks
            fetch(held[0].at[pl.ds(g * lay.blocks, lay.blocks)], left.at[pl.ds(spot, lay.blocks)])
        for i, d in enumerate(lines):
            spot = (k * lay.places + d) * lay.blocks
            if d > lay.near:
                fetch(held[1 + i], left.at[pl.ds(spot, lay.blocks)])
            else:
                for t in range(lay.blocks):
                    fetch(held[1 + i].at[pl.ds(t * lay.side, lay.side)], left.at[spot + t])
    for i in range(n_in):
        part = pl.ds(i * lay.blocks, lay.blocks)
        fetch(given_in[i].at[:, pl.ds(lay.pairs, lay.side)], rounded.at[part])
    total[...] = jnp.zeros_like(total)
    for copy in copies:
        copy.wait()
    used = sizes[0]

    for g in range(lay.owners):

        def group_step(group, carry):
            right = given_projected[g][group_input[group] - g * lay.spread]
            numbers = [entries[group * lay.unroll + i] for i in range(lay.unroll)]
            places = [jnp.minimum(lax.div(n, lay.points), lay.outputs - 1) for n in numbers]
            lefts = jnp.concatenate([left[q] for q in places], axis=0)
            both = jnp.dot(lefts, right, preferred_element_type=jnp.float32)
            for i in range(lay.unroll):
                mine = both[i * lay.side : (i + 1) * lay.side]
                tile = mine[:, : lay.side]
                for b in range(1, lay.points):
                    at_b = mine[:, b * lay.side : (b + 1) * lay.side]
                    tile = jnp.where(lax.rem(numbers[i], lay.points) == b, at_b, tile)
                tiles[group * lay.unroll + i] = tile.astype(jnp.bfloat16)
            add_products(lay, group - 1, group_input, entries, tiles, rounded, total)
            return carry

        first = 1 if g == 0 else sizes[lay.owners + g]
        last = used if g == lay.owners - 1 else sizes[lay.owners + g + 1]
        lax.fori_loop(first, last, group_step, 0)
    span = chunk_groups * lay.unroll

    def store(chunk):
        part = pl.ds(chunk * span, span)
        return pltpu.make_async_copy(tiles.at[part], tiles_out.at[part], out_sems.at[chunk])

    for chunk in range(lay.groups // chunk_groups):

        @pl.when(used > chunk * chunk_groups)
        def _():
            store(chunk).start()

    add_products(lay, used - 1, group_input, entries, tiles, rounded, total)
    own = lay.places * lay.blocks
    own_sum[...] = total[0:own]
    other_sum[...] = total[own : 2 * own]
    for chunk in range(lay.groups // chunk_groups):

        @pl.when(used > chunk * chunk_groups)
        def _():
            store(chunk).wait()


def make_tiles(lay, plan, inputs, outputs, projected):
    smem = pl.BlockSpec(memory_space=pltpu.SMEM)
    hbm = pl.BlockSpec(memory_space=pl.ANY)
    vmem = pl.BlockSpec(memory_space=pltpu.VMEM)
    own = lay.places * lay.blocks
    sums = jax.ShapeDtypeStruct((own, lay.side, lay.width), jnp.float32)
    n_copies = len(inputs) + 2 * lay.places * lay.blocks
    tiles = (lay.groups * lay.unroll, lay.side, lay.side)
    return pl.pallas_call(
        functools.partial(tiles_kernel, lay),
        out_shape=(sums, sums, jax.ShapeDtypeStruct(tiles, jnp.bfloat16)),
        in_specs=[smem] * 3 + [hbm] * (len(inputs) + len(outputs)) + [vmem] * len(projected),
        out_specs=(vmem, vmem, hbm),
        scratch_shapes=[
            pltpu.VMEM((lay.outputs, lay.side, lay.pairs), jnp.bfloat16),
            pltpu.VMEM((lay.inputs, lay.side, lay.width), jnp.bfloat16),
            pltpu.VMEM(tiles, jnp.bfloat16),
            pltpu.VMEM((lay.outputs + 1, lay.side, lay.width), jnp.float32),
            pltpu.SemaphoreType.DMA((n_copies,)),
            pltpu.SemaphoreType.DMA((lay.groups // chunk_groups,)),
        ],
        compiler_params=pltpu.CompilerParams(vmem_limit_bytes=lay.vmem),
        cost_estimate=pl.CostEstimate(flops=4_000_000_000, bytes_accessed=30_000_000, transcendentals=0),
    )(plan[2], *plan[3:], *inputs, *outputs, *projected)


def apply_kernel(lay, sizes, group_input, entries, tiles_in, *refs):
    given_vec = refs[: lay.cols]
    own_sum, other_sum = refs[lay.cols : lay.cols + 2]
    rounded, tiles, total, sems, out_sems = refs[lay.cols + 2 :]
    used = sizes[0]
    span = chunk_groups * lay.unroll

    def load(chunk):
        part = pl.ds(chunk * span, span)
        return pltpu.make_async_copy(tiles_in.at[part], tiles.at[part], out_sems.at[chunk])

    for chunk in range(lay.groups // chunk_groups):

        @pl.when(used > chunk * chunk_groups)
        def _():
            load(chunk).start()

    copies = []
    for d in range(lay.cols):
        for g in range(lay.owners):
            target = rounded.at[pl.ds((g * lay.cols + d) * lay.blocks, lay.blocks)]
            copies.append(pltpu.make_async_copy(given_vec[d].at[g], target, sems.at[len(copies)]))
            copies[-1].start()
    total[...] = jnp.zeros_like(total)
    for copy in copies:
        copy.wait()
    for chunk in range(lay.groups // chunk_groups):

        @pl.when(used > chunk * chunk_groups)
        def _():
            load(chunk).wait()

    def group_step(group, carry):
        add_products(lay, group, group_input, entries, tiles, rounded, total)
        return carry

    lax.fori_loop(1, used, group_step, 0)
    own = lay.places * lay.blocks
    own_sum[...] = total[0:own]
    other_sum[...] = total[own : 2 * own]


def apply_tiles(lay, plan, tiles, rounded):
    smem = pl.BlockSpec(memory_space=pltpu.SMEM)
    hbm = pl.BlockSpec(memory_space=pl.ANY)
    vmem = pl.BlockSpec(memory_space=pltpu.VMEM)
    own = lay.places * lay.blocks
    sums = jax.ShapeDtypeStruct((own, lay.side, lay.width), jnp.float32)
    return pl.pallas_call(
        functools.partial(apply_kernel, lay),
        out_shape=(sums, sums),
        in_specs=[smem] * 3 + [hbm] * (1 + len(rounded)),
        out_specs=(vmem, vmem),
        scratch_shapes=[
            pltpu.VMEM((lay.inputs, lay.side, lay.width), jnp.bfloat16),
            pltpu.VMEM(tiles.shape, jnp.bfloat16),
            pltpu.VMEM((lay.outputs + 1, lay.side, lay.width), jnp.float32),
            pltpu.SemaphoreType.DMA((len(rounded) * lay.owners,)),
            pltpu.SemaphoreType.DMA((lay.groups // chunk_groups,)),
        ],
        compiler_params=pltpu.CompilerParams(vmem_limit_bytes=lay.vmem),
        cost_estimate=pl.CostEstimate(flops=400_000_000, bytes_accessed=4_000_000, transcendentals=0),
    )(plan[2], *plan[3:], tiles, *rounded)


def on_device(
    vectors, energies, intersections, coarse, fine_coarse, coarse_slot, tile_codes, tile_count
):
    rows = lax.axis_size("row")
    cols = lax.axis_size("col")
    row_id = lax.axis_index("row")
    col_id = lax.axis_index("col")
    blocks, pairs, side = intersections.shape
    width = vectors.shape[1]
    points, slots_dev = coarse.shape[:2]
    lay = Layout(rows, cols, blocks, pairs, side, width, points, slots_dev, tile_codes.shape[1], 4)
    if lay.groups * lay.unroll * side * side * 2 > 16 * mib:
        lay = Layout(rows, cols, blocks, pairs, side, width, points, slots_dev, tile_codes.shape[1], 1)
    near = lay.near

    def move(array, row_step, col_step):
        pairs_list = [
            (r * cols + c, (r ^ row_step) * cols + (c ^ col_step)) for r in range(rows) for c in range(cols)
        ]
        return lax.ppermute(array, axes, pairs_list)

    def along(array, step):
        return move(array, 2 * step, 0)

    def to_core(array):
        return move(array, 1, 0)

    def in_plane(array):
        return [array] + [move(array, 0, d) for d in range(1, cols)]

    start = vectors.reshape(blocks, side, width)
    energy = energies.reshape(blocks, side, 1)
    two_owners = lay.owners == 2
    ids = jnp.stack([row_id // 2, row_id % 2, col_id]).astype(jnp.int32)
    listed = jnp.concatenate([tile_codes, tile_count[:, None]], axis=1)
    n_listed = listed.shape[1]
    digits = jnp.concatenate([listed[0] >> 8, listed[0] & 255]).astype(jnp.bfloat16)
    depth = 16 * -(-2 * n_listed // (16 * width * blocks))
    digits = jnp.pad(digits, (0, blocks * depth * width - 2 * n_listed)).reshape(blocks, depth, width)
    joined = jnp.concatenate([intersections, start.astype(jnp.bfloat16), digits], axis=1)

    partner = [along(joined, near)] if two_owners else []
    inputs = in_plane(joined)
    late_coarse, late_joined = lax.optimization_barrier((coarse, joined))
    near_coarse = [along(late_coarse[:1], e) for e in range(1, near)]
    turned, mixed = turn_own(lay, late_joined, late_coarse)
    held = (partner, inputs, near_coarse, turned, mixed)
    partner, inputs, near_coarse, turned, mixed = lax.optimization_barrier(held)
    if two_owners:
        sent = partner[0][:, pairs + side :].reshape(-1)[: 2 * n_listed].astype(jnp.int32)
        listed = jnp.concatenate([listed, ((sent[:n_listed] << 8) + sent[n_listed:])[None]], axis=0)
    plan = make_plan(lay, ids, listed, fine_coarse, coarse_slot)
    for part in partner:
        inputs = inputs + in_plane(part)
    lines = [along(mixed if d < near else turned, d) for d in lay.line_steps()]
    for part in partner:
        turned = turn_both(lay, part, turned)
    held = (inputs, turned, lines, near_coarse, plan, coarse)
    inputs, turned, lines, near_coarse, plan, coarse = lax.optimization_barrier(held)
    blocks_coarse = [coarse, to_core(coarse)]
    lefts = [turned] + lines
    lefts_core = [to_core(part) for part in lefts]
    for e in range(1, near):
        first_rows = near_coarse[e - 1]
        blocks_coarse += [first_rows, lefts[e], to_core(first_rows), lefts_core[e]]
    lefts = lefts + lefts_core
    projected = [
        project(lay, g, plan, inputs[g * cols : (g + 1) * cols], blocks_coarse) for g in range(lay.owners)
    ]
    own_sum, other_sum, tiles = make_tiles(lay, plan, inputs, lefts, projected)

    def over_core(own_part, other_part):
        return (own_part + to_core(other_part)).reshape(lay.places, blocks, side, width)

    def shifted_part(field):
        return energy * field - spectrum_center * field

    merged = over_core(own_sum, other_sum)
    if two_owners:
        sums = jnp.stack([merged[0] + shifted_part(start), merged[near]])
        for e in range(1, near):
            sent = jnp.stack([merged[e], merged[e ^ near]]).astype(jnp.bfloat16)
            sums = sums + along(sent, e).astype(jnp.float32)
        sums = sums + along(sums.astype(jnp.bfloat16), near)[::-1].astype(jnp.float32)
    else:
        sums = merged + shifted_part(start)[None]

    firsts = sums / spectrum_half
    first = firsts[0]
    own_sum, other_sum = apply_tiles(lay, plan, tiles, in_plane(firsts.astype(jnp.bfloat16)))
    merged = over_core(own_sum, other_sum)
    last = merged[0]
    for d in range(1, lay.places):
        last = last + along(merged[d].astype(jnp.bfloat16), d).astype(jnp.float32)
    second = 2.0 * ((shifted_part(first) + last) / spectrum_half) - start
    return first.reshape(vectors.shape), second.reshape(vectors.shape)


def solution(mesh):
    in_specs = (
        P(axes, None),
        P(axes),
        P(axes, None, None),
        P("col", "row", None, None),
        P(),
        P(),
        P(axes, None),
        P(axes),
    )
    out_specs = (P(axes, None), P(axes, None))
    return jax.shard_map(
        on_device, mesh=mesh, in_specs=in_specs, out_specs=out_specs, check_vma=False
    )
```

```python
import functools

import jax
import jax.numpy as jnp
from jax import lax
from jax.experimental import pallas as pl
from jax.experimental.pallas import tpu as pltpu
from jax.sharding import PartitionSpec as P

spectrum_center = 2.0
spectrum_half = 3.0
axes = ("row", "col")
chunk_groups = 8
mib = 1 << 20


class Layout:
    def __init__(self, rows, cols, blocks, pairs, side, width, points, slots_dev, tile_max, unroll):
        self.rows, self.cols, self.blocks = rows, cols, blocks
        self.pairs, self.side, self.width = pairs, side, width
        self.points, self.slots_dev, self.tile_max = points, slots_dev, tile_max
        self.places = rows // 2
        self.near = max(self.places // 2, 1)
        self.owners = 2 if self.places > 1 else 1
        self.spread = cols * blocks
        self.inputs = self.owners * self.spread
        self.outputs = rows * blocks
        self.slots = 2 * self.near * slots_dev
        self.unroll = unroll
        self.vmem = 60 * mib
        most = self.owners * tile_max + self.inputs * (unroll - 1) + unroll
        self.groups = -(-most // (unroll * chunk_groups)) * chunk_groups

    def line_steps(self):
        return [d for d in range(1, self.places) if d != self.near]


def plan_kernel(lay, ids, listed, fine, stored, slot_of, valid, sizes, group_input, entries, fill):
    place, core, col = ids[0], ids[1], ids[2]
    half = lax.div(place, lay.near)
    blank = lay.outputs * lay.points

    for owner in range(lay.owners):

        def examine(i, found):
            p = owner * lay.spread + i
            from_col = lax.bitwise_xor(lax.div(i, lay.blocks), col)
            from_place = lax.bitwise_xor(place, owner * lay.near)
            block = ((from_place * 2 + core) * lay.cols + from_col) * lay.blocks + lax.rem(i, lay.blocks)
            position = stored[fine[block]]
            at_row = lax.div(position, lay.slots_dev)
            at_place, at_core = lax.div(at_row, 2), lax.rem(at_row, 2)
            slot = (lax.bitwise_xor(at_place, place) * 2 + lax.bitwise_xor(at_core, core)) * lay.slots_dev
            slot = slot + lax.rem(position, lay.slots_dev)
            here = lax.div(at_place, lay.near) == half
            slot_of[p] = jnp.where(here, slot, -1)
            valid[owner * (lay.spread + 1) + found] = i
            fill[p] = 0
            return found + here.astype(jnp.int32)

        sizes[1 + owner] = lax.fori_loop(0, lay.spread, examine, 0)

    def input_of(owner, code):
        j = lax.rem(code, lay.spread)
        from_col = lax.bitwise_xor(lax.div(j, lay.blocks), col)
        return owner * lay.spread + from_col * lay.blocks + lax.rem(j, lay.blocks)

    for owner in range(lay.owners):

        def count(i, carry):
            p = input_of(owner, listed[owner, i])
            fill[p] = fill[p] + 1
            return carry

        lax.fori_loop(0, listed[owner, lay.tile_max], count, 0)

    group_input[0] = 0

    def place_groups(p, start):
        used = jnp.where(slot_of[p] >= 0, fill[p], 0)
        fill[p] = start * lay.unroll
        end = start + lax.div(used + (lay.unroll - 1), lay.unroll)

        def name(group, carry):
            group_input[group] = p
            return carry

        lax.fori_loop(start, end, name, 0)
        return end

    total = 1
    for owner in range(lay.owners):
        if owner > 0:
            sizes[lay.owners + owner] = total
        total = lax.fori_loop(owner * lay.spread, (owner + 1) * lay.spread, place_groups, total)
    sizes[0] = total

    def clear(i, carry):
        entries[i] = blank
        return carry

    lax.fori_loop(0, total * lay.unroll, clear, 0)

    for owner in range(lay.owners):

        def put(i, carry):
            code = listed[owner, i]
            p = input_of(owner, code)

            @pl.when(slot_of[p] >= 0)
            def _():
                out = lax.div(code, lay.spread)
                at_row = lax.div(out, lay.blocks)
                within = lax.rem(out, lay.blocks)
                far = lax.bitwise_xor(lax.div(at_row, 2), place)
                other = lax.bitwise_xor(lax.rem(at_row, 2), core)
                q = (other * lay.places + far) * lay.blocks + within
                a = fine[(at_row * lay.cols + col) * lay.blocks + within] - col * lay.points
                spot = fill[p]
                entries[spot] = q * lay.points + a
                fill[p] = spot + 1

            return carry

        lax.fori_loop(0, listed[owner, lay.tile_max], put, 0)


def make_plan(lay, ids, listed, fine, stored):
    smem = pl.BlockSpec(memory_space=pltpu.SMEM)
    lengths = (
        lay.inputs,
        lay.owners * (lay.spread + 1),
        2 * lay.owners,
        lay.groups,
        lay.groups * lay.unroll,
    )
    return pl.pallas_call(
        functools.partial(plan_kernel, lay),
        out_shape=tuple(jax.ShapeDtypeStruct((n,), jnp.int32) for n in lengths),
        in_specs=[smem] * 4,
        out_specs=(smem,) * 5,
        scratch_shapes=[pltpu.SMEM((lay.inputs,), jnp.int32)],
        cost_estimate=pl.CostEstimate(flops=0, bytes_accessed=20_000_000, transcendentals=0),
    )(ids, listed, fine, stored)


def add_products(lay, group, group_input, entries, tiles, rounded, total):
    held = tiles[pl.ds(group * lay.unroll, lay.unroll)].reshape(lay.unroll * lay.side, lay.side)
    products = jnp.dot(held, rounded[group_input[group]], preferred_element_type=jnp.float32)
    for i in range(lay.unroll):
        q = lax.div(entries[group * lay.unroll + i], lay.points)
        total[q] = total[q] + products[i * lay.side : (i + 1) * lay.side]


def turn_own_kernel(lay, given, coarse, turned, mixed):
    for t in range(lay.blocks):
        block = given[t, 0 : lay.pairs, :].T
        turned[t] = block
        mixed[t * lay.side : (t + 1) * lay.side, :] = block
    row = lay.blocks * lay.side
    for a in range(1, lay.points):
        for at in range(lay.slots_dev):
            mixed[row : row + lay.pairs, :] = coarse[a, at]
            row += lay.pairs


def turn_own(lay, joined, coarse):
    vmem = pl.BlockSpec(memory_space=pltpu.VMEM)
    rows = lay.blocks * lay.side + (lay.points - 1) * lay.slots_dev * lay.pairs
    return pl.pallas_call(
        functools.partial(turn_own_kernel, lay),
        out_shape=(
            jax.ShapeDtypeStruct((lay.blocks, lay.side, lay.pairs), jnp.bfloat16),
            jax.ShapeDtypeStruct((rows, lay.pairs), jnp.bfloat16),
        ),
        in_specs=[vmem] * 2,
        out_specs=(vmem,) * 2,
        compiler_params=pltpu.CompilerParams(vmem_limit_bytes=16 * mib),
        cost_estimate=pl.CostEstimate(flops=1_000_000, bytes_accessed=5_000_000, transcendentals=0),
    )(joined, coarse)


def turn_both_kernel(lay, given, own, out):
    out[0 : lay.blocks] = own[...]
    for t in range(lay.blocks):
        out[lay.blocks + t] = given[t, 0 : lay.pairs, :].T


def turn_both(lay, partner, own):
    vmem = pl.BlockSpec(memory_space=pltpu.VMEM)
    return pl.pallas_call(
        functools.partial(turn_both_kernel, lay),
        out_shape=jax.ShapeDtypeStruct((2 * lay.blocks, lay.side, lay.pairs), jnp.bfloat16),
        in_specs=[vmem] * 2,
        out_specs=vmem,
        compiler_params=pltpu.CompilerParams(vmem_limit_bytes=16 * mib),
        cost_estimate=pl.CostEstimate(flops=1_000_000, bytes_accessed=5_000_000, transcendentals=0),
    )(partner, own)


def tiles_kernel(lay, slot_of, valid, sizes, group_input, entries, *refs):
    lines = lay.line_steps()
    refs = list(refs)
    given_in = [refs.pop(0) for _ in range(lay.owners * lay.cols)]
    given_out = [refs.pop(0) for _ in range(2 * (1 + len(lines)))]
    given_coarse = [refs.pop(0) for _ in range(2 * (2 * lay.near - 1))]
    own_sum, other_sum, tiles_out = refs[:3]
    right, left, blocks, projected, rounded, tiles, total, sems, sum_sems, out_sems = refs[3:]
    started, waited = [], []

    def fetch(source, target):
        started.append(pltpu.make_async_copy(source, target, sems.at[len(started) + len(waited)]))
        started[-1].start()

    def arrive(count):
        for copy in started[:count]:
            copy.wait()
        waited.extend(started[:count])
        del started[:count]

    def fetch_inputs(owner):
        for i in range(owner * lay.cols, (owner + 1) * lay.cols):
            part = pl.ds(i * lay.blocks, lay.blocks)
            fetch(given_in[i].at[:, pl.ds(0, lay.pairs)], right.at[part])

    for i in range(2 * lay.near):
        first = given_coarse.pop(0)
        for a in range(first.shape[0]):
            fetch(first.at[a], blocks.at[a, pl.ds(i * lay.slots_dev, lay.slots_dev)])
        if i < 2:
            continue
        rest = given_coarse.pop(0)
        for a in range(1, lay.points):
            for at in range(lay.slots_dev):
                row = lay.blocks * lay.side + ((a - 1) * lay.slots_dev + at) * lay.pairs
                fetch(rest.at[pl.ds(row, lay.pairs)], blocks.at[a, i * lay.slots_dev + at])
    fetch_inputs(0)
    for_projection = len(started)
    for k in range(2):
        held = given_out[k * (1 + len(lines)) :]
        for g in range(lay.owners):
            spot = (k * lay.places + g * lay.near) * lay.blocks
            fetch(held[0].at[pl.ds(g * lay.blocks, lay.blocks)], left.at[pl.ds(spot, lay.blocks)])
        for i, d in enumerate(lines):
            spot = (k * lay.places + d) * lay.blocks
            if d > lay.near:
                fetch(held[1 + i], left.at[pl.ds(spot, lay.blocks)])
            else:
                for t in range(lay.blocks):
                    fetch(held[1 + i].at[pl.ds(t * lay.side, lay.side)], left.at[spot + t])
    for i, ref in enumerate(given_in):
        part = pl.ds(i * lay.blocks, lay.blocks)
        fetch(ref.at[:, pl.ds(lay.pairs, lay.side)], rounded.at[part])
    for_tiles = len(started) - for_projection
    for owner in range(1, lay.owners):
        fetch_inputs(owner)
    total[...] = jnp.zeros_like(total)
    arrive(for_projection)
    used = sizes[0]

    for owner in range(lay.owners):
        found = sizes[1 + owner]

        def visit(step, carry):
            for lane in range(2):
                i = valid[owner * (lay.spread + 1) + jnp.minimum(2 * step + lane, found - 1)]
                p = owner * lay.spread + i
                for a in range(lay.points):
                    projected[i, :, a * lay.side : (a + 1) * lay.side] = jnp.dot(
                        blocks[a, slot_of[p]], right[p], preferred_element_type=jnp.float32
                    ).astype(jnp.bfloat16)
            return carry

        lax.fori_loop(0, lax.div(found + 1, 2), visit, 0)
        arrive(for_tiles if owner == 0 else 0)

        def group_step(group, carry):
            block = projected[group_input[group] - owner * lay.spread]
            numbers = [entries[group * lay.unroll + i] for i in range(lay.unroll)]
            places = [jnp.minimum(lax.div(n, lay.points), lay.outputs - 1) for n in numbers]
            lefts = jnp.concatenate([left[q] for q in places], axis=0)
            both = jnp.dot(lefts, block, preferred_element_type=jnp.float32)
            for i in range(lay.unroll):
                mine = both[i * lay.side : (i + 1) * lay.side]
                tile = mine[:, : lay.side]
                for b in range(1, lay.points):
                    at_b = mine[:, b * lay.side : (b + 1) * lay.side]
                    tile = jnp.where(lax.rem(numbers[i], lay.points) == b, at_b, tile)
                tiles[group * lay.unroll + i] = tile.astype(jnp.bfloat16)
            add_products(lay, group - 1, group_input, entries, tiles, rounded, total)
            return carry

        first = 1 if owner == 0 else sizes[lay.owners + owner]
        last = used if owner == lay.owners - 1 else sizes[lay.owners + owner + 1]
        lax.fori_loop(first, last, group_step, 0)
        if owner < lay.owners - 1:
            arrive(lay.cols)

    span = chunk_groups * lay.unroll

    def store(chunk):
        part = pl.ds(chunk * span, span)
        return pltpu.make_async_copy(tiles.at[part], tiles_out.at[part], out_sems.at[chunk])

    for chunk in range(lay.groups // chunk_groups):

        @pl.when(used > chunk * chunk_groups)
        def _():
            store(chunk).start()

    add_products(lay, used - 1, group_input, entries, tiles, rounded, total)
    give_sums(lay, total, own_sum, other_sum, sum_sems)
    for chunk in range(lay.groups // chunk_groups):

        @pl.when(used > chunk * chunk_groups)
        def _():
            store(chunk).wait()


def give_sums(lay, total, own_sum, other_sum, sems):
    own = lay.places * lay.blocks
    for copy in (
        pltpu.make_async_copy(total.at[pl.ds(own, own)], other_sum, sems.at[1]),
        pltpu.make_async_copy(total.at[pl.ds(0, own)], own_sum, sems.at[0]),
    ):
        copy.start()
    pltpu.make_async_copy(total.at[pl.ds(own, own)], other_sum, sems.at[1]).wait()
    pltpu.make_async_copy(total.at[pl.ds(0, own)], own_sum, sems.at[0]).wait()


def make_tiles(lay, plan, inputs, outputs, coarse):
    smem = pl.BlockSpec(memory_space=pltpu.SMEM)
    hbm = pl.BlockSpec(memory_space=pl.ANY)
    own = lay.places * lay.blocks
    sums = jax.ShapeDtypeStruct((own, lay.side, lay.width), jnp.float32)
    n_copies = 2 * len(inputs) + 2 * lay.places * lay.blocks + lay.slots * lay.points
    tiles = (lay.groups * lay.unroll, lay.side, lay.side)
    return pl.pallas_call(
        functools.partial(tiles_kernel, lay),
        out_shape=(sums, sums, jax.ShapeDtypeStruct(tiles, jnp.bfloat16)),
        in_specs=[smem] * 5 + [hbm] * (len(inputs) + len(outputs) + len(coarse)),
        out_specs=(hbm,) * 3,
        scratch_shapes=[
            pltpu.VMEM((lay.inputs, lay.pairs, lay.side), jnp.bfloat16),
            pltpu.VMEM((lay.outputs, lay.side, lay.pairs), jnp.bfloat16),
            pltpu.VMEM((lay.points, lay.slots, lay.pairs, lay.pairs), jnp.bfloat16),
            pltpu.VMEM((lay.spread, lay.pairs, lay.points * lay.side), jnp.bfloat16),
            pltpu.VMEM((lay.inputs, lay.side, lay.width), jnp.bfloat16),
            pltpu.VMEM(tiles, jnp.bfloat16),
            pltpu.VMEM((lay.outputs + 1, lay.side, lay.width), jnp.float32),
            pltpu.SemaphoreType.DMA((n_copies,)),
            pltpu.SemaphoreType.DMA((2,)),
            pltpu.SemaphoreType.DMA((lay.groups // chunk_groups,)),
        ],
        compiler_params=pltpu.CompilerParams(vmem_limit_bytes=lay.vmem),
        cost_estimate=pl.CostEstimate(flops=4_000_000_000, bytes_accessed=30_000_000, transcendentals=0),
    )(*plan, *inputs, *outputs, *coarse)


def apply_kernel(lay, sizes, group_input, entries, tiles_in, *refs):
    given_vec = refs[: lay.cols]
    own_sum, other_sum = refs[lay.cols : lay.cols + 2]
    rounded, tiles, total, sems, sum_sems, out_sems = refs[lay.cols + 2 :]
    used = sizes[0]
    span = chunk_groups * lay.unroll

    def load(chunk):
        part = pl.ds(chunk * span, span)
        return pltpu.make_async_copy(tiles_in.at[part], tiles.at[part], out_sems.at[chunk])

    for chunk in range(lay.groups // chunk_groups):

        @pl.when(used > chunk * chunk_groups)
        def _():
            load(chunk).start()

    copies = []
    for d in range(lay.cols):
        for g in range(lay.owners):
            target = rounded.at[pl.ds((g * lay.cols + d) * lay.blocks, lay.blocks)]
            copies.append(pltpu.make_async_copy(given_vec[d].at[g], target, sems.at[len(copies)]))
            copies[-1].start()
    total[...] = jnp.zeros_like(total)
    for copy in copies:
        copy.wait()
    for chunk in range(lay.groups // chunk_groups):

        @pl.when(used > chunk * chunk_groups)
        def _():
            load(chunk).wait()

    def group_step(group, carry):
        add_products(lay, group, group_input, entries, tiles, rounded, total)
        return carry

    lax.fori_loop(1, used, group_step, 0)
    give_sums(lay, total, own_sum, other_sum, sum_sems)


def apply_tiles(lay, plan, tiles, rounded):
    smem = pl.BlockSpec(memory_space=pltpu.SMEM)
    hbm = pl.BlockSpec(memory_space=pl.ANY)
    own = lay.places * lay.blocks
    sums = jax.ShapeDtypeStruct((own, lay.side, lay.width), jnp.float32)
    return pl.pallas_call(
        functools.partial(apply_kernel, lay),
        out_shape=(sums, sums),
        in_specs=[smem] * 3 + [hbm] * (1 + len(rounded)),
        out_specs=(hbm, hbm),
        scratch_shapes=[
            pltpu.VMEM((lay.inputs, lay.side, lay.width), jnp.bfloat16),
            pltpu.VMEM(tiles.shape, jnp.bfloat16),
            pltpu.VMEM((lay.outputs + 1, lay.side, lay.width), jnp.float32),
            pltpu.SemaphoreType.DMA((len(rounded) * lay.owners,)),
            pltpu.SemaphoreType.DMA((2,)),
            pltpu.SemaphoreType.DMA((lay.groups // chunk_groups,)),
        ],
        compiler_params=pltpu.CompilerParams(vmem_limit_bytes=lay.vmem),
        cost_estimate=pl.CostEstimate(flops=400_000_000, bytes_accessed=4_000_000, transcendentals=0),
    )(*plan[2:], tiles, *rounded)


def on_device(
    vectors, energies, intersections, coarse, fine_coarse, coarse_slot, tile_codes, tile_count
):
    rows = lax.axis_size("row")
    cols = lax.axis_size("col")
    row_id = lax.axis_index("row")
    col_id = lax.axis_index("col")
    blocks, pairs, side = intersections.shape
    width = vectors.shape[1]
    points, slots_dev = coarse.shape[:2]
    lay = Layout(rows, cols, blocks, pairs, side, width, points, slots_dev, tile_codes.shape[1], 4)
    if lay.groups * lay.unroll * side * side * 2 > 16 * mib:
        lay = Layout(rows, cols, blocks, pairs, side, width, points, slots_dev, tile_codes.shape[1], 1)
    near = lay.near

    def move(array, row_step, col_step):
        pairs_list = [
            (r * cols + c, (r ^ row_step) * cols + (c ^ col_step)) for r in range(rows) for c in range(cols)
        ]
        return lax.ppermute(array, axes, pairs_list)

    def along(array, step):
        return move(array, 2 * step, 0)

    def to_core(array):
        return move(array, 1, 0)

    def in_plane(array):
        return [array] + [move(array, 0, d) for d in range(1, cols)]

    start = vectors.reshape(blocks, side, width)
    energy = energies.reshape(blocks, side, 1)
    two_owners = lay.owners == 2
    ids = jnp.stack([row_id // 2, row_id % 2, col_id]).astype(jnp.int32)
    listed = jnp.concatenate([tile_codes, tile_count[:, None]], axis=1)
    n_listed = listed.shape[1]
    digits = jnp.concatenate([listed[0] >> 8, listed[0] & 255]).astype(jnp.bfloat16)
    depth = 16 * -(-2 * n_listed // (16 * width * blocks))
    digits = jnp.pad(digits, (0, blocks * depth * width - 2 * n_listed)).reshape(blocks, depth, width)
    joined = jnp.concatenate([intersections, start.astype(jnp.bfloat16), digits], axis=1)

    inputs = in_plane(joined)
    partner = [along(joined, near)] if two_owners else []
    late_coarse, late_joined = lax.optimization_barrier((coarse, joined))
    near_coarse = [along(late_coarse[:1], e) for e in range(1, near)]
    turned, mixed = turn_own(lay, late_joined, late_coarse)
    held = (partner, inputs, near_coarse, turned, mixed)
    partner, inputs, near_coarse, turned, mixed = lax.optimization_barrier(held)
    if two_owners:
        sent = partner[0][:, pairs + side :].reshape(-1)[: 2 * n_listed].astype(jnp.int32)
        listed = jnp.concatenate([listed, ((sent[:n_listed] << 8) + sent[n_listed:])[None]], axis=0)
    plan = make_plan(lay, ids, listed, fine_coarse, coarse_slot)
    for part in partner:
        inputs = inputs + in_plane(part)
    lines = [along(mixed if d < near else turned, d) for d in lay.line_steps()]
    for part in partner:
        turned = turn_both(lay, part, turned)
    held = (inputs, turned, lines, near_coarse, plan, coarse)
    inputs, turned, lines, near_coarse, plan, coarse = lax.optimization_barrier(held)
    blocks_coarse = [coarse, to_core(coarse)]
    lefts = [turned] + lines
    lefts_core = [to_core(part) for part in lefts]
    for e in range(1, near):
        first_rows = near_coarse[e - 1]
        blocks_coarse += [first_rows, lefts[e], to_core(first_rows), lefts_core[e]]
    lefts = lefts + lefts_core
    own_sum, other_sum, tiles = make_tiles(lay, plan, inputs, lefts, blocks_coarse)

    def over_core(own_part, other_part):
        return (own_part + to_core(other_part)).reshape(lay.places, blocks, side, width)

    def shifted_part(field):
        return energy * field - spectrum_center * field

    merged = over_core(own_sum, other_sum)
    if two_owners:
        sums = jnp.stack([merged[0] + shifted_part(start), merged[near]])
        for e in range(1, near):
            sent = jnp.stack([merged[e], merged[e ^ near]]).astype(jnp.bfloat16)
            sums = sums + along(sent, e).astype(jnp.float32)
        sums = sums + along(sums.astype(jnp.bfloat16), near)[::-1].astype(jnp.float32)
    else:
        sums = merged + shifted_part(start)[None]

    firsts = sums / spectrum_half
    first = firsts[0]
    own_sum, other_sum = apply_tiles(lay, plan, tiles, in_plane(firsts.astype(jnp.bfloat16)))
    merged = over_core(own_sum, other_sum)
    last = merged[0]
    for d in range(1, lay.places):
        last = last + along(merged[d].astype(jnp.bfloat16), d).astype(jnp.float32)
    second = 2.0 * ((shifted_part(first) + last) / spectrum_half) - start
    return first.reshape(vectors.shape), second.reshape(vectors.shape)


def solution(mesh):
    in_specs = (
        P(axes, None),
        P(axes),
        P(axes, None, None),
        P("col", "row", None, None),
        P(),
        P(),
        P(axes, None),
        P(axes),
    )
    out_specs = (P(axes, None), P(axes, None))
    return jax.shard_map(
        on_device, mesh=mesh, in_specs=in_specs, out_specs=out_specs, check_vma=False
    )
```

```python
import functools

import jax
import jax.numpy as jnp
from jax import lax
from jax.experimental import pallas as pl
from jax.experimental.pallas import tpu as pltpu
from jax.sharding import PartitionSpec as P

spectrum_center = 2.0
spectrum_half = 3.0
axes = ("row", "col")
chunk_groups = 8
mib = 1 << 20


class Layout:
    def __init__(self, rows, cols, blocks, pairs, side, width, points, slots_dev, tile_max, unroll):
        self.rows, self.cols, self.blocks = rows, cols, blocks
        self.pairs, self.side, self.width = pairs, side, width
        self.points, self.slots_dev, self.tile_max = points, slots_dev, tile_max
        self.places = rows // 2
        self.near = max(self.places // 2, 1)
        self.owners = 2 if self.places > 1 else 1
        self.spread = cols * blocks
        self.inputs = self.owners * self.spread
        self.outputs = rows * blocks
        self.slots = 2 * self.near * slots_dev
        self.unroll = unroll
        self.vmem = 60 * mib
        most = self.owners * tile_max + self.inputs * (unroll - 1) + unroll
        self.groups = -(-most // (unroll * chunk_groups)) * chunk_groups

    def line_steps(self):
        return [d for d in range(1, self.places) if d != self.near]


def plan_kernel(lay, ids, listed, fine, stored, slot_of, valid, sizes, group_input, entries, fill):
    place, core, col = ids[0], ids[1], ids[2]
    half = lax.div(place, lay.near)
    blank = lay.outputs * lay.points

    for owner in range(lay.owners):

        def examine(i, found):
            p = owner * lay.spread + i
            from_col = lax.bitwise_xor(lax.div(i, lay.blocks), col)
            from_place = lax.bitwise_xor(place, owner * lay.near)
            block = ((from_place * 2 + core) * lay.cols + from_col) * lay.blocks + lax.rem(i, lay.blocks)
            position = stored[fine[block]]
            at_row = lax.div(position, lay.slots_dev)
            at_place, at_core = lax.div(at_row, 2), lax.rem(at_row, 2)
            slot = (lax.bitwise_xor(at_place, place) * 2 + lax.bitwise_xor(at_core, core)) * lay.slots_dev
            slot = slot + lax.rem(position, lay.slots_dev)
            here = lax.div(at_place, lay.near) == half
            slot_of[p] = jnp.where(here, slot, -1)
            valid[owner * (lay.spread + 1) + found] = i
            fill[p] = 0
            return found + here.astype(jnp.int32)

        sizes[1 + owner] = lax.fori_loop(0, lay.spread, examine, 0)

    def input_of(owner, code):
        j = lax.rem(code, lay.spread)
        from_col = lax.bitwise_xor(lax.div(j, lay.blocks), col)
        return owner * lay.spread + from_col * lay.blocks + lax.rem(j, lay.blocks)

    for owner in range(lay.owners):

        def count(i, carry):
            p = input_of(owner, listed[owner, i])
            fill[p] = fill[p] + 1
            return carry

        lax.fori_loop(0, listed[owner, lay.tile_max], count, 0)

    group_input[0] = 0

    def place_groups(p, start):
        used = jnp.where(slot_of[p] >= 0, fill[p], 0)
        fill[p] = start * lay.unroll
        end = start + lax.div(used + (lay.unroll - 1), lay.unroll)

        def name(group, carry):
            group_input[group] = p
            return carry

        lax.fori_loop(start, end, name, 0)
        return end

    total = 1
    for owner in range(lay.owners):
        if owner > 0:
            sizes[lay.owners + owner] = total
        total = lax.fori_loop(owner * lay.spread, (owner + 1) * lay.spread, place_groups, total)
    sizes[0] = total

    def clear(i, carry):
        entries[i] = blank
        return carry

    lax.fori_loop(0, total * lay.unroll, clear, 0)

    for owner in range(lay.owners):

        def put(i, carry):
            code = listed[owner, i]
            p = input_of(owner, code)

            @pl.when(slot_of[p] >= 0)
            def _():
                out = lax.div(code, lay.spread)
                at_row = lax.div(out, lay.blocks)
                within = lax.rem(out, lay.blocks)
                far = lax.bitwise_xor(lax.div(at_row, 2), place)
                other = lax.bitwise_xor(lax.rem(at_row, 2), core)
                q = (other * lay.places + far) * lay.blocks + within
                a = fine[(at_row * lay.cols + col) * lay.blocks + within] - col * lay.points
                spot = fill[p]
                entries[spot] = q * lay.points + a
                fill[p] = spot + 1

            return carry

        lax.fori_loop(0, listed[owner, lay.tile_max], put, 0)


def make_plan(lay, ids, listed, fine, stored):
    smem = pl.BlockSpec(memory_space=pltpu.SMEM)
    lengths = (
        lay.inputs,
        lay.owners * (lay.spread + 1),
        2 * lay.owners,
        lay.groups,
        lay.groups * lay.unroll,
    )
    return pl.pallas_call(
        functools.partial(plan_kernel, lay),
        out_shape=tuple(jax.ShapeDtypeStruct((n,), jnp.int32) for n in lengths),
        in_specs=[smem] * 4,
        out_specs=(smem,) * 5,
        scratch_shapes=[pltpu.SMEM((lay.inputs,), jnp.int32)],
        cost_estimate=pl.CostEstimate(flops=0, bytes_accessed=20_000_000, transcendentals=0),
    )(ids, listed, fine, stored)


def add_products(lay, group, group_input, entries, tiles, rounded, total):
    held = tiles[pl.ds(group * lay.unroll, lay.unroll)].reshape(lay.unroll * lay.side, lay.side)
    products = jnp.dot(held, rounded[group_input[group]], preferred_element_type=jnp.float32)
    for i in range(lay.unroll):
        q = lax.div(entries[group * lay.unroll + i], lay.points)
        total[q] = total[q] + products[i * lay.side : (i + 1) * lay.side]


def turn_own_kernel(lay, given, turned):
    for t in range(lay.blocks):
        turned[t] = given[t, 0 : lay.pairs, :].T


def turn_own(lay, joined):
    vmem = pl.BlockSpec(memory_space=pltpu.VMEM)
    return pl.pallas_call(
        functools.partial(turn_own_kernel, lay),
        out_shape=jax.ShapeDtypeStruct((lay.blocks, lay.side, lay.pairs), jnp.bfloat16),
        in_specs=[vmem],
        out_specs=vmem,
        compiler_params=pltpu.CompilerParams(vmem_limit_bytes=16 * mib),
        cost_estimate=pl.CostEstimate(flops=1_000_000, bytes_accessed=5_000_000, transcendentals=0),
    )(joined)


def turn_both_kernel(lay, given, own, out):
    out[0 : lay.blocks] = own[...]
    for t in range(lay.blocks):
        out[lay.blocks + t] = given[t, 0 : lay.pairs, :].T


def turn_both(lay, partner, own):
    vmem = pl.BlockSpec(memory_space=pltpu.VMEM)
    return pl.pallas_call(
        functools.partial(turn_both_kernel, lay),
        out_shape=jax.ShapeDtypeStruct((2 * lay.blocks, lay.side, lay.pairs), jnp.bfloat16),
        in_specs=[vmem] * 2,
        out_specs=vmem,
        compiler_params=pltpu.CompilerParams(vmem_limit_bytes=16 * mib),
        cost_estimate=pl.CostEstimate(flops=1_000_000, bytes_accessed=5_000_000, transcendentals=0),
    )(partner, own)


def project_kernel(lay, slot_of, valid, sizes, *refs):
    refs = list(refs)
    given_in = [refs.pop(0) for _ in range(lay.owners * lay.cols)]
    given_coarse = [refs.pop(0) for _ in range(2 * lay.near)]
    out, right, blocks, projected, sems, out_sems = refs
    sets = []

    def fetch(source, target, index):
        sets[-1].append(pltpu.make_async_copy(source, target, sems.at[index]))
        sets[-1][-1].start()

    for owner in range(lay.owners):
        sets.append([])
        if owner == 0:
            for i in range(2 * lay.near):
                for a in range(lay.points):
                    target = blocks.at[a, pl.ds(i * lay.slots_dev, lay.slots_dev)]
                    fetch(given_coarse[i].at[a], target, i * lay.points + a)
        for i in range(owner * lay.cols, (owner + 1) * lay.cols):
            part = pl.ds(i * lay.blocks, lay.blocks)
            source = given_in[i].at[:, pl.ds(0, lay.pairs)]
            fetch(source, right.at[part], 2 * lay.near * lay.points + i)

    for owner in range(lay.owners):
        for copy in sets[owner]:
            copy.wait()
        found = sizes[1 + owner]

        def store(i):
            p = owner * lay.spread + i
            return pltpu.make_async_copy(projected.at[p], out.at[p], out_sems.at[p])

        def visit(step, carry):
            for lane in range(2):
                i = valid[owner * (lay.spread + 1) + jnp.minimum(2 * step + lane, found - 1)]
                p = owner * lay.spread + i
                for a in range(lay.points):
                    projected[p, :, a * lay.side : (a + 1) * lay.side] = jnp.dot(
                        blocks[a, slot_of[p]], right[p], preferred_element_type=jnp.float32
                    ).astype(jnp.bfloat16)
            return carry

        lax.fori_loop(0, lax.div(found + 1, 2), visit, 0)
        for i in range(lay.spread):

            @pl.when(slot_of[owner * lay.spread + i] >= 0)
            def _():
                store(i).start()

    for p in range(lay.inputs):

        @pl.when(slot_of[p] >= 0)
        def _():
            pltpu.make_async_copy(projected.at[p], out.at[p], out_sems.at[p]).wait()


def project(lay, plan, inputs, coarse):
    smem = pl.BlockSpec(memory_space=pltpu.SMEM)
    hbm = pl.BlockSpec(memory_space=pl.ANY)
    shape = (lay.inputs, lay.pairs, lay.points * lay.side)
    return pl.pallas_call(
        functools.partial(project_kernel, lay),
        out_shape=jax.ShapeDtypeStruct(shape, jnp.bfloat16),
        in_specs=[smem] * 3 + [hbm] * (len(inputs) + len(coarse)),
        out_specs=hbm,
        scratch_shapes=[
            pltpu.VMEM((lay.inputs, lay.pairs, lay.side), jnp.bfloat16),
            pltpu.VMEM((lay.points, lay.slots, lay.pairs, lay.pairs), jnp.bfloat16),
            pltpu.VMEM(shape, jnp.bfloat16),
            pltpu.SemaphoreType.DMA((len(inputs) + len(coarse) * lay.points,)),
            pltpu.SemaphoreType.DMA((lay.inputs,)),
        ],
        compiler_params=pltpu.CompilerParams(vmem_limit_bytes=lay.vmem),
        cost_estimate=pl.CostEstimate(flops=2_000_000_000, bytes_accessed=25_000_000, transcendentals=0),
    )(*plan[:3], *inputs, *coarse)


def tiles_kernel(lay, slot_of, sizes, group_input, entries, *refs):
    lines = lay.line_steps()
    refs = list(refs)
    given_in = [refs.pop(0) for _ in range(lay.owners * lay.cols)]
    given_out = [refs.pop(0) for _ in range(2 * (1 + len(lines)))]
    given_projected = refs.pop(0)
    own_sum, other_sum, tiles_out = refs[:3]
    left, projected, rounded, tiles, total, sems, sum_sems, in_sems, out_sems = refs[3:]
    copies = []

    def fetch(source, target):
        copies.append(pltpu.make_async_copy(source, target, sems.at[len(copies)]))
        copies[-1].start()

    def load(p):
        return pltpu.make_async_copy(given_projected.at[p], projected.at[p], in_sems.at[p])

    for k in range(2):
        held = given_out[k * (1 + len(lines)) :]
        for g in range(lay.owners):
            spot = (k * lay.places + g * lay.near) * lay.blocks
            fetch(held[0].at[pl.ds(g * lay.blocks, lay.blocks)], left.at[pl.ds(spot, lay.blocks)])
        for i, d in enumerate(lines):
            spot = (k * lay.places + d) * lay.blocks
            fetch(held[1 + i], left.at[pl.ds(spot, lay.blocks)])
    for i, ref in enumerate(given_in):
        part = pl.ds(i * lay.blocks, lay.blocks)
        fetch(ref.at[:, pl.ds(lay.pairs, lay.side)], rounded.at[part])
    for p in range(lay.inputs):

        @pl.when(slot_of[p] >= 0)
        def _():
            load(p).start()

    total[...] = jnp.zeros_like(total)
    for copy in copies:
        copy.wait()
    used = sizes[0]

    for owner in range(lay.owners):
        for p in range(owner * lay.spread, (owner + 1) * lay.spread):

            @pl.when(slot_of[p] >= 0)
            def _():
                load(p).wait()

        def group_step(group, carry):
            block = projected[group_input[group]]
            numbers = [entries[group * lay.unroll + i] for i in range(lay.unroll)]
            places = [jnp.minimum(lax.div(n, lay.points), lay.outputs - 1) for n in numbers]
            lefts = jnp.concatenate([left[q] for q in places], axis=0)
            both = jnp.dot(lefts, block, preferred_element_type=jnp.float32)
            for i in range(lay.unroll):
                mine = both[i * lay.side : (i + 1) * lay.side]
                tile = mine[:, : lay.side]
                for b in range(1, lay.points):
                    at_b = mine[:, b * lay.side : (b + 1) * lay.side]
                    tile = jnp.where(lax.rem(numbers[i], lay.points) == b, at_b, tile)
                tiles[group * lay.unroll + i] = tile.astype(jnp.bfloat16)
            add_products(lay, group - 1, group_input, entries, tiles, rounded, total)
            return carry

        first = 1 if owner == 0 else sizes[lay.owners + owner]
        last = used if owner == lay.owners - 1 else sizes[lay.owners + owner + 1]
        lax.fori_loop(first, last, group_step, 0)

    span = chunk_groups * lay.unroll

    def store(chunk):
        part = pl.ds(chunk * span, span)
        return pltpu.make_async_copy(tiles.at[part], tiles_out.at[part], out_sems.at[chunk])

    for chunk in range(lay.groups // chunk_groups):

        @pl.when(used > chunk * chunk_groups)
        def _():
            store(chunk).start()

    add_products(lay, used - 1, group_input, entries, tiles, rounded, total)
    give_sums(lay, total, own_sum, other_sum, sum_sems)
    for chunk in range(lay.groups // chunk_groups):

        @pl.when(used > chunk * chunk_groups)
        def _():
            store(chunk).wait()


def give_sums(lay, total, own_sum, other_sum, sems):
    own = lay.places * lay.blocks
    for copy in (
        pltpu.make_async_copy(total.at[pl.ds(own, own)], other_sum, sems.at[1]),
        pltpu.make_async_copy(total.at[pl.ds(0, own)], own_sum, sems.at[0]),
    ):
        copy.start()
    pltpu.make_async_copy(total.at[pl.ds(own, own)], other_sum, sems.at[1]).wait()
    pltpu.make_async_copy(total.at[pl.ds(0, own)], own_sum, sems.at[0]).wait()


def make_tiles(lay, plan, inputs, outputs, projected):
    smem = pl.BlockSpec(memory_space=pltpu.SMEM)
    hbm = pl.BlockSpec(memory_space=pl.ANY)
    own = lay.places * lay.blocks
    sums = jax.ShapeDtypeStruct((own, lay.side, lay.width), jnp.float32)
    tiles = (lay.groups * lay.unroll, lay.side, lay.side)
    return pl.pallas_call(
        functools.partial(tiles_kernel, lay),
        out_shape=(sums, sums, jax.ShapeDtypeStruct(tiles, jnp.bfloat16)),
        in_specs=[smem] * 4 + [hbm] * (len(inputs) + len(outputs) + 1),
        out_specs=(hbm,) * 3,
        scratch_shapes=[
            pltpu.VMEM((lay.outputs, lay.side, lay.pairs), jnp.bfloat16),
            pltpu.VMEM(projected.shape, jnp.bfloat16),
            pltpu.VMEM((lay.inputs, lay.side, lay.width), jnp.bfloat16),
            pltpu.VMEM(tiles, jnp.bfloat16),
            pltpu.VMEM((lay.outputs + 1, lay.side, lay.width), jnp.float32),
            pltpu.SemaphoreType.DMA((len(inputs) + 2 * lay.places,)),
            pltpu.SemaphoreType.DMA((2,)),
            pltpu.SemaphoreType.DMA((lay.inputs,)),
            pltpu.SemaphoreType.DMA((lay.groups // chunk_groups,)),
        ],
        compiler_params=pltpu.CompilerParams(vmem_limit_bytes=lay.vmem),
        cost_estimate=pl.CostEstimate(flops=4_000_000_000, bytes_accessed=30_000_000, transcendentals=0),
    )(plan[0], *plan[2:], *inputs, *outputs, projected)


def apply_kernel(lay, sizes, group_input, entries, tiles_in, *refs):
    given_vec = refs[: lay.cols]
    own_sum, other_sum = refs[lay.cols : lay.cols + 2]
    rounded, tiles, total, sems, sum_sems, out_sems = refs[lay.cols + 2 :]
    used = sizes[0]
    span = chunk_groups * lay.unroll

    def load(chunk):
        part = pl.ds(chunk * span, span)
        return pltpu.make_async_copy(tiles_in.at[part], tiles.at[part], out_sems.at[chunk])

    for chunk in range(lay.groups // chunk_groups):

        @pl.when(used > chunk * chunk_groups)
        def _():
            load(chunk).start()

    copies = []
    for d in range(lay.cols):
        for g in range(lay.owners):
            target = rounded.at[pl.ds((g * lay.cols + d) * lay.blocks, lay.blocks)]
            copies.append(pltpu.make_async_copy(given_vec[d].at[g], target, sems.at[len(copies)]))
            copies[-1].start()
    total[...] = jnp.zeros_like(total)
    for copy in copies:
        copy.wait()
    for chunk in range(lay.groups // chunk_groups):

        @pl.when(used > chunk * chunk_groups)
        def _():
            load(chunk).wait()

    def group_step(group, carry):
        add_products(lay, group, group_input, entries, tiles, rounded, total)
        return carry

    lax.fori_loop(1, used, group_step, 0)
    give_sums(lay, total, own_sum, other_sum, sum_sems)


def apply_tiles(lay, plan, tiles, rounded):
    smem = pl.BlockSpec(memory_space=pltpu.SMEM)
    hbm = pl.BlockSpec(memory_space=pl.ANY)
    own = lay.places * lay.blocks
    sums = jax.ShapeDtypeStruct((own, lay.side, lay.width), jnp.float32)
    return pl.pallas_call(
        functools.partial(apply_kernel, lay),
        out_shape=(sums, sums),
        in_specs=[smem] * 3 + [hbm] * (1 + len(rounded)),
        out_specs=(hbm, hbm),
        scratch_shapes=[
            pltpu.VMEM((lay.inputs, lay.side, lay.width), jnp.bfloat16),
            pltpu.VMEM(tiles.shape, jnp.bfloat16),
            pltpu.VMEM((lay.outputs + 1, lay.side, lay.width), jnp.float32),
            pltpu.SemaphoreType.DMA((len(rounded) * lay.owners,)),
            pltpu.SemaphoreType.DMA((2,)),
            pltpu.SemaphoreType.DMA((lay.groups // chunk_groups,)),
        ],
        compiler_params=pltpu.CompilerParams(vmem_limit_bytes=lay.vmem),
        cost_estimate=pl.CostEstimate(flops=400_000_000, bytes_accessed=4_000_000, transcendentals=0),
    )(*plan[2:], tiles, *rounded)


def on_device(
    vectors, energies, intersections, coarse, fine_coarse, coarse_slot, tile_codes, tile_count
):
    rows = lax.axis_size("row")
    cols = lax.axis_size("col")
    row_id = lax.axis_index("row")
    col_id = lax.axis_index("col")
    blocks, pairs, side = intersections.shape
    width = vectors.shape[1]
    points, slots_dev = coarse.shape[:2]
    lay = Layout(rows, cols, blocks, pairs, side, width, points, slots_dev, tile_codes.shape[1], 4)
    if lay.groups * lay.unroll * side * side * 2 > 16 * mib:
        lay = Layout(rows, cols, blocks, pairs, side, width, points, slots_dev, tile_codes.shape[1], 1)
    near = lay.near

    def move(array, row_step, col_step):
        pairs_list = [
            (r * cols + c, (r ^ row_step) * cols + (c ^ col_step)) for r in range(rows) for c in range(cols)
        ]
        return lax.ppermute(array, axes, pairs_list)

    def along(array, step):
        return move(array, 2 * step, 0)

    def to_core(array):
        return move(array, 1, 0)

    def in_plane(array):
        return [array] + [move(array, 0, d) for d in range(1, cols)]

    start = vectors.reshape(blocks, side, width)
    energy = energies.reshape(blocks, side, 1)
    two_owners = lay.owners == 2
    ids = jnp.stack([row_id // 2, row_id % 2, col_id]).astype(jnp.int32)
    listed = jnp.concatenate([tile_codes, tile_count[:, None]], axis=1)
    n_listed = listed.shape[1]
    digits = jnp.concatenate([listed[0] >> 8, listed[0] & 255]).astype(jnp.bfloat16)
    depth = 16 * -(-2 * n_listed // (16 * width * blocks))
    digits = jnp.pad(digits, (0, blocks * depth * width - 2 * n_listed)).reshape(blocks, depth, width)
    joined = jnp.concatenate([intersections, start.astype(jnp.bfloat16), digits], axis=1)

    near_coarse = [along(coarse, e) for e in range(1, near)]
    partner = [along(joined, near)] if two_owners else []
    inputs = in_plane(joined)
    inputs, partner, late_joined = lax.optimization_barrier((inputs, partner, joined))
    if two_owners:
        sent = partner[0][:, pairs + side :].reshape(-1)[: 2 * n_listed].astype(jnp.int32)
        listed = jnp.concatenate([listed, ((sent[:n_listed] << 8) + sent[n_listed:])[None]], axis=0)
    plan = make_plan(lay, ids, listed, fine_coarse, coarse_slot)
    for part in partner:
        inputs = inputs + in_plane(part)
    turned = turn_own(lay, late_joined)
    turned, near_coarse, plan = lax.optimization_barrier((turned, near_coarse, plan))
    lines = [along(turned, d) for d in lay.line_steps()]
    for part in partner:
        turned = turn_both(lay, part, turned)
    far = lines[near - 1 :]
    held = (inputs, near_coarse, far, coarse)
    inputs, near_coarse, far, late_coarse = lax.optimization_barrier(held)
    blocks_coarse = []
    for part in [late_coarse] + near_coarse:
        blocks_coarse += [part, to_core(part)]
    projected = project(lay, plan, inputs, blocks_coarse)
    late, projected = lax.optimization_barrier((lines[: near - 1], projected))
    lefts = [turned] + late + far
    lefts = lefts + [to_core(part) for part in lefts]
    own_sum, other_sum, tiles = make_tiles(lay, plan, inputs, lefts, projected)

    def over_core(own_part, other_part):
        return (own_part + to_core(other_part)).reshape(lay.places, blocks, side, width)

    def shifted_part(field):
        return energy * field - spectrum_center * field

    merged = over_core(own_sum, other_sum)
    if two_owners:
        sums = jnp.stack([merged[0] + shifted_part(start), merged[near]])
        for e in range(1, near):
            sent = jnp.stack([merged[e], merged[e ^ near]]).astype(jnp.bfloat16)
            sums = sums + along(sent, e).astype(jnp.float32)
        sums = sums + along(sums.astype(jnp.bfloat16), near)[::-1].astype(jnp.float32)
    else:
        sums = merged + shifted_part(start)[None]

    firsts = sums / spectrum_half
    first = firsts[0]
    own_sum, other_sum = apply_tiles(lay, plan, tiles, in_plane(firsts.astype(jnp.bfloat16)))
    merged = over_core(own_sum, other_sum)
    last = merged[0]
    for d in range(1, lay.places):
        last = last + along(merged[d].astype(jnp.bfloat16), d).astype(jnp.float32)
    second = 2.0 * ((shifted_part(first) + last) / spectrum_half) - start
    return first.reshape(vectors.shape), second.reshape(vectors.shape)


def solution(mesh):
    in_specs = (
        P(axes, None),
        P(axes),
        P(axes, None, None),
        P("col", "row", None, None),
        P(),
        P(),
        P(axes, None),
        P(axes),
    )
    out_specs = (P(axes, None), P(axes, None))
    return jax.shard_map(
        on_device, mesh=mesh, in_specs=in_specs, out_specs=out_specs, check_vma=False
    )
```

```python
import functools

import jax
import jax.numpy as jnp
from jax import lax
from jax.experimental import pallas as pl
from jax.experimental.pallas import tpu as pltpu
from jax.sharding import PartitionSpec as P

spectrum_center = 2.0
spectrum_half = 3.0
axes = ("row", "col")
chunk_groups = 8
mib = 1 << 20


class Layout:
    def __init__(self, rows, cols, blocks, pairs, side, width, points, slots_dev, tile_max, unroll):
        self.rows, self.cols, self.blocks = rows, cols, blocks
        self.pairs, self.side, self.width = pairs, side, width
        self.points, self.slots_dev, self.tile_max = points, slots_dev, tile_max
        self.places = rows // 2
        self.near = max(self.places // 2, 1)
        self.owners = 2 if self.places > 1 else 1
        self.spread = cols * blocks
        self.inputs = self.owners * self.spread
        self.outputs = rows * blocks
        self.slots = 2 * self.near * slots_dev
        self.unroll = unroll
        self.vmem = 60 * mib
        most = self.owners * tile_max + self.inputs * (unroll - 1) + unroll
        self.groups = -(-most // (unroll * chunk_groups)) * chunk_groups

    def line_steps(self):
        return [d for d in range(1, self.places) if d != self.near]


def plan_kernel(lay, ids, listed, fine, stored, slot_of, valid, sizes, group_input, entries, fill):
    place, core, col = ids[0], ids[1], ids[2]
    half = lax.div(place, lay.near)
    blank = lay.outputs * lay.points

    for owner in range(lay.owners):

        def examine(i, found):
            p = owner * lay.spread + i
            from_col = lax.bitwise_xor(lax.div(i, lay.blocks), col)
            from_place = lax.bitwise_xor(place, owner * lay.near)
            block = ((from_place * 2 + core) * lay.cols + from_col) * lay.blocks + lax.rem(i, lay.blocks)
            position = stored[fine[block]]
            at_row = lax.div(position, lay.slots_dev)
            at_place, at_core = lax.div(at_row, 2), lax.rem(at_row, 2)
            slot = (lax.bitwise_xor(at_place, place) * 2 + lax.bitwise_xor(at_core, core)) * lay.slots_dev
            slot = slot + lax.rem(position, lay.slots_dev)
            here = lax.div(at_place, lay.near) == half
            slot_of[p] = jnp.where(here, slot, -1)
            valid[owner * (lay.spread + 1) + found] = i
            fill[p] = 0
            return found + here.astype(jnp.int32)

        sizes[1 + owner] = lax.fori_loop(0, lay.spread, examine, 0)

    def input_of(owner, code):
        j = lax.rem(code, lay.spread)
        from_col = lax.bitwise_xor(lax.div(j, lay.blocks), col)
        return owner * lay.spread + from_col * lay.blocks + lax.rem(j, lay.blocks)

    for owner in range(lay.owners):

        def count(i, carry):
            p = input_of(owner, listed[owner, i])
            fill[p] = fill[p] + 1
            return carry

        lax.fori_loop(0, listed[owner, lay.tile_max], count, 0)

    group_input[0] = 0

    def place_groups(p, start):
        used = jnp.where(slot_of[p] >= 0, fill[p], 0)
        fill[p] = start * lay.unroll
        end = start + lax.div(used + (lay.unroll - 1), lay.unroll)

        def name(group, carry):
            group_input[group] = p
            return carry

        lax.fori_loop(start, end, name, 0)
        return end

    total = 1
    for owner in range(lay.owners):
        if owner > 0:
            sizes[lay.owners + owner] = total
        total = lax.fori_loop(owner * lay.spread, (owner + 1) * lay.spread, place_groups, total)
    sizes[0] = total

    def clear(i, carry):
        entries[i] = blank
        return carry

    lax.fori_loop(0, total * lay.unroll, clear, 0)

    for owner in range(lay.owners):

        def put(i, carry):
            code = listed[owner, i]
            p = input_of(owner, code)

            @pl.when(slot_of[p] >= 0)
            def _():
                out = lax.div(code, lay.spread)
                at_row = lax.div(out, lay.blocks)
                within = lax.rem(out, lay.blocks)
                far = lax.bitwise_xor(lax.div(at_row, 2), place)
                other = lax.bitwise_xor(lax.rem(at_row, 2), core)
                q = (other * lay.places + far) * lay.blocks + within
                a = fine[(at_row * lay.cols + col) * lay.blocks + within] - col * lay.points
                spot = fill[p]
                entries[spot] = q * lay.points + a
                fill[p] = spot + 1

            return carry

        lax.fori_loop(0, listed[owner, lay.tile_max], put, 0)


def make_plan(lay, ids, listed, fine, stored):
    smem = pl.BlockSpec(memory_space=pltpu.SMEM)
    lengths = (
        lay.inputs,
        lay.owners * (lay.spread + 1),
        2 * lay.owners,
        lay.groups,
        lay.groups * lay.unroll,
    )
    return pl.pallas_call(
        functools.partial(plan_kernel, lay),
        out_shape=tuple(jax.ShapeDtypeStruct((n,), jnp.int32) for n in lengths),
        in_specs=[smem] * 4,
        out_specs=(smem,) * 5,
        scratch_shapes=[pltpu.SMEM((lay.inputs,), jnp.int32)],
        cost_estimate=pl.CostEstimate(flops=0, bytes_accessed=20_000_000, transcendentals=0),
    )(ids, listed, fine, stored)


def add_products(lay, group, group_input, entries, tiles, rounded, total):
    held = tiles[pl.ds(group * lay.unroll, lay.unroll)].reshape(lay.unroll * lay.side, lay.side)
    products = jnp.dot(held, rounded[group_input[group]], preferred_element_type=jnp.float32)
    for i in range(lay.unroll):
        q = lax.div(entries[group * lay.unroll + i], lay.points)
        total[q] = total[q] + products[i * lay.side : (i + 1) * lay.side]


def turn_own_kernel(lay, given, turned):
    for t in range(lay.blocks):
        turned[t] = given[t, 0 : lay.pairs, :].T


def turn_own(lay, joined):
    vmem = pl.BlockSpec(memory_space=pltpu.VMEM)
    return pl.pallas_call(
        functools.partial(turn_own_kernel, lay),
        out_shape=jax.ShapeDtypeStruct((lay.blocks, lay.side, lay.pairs), jnp.bfloat16),
        in_specs=[vmem],
        out_specs=vmem,
        compiler_params=pltpu.CompilerParams(vmem_limit_bytes=16 * mib),
        cost_estimate=pl.CostEstimate(flops=1_000_000, bytes_accessed=5_000_000, transcendentals=0),
    )(joined)


def turn_both_kernel(lay, given, own, out):
    out[0 : lay.blocks] = own[...]
    for t in range(lay.blocks):
        out[lay.blocks + t] = given[t, 0 : lay.pairs, :].T


def turn_both(lay, partner, own):
    vmem = pl.BlockSpec(memory_space=pltpu.VMEM)
    return pl.pallas_call(
        functools.partial(turn_both_kernel, lay),
        out_shape=jax.ShapeDtypeStruct((2 * lay.blocks, lay.side, lay.pairs), jnp.bfloat16),
        in_specs=[vmem] * 2,
        out_specs=vmem,
        compiler_params=pltpu.CompilerParams(vmem_limit_bytes=16 * mib),
        cost_estimate=pl.CostEstimate(flops=1_000_000, bytes_accessed=5_000_000, transcendentals=0),
    )(partner, own)


def project_kernel(lay, owner, slot_of, valid, sizes, *refs):
    refs = list(refs)
    given_in = [refs.pop(0) for _ in range(lay.cols)]
    given_coarse = [refs.pop(0) for _ in range(2 * lay.near)]
    out, right, blocks, projected, sems, out_sems = refs
    copies = []

    def fetch(source, target):
        copies.append(pltpu.make_async_copy(source, target, sems.at[len(copies)]))
        copies[-1].start()

    for i in range(2 * lay.near):
        for a in range(lay.points):
            fetch(given_coarse[i].at[a], blocks.at[a, pl.ds(i * lay.slots_dev, lay.slots_dev)])
    for i in range(lay.cols):
        fetch(given_in[i].at[:, pl.ds(0, lay.pairs)], right.at[pl.ds(i * lay.blocks, lay.blocks)])
    for copy in copies:
        copy.wait()
    found = sizes[1 + owner]

    def visit(step, carry):
        for lane in range(2):
            i = valid[owner * (lay.spread + 1) + jnp.minimum(2 * step + lane, found - 1)]
            slot = slot_of[owner * lay.spread + i]
            for a in range(lay.points):
                projected[i, :, a * lay.side : (a + 1) * lay.side] = jnp.dot(
                    blocks[a, slot], right[i], preferred_element_type=jnp.float32
                ).astype(jnp.bfloat16)
        return carry

    lax.fori_loop(0, lax.div(found + 1, 2), visit, 0)

    def store(i):
        return pltpu.make_async_copy(projected.at[i], out.at[i], out_sems.at[i])

    for i in range(lay.spread):

        @pl.when(slot_of[owner * lay.spread + i] >= 0)
        def _():
            store(i).start()

    for i in range(lay.spread):

        @pl.when(slot_of[owner * lay.spread + i] >= 0)
        def _():
            store(i).wait()


def project(lay, owner, plan, inputs, coarse):
    smem = pl.BlockSpec(memory_space=pltpu.SMEM)
    hbm = pl.BlockSpec(memory_space=pl.ANY)
    shape = (lay.spread, lay.pairs, lay.points * lay.side)
    return pl.pallas_call(
        functools.partial(project_kernel, lay, owner),
        out_shape=jax.ShapeDtypeStruct(shape, jnp.bfloat16),
        in_specs=[smem] * 3 + [hbm] * (len(inputs) + len(coarse)),
        out_specs=hbm,
        scratch_shapes=[
            pltpu.VMEM((lay.spread, lay.pairs, lay.side), jnp.bfloat16),
            pltpu.VMEM((lay.points, lay.slots, lay.pairs, lay.pairs), jnp.bfloat16),
            pltpu.VMEM(shape, jnp.bfloat16),
            pltpu.SemaphoreType.DMA((len(inputs) + len(coarse) * lay.points,)),
            pltpu.SemaphoreType.DMA((lay.spread,)),
        ],
        compiler_params=pltpu.CompilerParams(vmem_limit_bytes=lay.vmem),
        cost_estimate=pl.CostEstimate(flops=1_000_000_000, bytes_accessed=16_000_000, transcendentals=0),
    )(*plan[:3], *inputs, *coarse)


def tiles_kernel(lay, slot_of, sizes, group_input, entries, *refs):
    lines = lay.line_steps()
    refs = list(refs)
    given_in = [refs.pop(0) for _ in range(lay.owners * lay.cols)]
    given_out = [refs.pop(0) for _ in range(2 * (1 + len(lines)))]
    given_projected = [refs.pop(0) for _ in range(lay.owners)]
    own_sum, other_sum, tiles_out = refs[:3]
    left, projected, rounded, tiles, total, sems, sum_sems, in_sems, out_sems = refs[3:]
    copies = []

    def fetch(source, target):
        copies.append(pltpu.make_async_copy(source, target, sems.at[len(copies)]))
        copies[-1].start()

    def load(p):
        source = given_projected[p // lay.spread].at[p % lay.spread]
        return pltpu.make_async_copy(source, projected.at[p], in_sems.at[p])

    for k in range(2):
        held = given_out[k * (1 + len(lines)) :]
        for g in range(lay.owners):
            spot = (k * lay.places + g * lay.near) * lay.blocks
            fetch(held[0].at[pl.ds(g * lay.blocks, lay.blocks)], left.at[pl.ds(spot, lay.blocks)])
        for i, d in enumerate(lines):
            spot = (k * lay.places + d) * lay.blocks
            fetch(held[1 + i], left.at[pl.ds(spot, lay.blocks)])
    for i, ref in enumerate(given_in):
        part = pl.ds(i * lay.blocks, lay.blocks)
        fetch(ref.at[:, pl.ds(lay.pairs, lay.side)], rounded.at[part])
    for p in range(lay.inputs):

        @pl.when(slot_of[p] >= 0)
        def _():
            load(p).start()

    total[...] = jnp.zeros_like(total)
    for copy in copies:
        copy.wait()
    used = sizes[0]

    for owner in range(lay.owners):
        for p in range(owner * lay.spread, (owner + 1) * lay.spread):

            @pl.when(slot_of[p] >= 0)
            def _():
                load(p).wait()

        def group_step(group, carry):
            block = projected[group_input[group]]
            numbers = [entries[group * lay.unroll + i] for i in range(lay.unroll)]
            places = [jnp.minimum(lax.div(n, lay.points), lay.outputs - 1) for n in numbers]
            lefts = jnp.concatenate([left[q] for q in places], axis=0)
            both = jnp.dot(lefts, block, preferred_element_type=jnp.float32)
            for i in range(lay.unroll):
                mine = both[i * lay.side : (i + 1) * lay.side]
                tile = mine[:, : lay.side]
                for b in range(1, lay.points):
                    at_b = mine[:, b * lay.side : (b + 1) * lay.side]
                    tile = jnp.where(lax.rem(numbers[i], lay.points) == b, at_b, tile)
                tiles[group * lay.unroll + i] = tile.astype(jnp.bfloat16)
            add_products(lay, group - 1, group_input, entries, tiles, rounded, total)
            return carry

        first = 1 if owner == 0 else sizes[lay.owners + owner]
        last = used if owner == lay.owners - 1 else sizes[lay.owners + owner + 1]
        lax.fori_loop(first, last, group_step, 0)

    span = chunk_groups * lay.unroll

    def store(chunk):
        part = pl.ds(chunk * span, span)
        return pltpu.make_async_copy(tiles.at[part], tiles_out.at[part], out_sems.at[chunk])

    for chunk in range(lay.groups // chunk_groups):

        @pl.when(used > chunk * chunk_groups)
        def _():
            store(chunk).start()

    add_products(lay, used - 1, group_input, entries, tiles, rounded, total)
    give_sums(lay, total, own_sum, other_sum, sum_sems)
    for chunk in range(lay.groups // chunk_groups):

        @pl.when(used > chunk * chunk_groups)
        def _():
            store(chunk).wait()


def give_sums(lay, total, own_sum, other_sum, sems):
    own = lay.places * lay.blocks
    for copy in (
        pltpu.make_async_copy(total.at[pl.ds(own, own)], other_sum, sems.at[1]),
        pltpu.make_async_copy(total.at[pl.ds(0, own)], own_sum, sems.at[0]),
    ):
        copy.start()
    pltpu.make_async_copy(total.at[pl.ds(own, own)], other_sum, sems.at[1]).wait()
    pltpu.make_async_copy(total.at[pl.ds(0, own)], own_sum, sems.at[0]).wait()


def make_tiles(lay, plan, inputs, outputs, projected):
    smem = pl.BlockSpec(memory_space=pltpu.SMEM)
    hbm = pl.BlockSpec(memory_space=pl.ANY)
    own = lay.places * lay.blocks
    sums = jax.ShapeDtypeStruct((own, lay.side, lay.width), jnp.float32)
    tiles = (lay.groups * lay.unroll, lay.side, lay.side)
    return pl.pallas_call(
        functools.partial(tiles_kernel, lay),
        out_shape=(sums, sums, jax.ShapeDtypeStruct(tiles, jnp.bfloat16)),
        in_specs=[smem] * 4 + [hbm] * (len(inputs) + len(outputs) + len(projected)),
        out_specs=(hbm,) * 3,
        scratch_shapes=[
            pltpu.VMEM((lay.outputs, lay.side, lay.pairs), jnp.bfloat16),
            pltpu.VMEM((lay.inputs, lay.pairs, lay.points * lay.side), jnp.bfloat16),
            pltpu.VMEM((lay.inputs, lay.side, lay.width), jnp.bfloat16),
            pltpu.VMEM(tiles, jnp.bfloat16),
            pltpu.VMEM((lay.outputs + 1, lay.side, lay.width), jnp.float32),
            pltpu.SemaphoreType.DMA((len(inputs) + 2 * lay.places,)),
            pltpu.SemaphoreType.DMA((2,)),
            pltpu.SemaphoreType.DMA((lay.inputs,)),
            pltpu.SemaphoreType.DMA((lay.groups // chunk_groups,)),
        ],
        compiler_params=pltpu.CompilerParams(vmem_limit_bytes=lay.vmem),
        cost_estimate=pl.CostEstimate(flops=4_000_000_000, bytes_accessed=30_000_000, transcendentals=0),
    )(plan[0], *plan[2:], *inputs, *outputs, *projected)


def apply_kernel(lay, sizes, group_input, entries, tiles_in, *refs):
    given_vec = refs[: lay.cols]
    own_sum, other_sum = refs[lay.cols : lay.cols + 2]
    rounded, tiles, total, sems, sum_sems, out_sems = refs[lay.cols + 2 :]
    used = sizes[0]
    span = chunk_groups * lay.unroll

    def load(chunk):
        part = pl.ds(chunk * span, span)
        return pltpu.make_async_copy(tiles_in.at[part], tiles.at[part], out_sems.at[chunk])

    for chunk in range(lay.groups // chunk_groups):

        @pl.when(used > chunk * chunk_groups)
        def _():
            load(chunk).start()

    copies = []
    for d in range(lay.cols):
        for g in range(lay.owners):
            target = rounded.at[pl.ds((g * lay.cols + d) * lay.blocks, lay.blocks)]
            copies.append(pltpu.make_async_copy(given_vec[d].at[g], target, sems.at[len(copies)]))
            copies[-1].start()
    total[...] = jnp.zeros_like(total)
    for copy in copies:
        copy.wait()
    for chunk in range(lay.groups // chunk_groups):

        @pl.when(used > chunk * chunk_groups)
        def _():
            load(chunk).wait()

    def group_step(group, carry):
        add_products(lay, group, group_input, entries, tiles, rounded, total)
        return carry

    lax.fori_loop(1, used, group_step, 0)
    give_sums(lay, total, own_sum, other_sum, sum_sems)


def apply_tiles(lay, plan, tiles, rounded):
    smem = pl.BlockSpec(memory_space=pltpu.SMEM)
    hbm = pl.BlockSpec(memory_space=pl.ANY)
    own = lay.places * lay.blocks
    sums = jax.ShapeDtypeStruct((own, lay.side, lay.width), jnp.float32)
    return pl.pallas_call(
        functools.partial(apply_kernel, lay),
        out_shape=(sums, sums),
        in_specs=[smem] * 3 + [hbm] * (1 + len(rounded)),
        out_specs=(hbm, hbm),
        scratch_shapes=[
            pltpu.VMEM((lay.inputs, lay.side, lay.width), jnp.bfloat16),
            pltpu.VMEM(tiles.shape, jnp.bfloat16),
            pltpu.VMEM((lay.outputs + 1, lay.side, lay.width), jnp.float32),
            pltpu.SemaphoreType.DMA((len(rounded) * lay.owners,)),
            pltpu.SemaphoreType.DMA((2,)),
            pltpu.SemaphoreType.DMA((lay.groups // chunk_groups,)),
        ],
        compiler_params=pltpu.CompilerParams(vmem_limit_bytes=lay.vmem),
        cost_estimate=pl.CostEstimate(flops=400_000_000, bytes_accessed=4_000_000, transcendentals=0),
    )(*plan[2:], tiles, *rounded)


def on_device(
    vectors, energies, intersections, coarse, fine_coarse, coarse_slot, tile_codes, tile_count
):
    rows = lax.axis_size("row")
    cols = lax.axis_size("col")
    row_id = lax.axis_index("row")
    col_id = lax.axis_index("col")
    blocks, pairs, side = intersections.shape
    width = vectors.shape[1]
    points, slots_dev = coarse.shape[:2]
    lay = Layout(rows, cols, blocks, pairs, side, width, points, slots_dev, tile_codes.shape[1], 4)
    if lay.groups * lay.unroll * side * side * 2 > 16 * mib:
        lay = Layout(rows, cols, blocks, pairs, side, width, points, slots_dev, tile_codes.shape[1], 1)
    near = lay.near

    def move(array, row_step, col_step):
        pairs_list = [
            (r * cols + c, (r ^ row_step) * cols + (c ^ col_step)) for r in range(rows) for c in range(cols)
        ]
        return lax.ppermute(array, axes, pairs_list)

    def along(array, step):
        return move(array, 2 * step, 0)

    def to_core(array):
        return move(array, 1, 0)

    def in_plane(array):
        return [array] + [move(array, 0, d) for d in range(1, cols)]

    start = vectors.reshape(blocks, side, width)
    energy = energies.reshape(blocks, side, 1)
    two_owners = lay.owners == 2
    ids = jnp.stack([row_id // 2, row_id % 2, col_id]).astype(jnp.int32)
    listed = jnp.concatenate([tile_codes, tile_count[:, None]], axis=1)
    n_listed = listed.shape[1]
    digits = jnp.concatenate([listed[0] >> 8, listed[0] & 255]).astype(jnp.bfloat16)
    depth = 16 * -(-2 * n_listed // (16 * width * blocks))
    digits = jnp.pad(digits, (0, blocks * depth * width - 2 * n_listed)).reshape(blocks, depth, width)
    joined = jnp.concatenate([intersections, start.astype(jnp.bfloat16), digits], axis=1)

    near_coarse = [along(coarse, e) for e in range(1, near)]
    partner = [along(joined, near)] if two_owners else []
    inputs = in_plane(joined)
    inputs, partner, late_joined = lax.optimization_barrier((inputs, partner, joined))
    if two_owners:
        sent = partner[0][:, pairs + side :].reshape(-1)[: 2 * n_listed].astype(jnp.int32)
        listed = jnp.concatenate([listed, ((sent[:n_listed] << 8) + sent[n_listed:])[None]], axis=0)
    plan = make_plan(lay, ids, listed, fine_coarse, coarse_slot)
    for part in partner:
        inputs = inputs + in_plane(part)
    turned = turn_own(lay, late_joined)
    turned, near_coarse, plan = lax.optimization_barrier((turned, near_coarse, plan))
    blocks_coarse = []
    for part in [coarse] + near_coarse:
        blocks_coarse += [part, to_core(part)]
    turned, blocks_coarse = lax.optimization_barrier((turned, blocks_coarse))
    lines = [along(turned, d) for d in lay.line_steps()]
    for part in partner:
        turned = turn_both(lay, part, turned)
    projected = [
        project(lay, g, plan, inputs[g * cols : (g + 1) * cols], blocks_coarse) for g in range(lay.owners)
    ]
    lines, turned, projected = lax.optimization_barrier((lines, turned, projected))
    lefts = [turned] + lines
    lefts = lefts + [to_core(part) for part in lefts]
    own_sum, other_sum, tiles = make_tiles(lay, plan, inputs, lefts, projected)

    def over_core(own_part, other_part):
        return (own_part + to_core(other_part)).reshape(lay.places, blocks, side, width)

    def shifted_part(field):
        return energy * field - spectrum_center * field

    merged = over_core(own_sum, other_sum)
    if two_owners:
        sums = jnp.stack([merged[0] + shifted_part(start), merged[near]])
        for e in range(1, near):
            sent = jnp.stack([merged[e], merged[e ^ near]]).astype(jnp.bfloat16)
            sums = sums + along(sent, e).astype(jnp.float32)
        sums = sums + along(sums.astype(jnp.bfloat16), near)[::-1].astype(jnp.float32)
    else:
        sums = merged + shifted_part(start)[None]

    firsts = sums / spectrum_half
    first = firsts[0]
    own_sum, other_sum = apply_tiles(lay, plan, tiles, in_plane(firsts.astype(jnp.bfloat16)))
    merged = over_core(own_sum, other_sum)
    last = merged[0]
    for d in range(1, lay.places):
        last = last + along(merged[d].astype(jnp.bfloat16), d).astype(jnp.float32)
    second = 2.0 * ((shifted_part(first) + last) / spectrum_half) - start
    return first.reshape(vectors.shape), second.reshape(vectors.shape)


def solution(mesh):
    in_specs = (
        P(axes, None),
        P(axes),
        P(axes, None, None),
        P("col", "row", None, None),
        P(),
        P(),
        P(axes, None),
        P(axes),
    )
    out_specs = (P(axes, None), P(axes, None))
    return jax.shard_map(
        on_device, mesh=mesh, in_specs=in_specs, out_specs=out_specs, check_vma=False
    )
```

```python
import functools

import jax
import jax.numpy as jnp
from jax import lax
from jax.experimental import pallas as pl
from jax.experimental.pallas import tpu as pltpu
from jax.sharding import PartitionSpec as P

spectrum_center = 2.0
spectrum_half = 3.0
axes = ("row", "col")
chunk_groups = 8
mib = 1 << 20


class Layout:
    def __init__(self, rows, cols, blocks, pairs, side, width, points, slots_dev, tile_max, unroll):
        self.rows, self.cols, self.blocks = rows, cols, blocks
        self.pairs, self.side, self.width = pairs, side, width
        self.points, self.slots_dev, self.tile_max = points, slots_dev, tile_max
        self.places = rows // 2
        self.near = max(self.places // 2, 1)
        self.owners = 2 if self.places > 1 else 1
        self.spread = cols * blocks
        self.inputs = self.owners * self.spread
        self.outputs = rows * blocks
        self.slots = 2 * self.near * slots_dev
        self.unroll = unroll
        self.vmem = 60 * mib
        most = self.owners * tile_max + self.inputs * (unroll - 1) + unroll
        self.groups = -(-most // (unroll * chunk_groups)) * chunk_groups

    def line_steps(self):
        return [d for d in range(1, self.places) if d != self.near]


def plan_kernel(lay, ids, listed, fine, stored, slot_of, valid, sizes, group_input, entries, fill):
    place, core, col = ids[0], ids[1], ids[2]
    half = lax.div(place, lay.near)
    blank = lay.outputs * lay.points

    for owner in range(lay.owners):

        def examine(i, found):
            p = owner * lay.spread + i
            from_col = lax.bitwise_xor(lax.div(i, lay.blocks), col)
            from_place = lax.bitwise_xor(place, owner * lay.near)
            block = ((from_place * 2 + core) * lay.cols + from_col) * lay.blocks + lax.rem(i, lay.blocks)
            position = stored[fine[block]]
            at_row = lax.div(position, lay.slots_dev)
            at_place, at_core = lax.div(at_row, 2), lax.rem(at_row, 2)
            slot = (lax.bitwise_xor(at_place, place) * 2 + lax.bitwise_xor(at_core, core)) * lay.slots_dev
            slot = slot + lax.rem(position, lay.slots_dev)
            here = lax.div(at_place, lay.near) == half
            slot_of[p] = jnp.where(here, slot, -1)
            valid[owner * (lay.spread + 1) + found] = i
            fill[p] = 0
            return found + here.astype(jnp.int32)

        sizes[1 + owner] = lax.fori_loop(0, lay.spread, examine, 0)

    def input_of(owner, code):
        j = lax.rem(code, lay.spread)
        from_col = lax.bitwise_xor(lax.div(j, lay.blocks), col)
        return owner * lay.spread + from_col * lay.blocks + lax.rem(j, lay.blocks)

    for owner in range(lay.owners):

        def count(i, carry):
            p = input_of(owner, listed[owner, i])
            fill[p] = fill[p] + 1
            return carry

        lax.fori_loop(0, listed[owner, lay.tile_max], count, 0)

    group_input[0] = 0

    def place_groups(p, start):
        used = jnp.where(slot_of[p] >= 0, fill[p], 0)
        fill[p] = start * lay.unroll
        end = start + lax.div(used + (lay.unroll - 1), lay.unroll)

        def name(group, carry):
            group_input[group] = p
            return carry

        lax.fori_loop(start, end, name, 0)
        return end

    total = 1
    for owner in range(lay.owners):
        if owner > 0:
            sizes[lay.owners + owner] = total
        total = lax.fori_loop(owner * lay.spread, (owner + 1) * lay.spread, place_groups, total)
    sizes[0] = total

    def clear(i, carry):
        entries[i] = blank
        return carry

    lax.fori_loop(0, total * lay.unroll, clear, 0)

    for owner in range(lay.owners):

        def put(i, carry):
            code = listed[owner, i]
            p = input_of(owner, code)

            @pl.when(slot_of[p] >= 0)
            def _():
                out = lax.div(code, lay.spread)
                at_row = lax.div(out, lay.blocks)
                within = lax.rem(out, lay.blocks)
                far = lax.bitwise_xor(lax.div(at_row, 2), place)
                other = lax.bitwise_xor(lax.rem(at_row, 2), core)
                q = (other * lay.places + far) * lay.blocks + within
                a = fine[(at_row * lay.cols + col) * lay.blocks + within] - col * lay.points
                spot = fill[p]
                entries[spot] = q * lay.points + a
                fill[p] = spot + 1

            return carry

        lax.fori_loop(0, listed[owner, lay.tile_max], put, 0)


def make_plan(lay, ids, listed, fine, stored):
    smem = pl.BlockSpec(memory_space=pltpu.SMEM)
    lengths = (
        lay.inputs,
        lay.owners * (lay.spread + 1),
        2 * lay.owners,
        lay.groups,
        lay.groups * lay.unroll,
    )
    return pl.pallas_call(
        functools.partial(plan_kernel, lay),
        out_shape=tuple(jax.ShapeDtypeStruct((n,), jnp.int32) for n in lengths),
        in_specs=[smem] * 4,
        out_specs=(smem,) * 5,
        scratch_shapes=[pltpu.SMEM((lay.inputs,), jnp.int32)],
        cost_estimate=pl.CostEstimate(flops=0, bytes_accessed=20_000_000, transcendentals=0),
    )(ids, listed, fine, stored)


def add_products(lay, group, group_input, entries, tiles, rounded, total):
    held = tiles[pl.ds(group * lay.unroll, lay.unroll)].reshape(lay.unroll * lay.side, lay.side)
    products = jnp.dot(held, rounded[group_input[group]], preferred_element_type=jnp.float32)
    for i in range(lay.unroll):
        q = lax.div(entries[group * lay.unroll + i], lay.points)
        total[q] = total[q] + products[i * lay.side : (i + 1) * lay.side]


def turn_own_kernel(lay, given, turned):
    for t in range(lay.blocks):
        turned[t] = given[t, 0 : lay.pairs, :].T


def turn_own(lay, joined):
    vmem = pl.BlockSpec(memory_space=pltpu.VMEM)
    return pl.pallas_call(
        functools.partial(turn_own_kernel, lay),
        out_shape=jax.ShapeDtypeStruct((lay.blocks, lay.side, lay.pairs), jnp.bfloat16),
        in_specs=[vmem],
        out_specs=vmem,
        compiler_params=pltpu.CompilerParams(vmem_limit_bytes=16 * mib),
        cost_estimate=pl.CostEstimate(flops=1_000_000, bytes_accessed=5_000_000, transcendentals=0),
    )(joined)


def turn_both_kernel(lay, given, own, out):
    out[0 : lay.blocks] = own[...]
    for t in range(lay.blocks):
        out[lay.blocks + t] = given[t, 0 : lay.pairs, :].T


def turn_both(lay, partner, own):
    vmem = pl.BlockSpec(memory_space=pltpu.VMEM)
    return pl.pallas_call(
        functools.partial(turn_both_kernel, lay),
        out_shape=jax.ShapeDtypeStruct((2 * lay.blocks, lay.side, lay.pairs), jnp.bfloat16),
        in_specs=[vmem] * 2,
        out_specs=vmem,
        compiler_params=pltpu.CompilerParams(vmem_limit_bytes=16 * mib),
        cost_estimate=pl.CostEstimate(flops=1_000_000, bytes_accessed=5_000_000, transcendentals=0),
    )(partner, own)


def project_kernel(lay, owner, slot_of, valid, sizes, *refs):
    refs = list(refs)
    given_in = [refs.pop(0) for _ in range(lay.cols)]
    given_coarse = [refs.pop(0) for _ in range(2 * lay.near)]
    out, right, blocks, projected, sems, out_sems = refs
    copies = []

    def fetch(source, target):
        copies.append(pltpu.make_async_copy(source, target, sems.at[len(copies)]))
        copies[-1].start()

    for i in range(2 * lay.near):
        for a in range(lay.points):
            fetch(given_coarse[i].at[a], blocks.at[a, pl.ds(i * lay.slots_dev, lay.slots_dev)])
    for i in range(lay.cols):
        fetch(given_in[i].at[:, pl.ds(0, lay.pairs)], right.at[pl.ds(i * lay.blocks, lay.blocks)])
    for copy in copies:
        copy.wait()
    found = sizes[1 + owner]

    def visit(step, carry):
        for lane in range(2):
            i = valid[owner * (lay.spread + 1) + jnp.minimum(2 * step + lane, found - 1)]
            slot = slot_of[owner * lay.spread + i]
            for a in range(lay.points):
                projected[i, :, a * lay.side : (a + 1) * lay.side] = jnp.dot(
                    blocks[a, slot], right[i], preferred_element_type=jnp.float32
                ).astype(jnp.bfloat16)
        return carry

    lax.fori_loop(0, lax.div(found + 1, 2), visit, 0)

    def store(i):
        return pltpu.make_async_copy(projected.at[i], out.at[i], out_sems.at[i])

    for i in range(lay.spread):

        @pl.when(slot_of[owner * lay.spread + i] >= 0)
        def _():
            store(i).start()

    for i in range(lay.spread):

        @pl.when(slot_of[owner * lay.spread + i] >= 0)
        def _():
            store(i).wait()


def project(lay, owner, plan, inputs, coarse):
    smem = pl.BlockSpec(memory_space=pltpu.SMEM)
    hbm = pl.BlockSpec(memory_space=pl.ANY)
    shape = (lay.spread, lay.pairs, lay.points * lay.side)
    return pl.pallas_call(
        functools.partial(project_kernel, lay, owner),
        out_shape=jax.ShapeDtypeStruct(shape, jnp.bfloat16),
        in_specs=[smem] * 3 + [hbm] * (len(inputs) + len(coarse)),
        out_specs=hbm,
        scratch_shapes=[
            pltpu.VMEM((lay.spread, lay.pairs, lay.side), jnp.bfloat16),
            pltpu.VMEM((lay.points, lay.slots, lay.pairs, lay.pairs), jnp.bfloat16),
            pltpu.VMEM(shape, jnp.bfloat16),
            pltpu.SemaphoreType.DMA((len(inputs) + len(coarse) * lay.points,)),
            pltpu.SemaphoreType.DMA((lay.spread,)),
        ],
        compiler_params=pltpu.CompilerParams(vmem_limit_bytes=lay.vmem),
        cost_estimate=pl.CostEstimate(flops=1_000_000_000, bytes_accessed=16_000_000, transcendentals=0),
    )(*plan[:3], *inputs, *coarse)


def tiles_kernel(lay, slot_of, sizes, group_input, entries, *refs):
    lines = lay.line_steps()
    refs = list(refs)
    given_in = [refs.pop(0) for _ in range(lay.owners * lay.cols)]
    given_out = [refs.pop(0) for _ in range(2 * (1 + len(lines)))]
    given_projected = [refs.pop(0) for _ in range(lay.owners)]
    own_sum, other_sum, tiles_out = refs[:3]
    left, projected, rounded, tiles, total, sems, sum_sems, in_sems, out_sems = refs[3:]
    copies = []

    def fetch(source, target):
        copies.append(pltpu.make_async_copy(source, target, sems.at[len(copies)]))
        copies[-1].start()

    def load(p):
        source = given_projected[p // lay.spread].at[p % lay.spread]
        return pltpu.make_async_copy(source, projected.at[p], in_sems.at[p])

    for k in range(2):
        held = given_out[k * (1 + len(lines)) :]
        for g in range(lay.owners):
            spot = (k * lay.places + g * lay.near) * lay.blocks
            fetch(held[0].at[pl.ds(g * lay.blocks, lay.blocks)], left.at[pl.ds(spot, lay.blocks)])
        for i, d in enumerate(lines):
            spot = (k * lay.places + d) * lay.blocks
            fetch(held[1 + i], left.at[pl.ds(spot, lay.blocks)])
    for i, ref in enumerate(given_in):
        part = pl.ds(i * lay.blocks, lay.blocks)
        fetch(ref.at[:, pl.ds(lay.pairs, lay.side)], rounded.at[part])
    for p in range(lay.inputs):

        @pl.when(slot_of[p] >= 0)
        def _():
            load(p).start()

    total[...] = jnp.zeros_like(total)
    for copy in copies:
        copy.wait()
    used = sizes[0]

    for owner in range(lay.owners):
        for p in range(owner * lay.spread, (owner + 1) * lay.spread):

            @pl.when(slot_of[p] >= 0)
            def _():
                load(p).wait()

        def group_step(group, carry):
            block = projected[group_input[group]]
            numbers = [entries[group * lay.unroll + i] for i in range(lay.unroll)]
            places = [jnp.minimum(lax.div(n, lay.points), lay.outputs - 1) for n in numbers]
            lefts = jnp.concatenate([left[q] for q in places], axis=0)
            both = jnp.dot(lefts, block, preferred_element_type=jnp.float32)
            for i in range(lay.unroll):
                mine = both[i * lay.side : (i + 1) * lay.side]
                tile = mine[:, : lay.side]
                for b in range(1, lay.points):
                    at_b = mine[:, b * lay.side : (b + 1) * lay.side]
                    tile = jnp.where(lax.rem(numbers[i], lay.points) == b, at_b, tile)
                tiles[group * lay.unroll + i] = tile.astype(jnp.bfloat16)
            add_products(lay, group - 1, group_input, entries, tiles, rounded, total)
            return carry

        first = 1 if owner == 0 else sizes[lay.owners + owner]
        last = used if owner == lay.owners - 1 else sizes[lay.owners + owner + 1]
        lax.fori_loop(first, last, group_step, 0)

    span = chunk_groups * lay.unroll

    def store(chunk):
        part = pl.ds(chunk * span, span)
        return pltpu.make_async_copy(tiles.at[part], tiles_out.at[part], out_sems.at[chunk])

    for chunk in range(lay.groups // chunk_groups):

        @pl.when(used > chunk * chunk_groups)
        def _():
            store(chunk).start()

    add_products(lay, used - 1, group_input, entries, tiles, rounded, total)
    give_sums(lay, total, own_sum, other_sum, sum_sems)
    for chunk in range(lay.groups // chunk_groups):

        @pl.when(used > chunk * chunk_groups)
        def _():
            store(chunk).wait()


def give_sums(lay, total, own_sum, other_sum, sems):
    own = lay.places * lay.blocks
    for copy in (
        pltpu.make_async_copy(total.at[pl.ds(own, own)], other_sum, sems.at[1]),
        pltpu.make_async_copy(total.at[pl.ds(0, own)], own_sum, sems.at[0]),
    ):
        copy.start()
    pltpu.make_async_copy(total.at[pl.ds(own, own)], other_sum, sems.at[1]).wait()
    pltpu.make_async_copy(total.at[pl.ds(0, own)], own_sum, sems.at[0]).wait()


def make_tiles(lay, plan, inputs, outputs, projected):
    smem = pl.BlockSpec(memory_space=pltpu.SMEM)
    hbm = pl.BlockSpec(memory_space=pl.ANY)
    own = lay.places * lay.blocks
    sums = jax.ShapeDtypeStruct((own, lay.side, lay.width), jnp.float32)
    tiles = (lay.groups * lay.unroll, lay.side, lay.side)
    return pl.pallas_call(
        functools.partial(tiles_kernel, lay),
        out_shape=(sums, sums, jax.ShapeDtypeStruct(tiles, jnp.bfloat16)),
        in_specs=[smem] * 4 + [hbm] * (len(inputs) + len(outputs) + len(projected)),
        out_specs=(hbm,) * 3,
        scratch_shapes=[
            pltpu.VMEM((lay.outputs, lay.side, lay.pairs), jnp.bfloat16),
            pltpu.VMEM((lay.inputs, lay.pairs, lay.points * lay.side), jnp.bfloat16),
            pltpu.VMEM((lay.inputs, lay.side, lay.width), jnp.bfloat16),
            pltpu.VMEM(tiles, jnp.bfloat16),
            pltpu.VMEM((lay.outputs + 1, lay.side, lay.width), jnp.float32),
            pltpu.SemaphoreType.DMA((len(inputs) + 2 * lay.places,)),
            pltpu.SemaphoreType.DMA((2,)),
            pltpu.SemaphoreType.DMA((lay.inputs,)),
            pltpu.SemaphoreType.DMA((lay.groups // chunk_groups,)),
        ],
        compiler_params=pltpu.CompilerParams(vmem_limit_bytes=lay.vmem),
        cost_estimate=pl.CostEstimate(flops=4_000_000_000, bytes_accessed=30_000_000, transcendentals=0),
    )(plan[0], *plan[2:], *inputs, *outputs, *projected)


def apply_kernel(lay, sizes, group_input, entries, tiles_in, *refs):
    given_vec = refs[: lay.cols]
    own_sum, other_sum = refs[lay.cols : lay.cols + 2]
    rounded, tiles, total, sems, sum_sems, out_sems = refs[lay.cols + 2 :]
    used = sizes[0]
    span = chunk_groups * lay.unroll

    def load(chunk):
        part = pl.ds(chunk * span, span)
        return pltpu.make_async_copy(tiles_in.at[part], tiles.at[part], out_sems.at[chunk])

    for chunk in range(lay.groups // chunk_groups):

        @pl.when(used > chunk * chunk_groups)
        def _():
            load(chunk).start()

    copies = []
    for d in range(lay.cols):
        for g in range(lay.owners):
            target = rounded.at[pl.ds((g * lay.cols + d) * lay.blocks, lay.blocks)]
            copies.append(pltpu.make_async_copy(given_vec[d].at[g], target, sems.at[len(copies)]))
            copies[-1].start()
    total[...] = jnp.zeros_like(total)
    for copy in copies:
        copy.wait()
    for chunk in range(lay.groups // chunk_groups):

        @pl.when(used > chunk * chunk_groups)
        def _():
            load(chunk).wait()

    def group_step(group, carry):
        add_products(lay, group, group_input, entries, tiles, rounded, total)
        return carry

    lax.fori_loop(1, used, group_step, 0)
    give_sums(lay, total, own_sum, other_sum, sum_sems)


def apply_tiles(lay, plan, tiles, rounded):
    smem = pl.BlockSpec(memory_space=pltpu.SMEM)
    hbm = pl.BlockSpec(memory_space=pl.ANY)
    own = lay.places * lay.blocks
    sums = jax.ShapeDtypeStruct((own, lay.side, lay.width), jnp.float32)
    return pl.pallas_call(
        functools.partial(apply_kernel, lay),
        out_shape=(sums, sums),
        in_specs=[smem] * 3 + [hbm] * (1 + len(rounded)),
        out_specs=(hbm, hbm),
        scratch_shapes=[
            pltpu.VMEM((lay.inputs, lay.side, lay.width), jnp.bfloat16),
            pltpu.VMEM(tiles.shape, jnp.bfloat16),
            pltpu.VMEM((lay.outputs + 1, lay.side, lay.width), jnp.float32),
            pltpu.SemaphoreType.DMA((len(rounded) * lay.owners,)),
            pltpu.SemaphoreType.DMA((2,)),
            pltpu.SemaphoreType.DMA((lay.groups // chunk_groups,)),
        ],
        compiler_params=pltpu.CompilerParams(vmem_limit_bytes=lay.vmem),
        cost_estimate=pl.CostEstimate(flops=400_000_000, bytes_accessed=4_000_000, transcendentals=0),
    )(*plan[2:], tiles, *rounded)


def on_device(
    vectors, energies, intersections, coarse, fine_coarse, coarse_slot, tile_codes, tile_count
):
    rows = lax.axis_size("row")
    cols = lax.axis_size("col")
    row_id = lax.axis_index("row")
    col_id = lax.axis_index("col")
    blocks, pairs, side = intersections.shape
    width = vectors.shape[1]
    points, slots_dev = coarse.shape[:2]
    lay = Layout(rows, cols, blocks, pairs, side, width, points, slots_dev, tile_codes.shape[1], 4)
    if lay.groups * lay.unroll * side * side * 2 > 16 * mib:
        lay = Layout(rows, cols, blocks, pairs, side, width, points, slots_dev, tile_codes.shape[1], 1)
    near = lay.near

    def move(array, row_step, col_step):
        pairs_list = [
            (r * cols + c, (r ^ row_step) * cols + (c ^ col_step)) for r in range(rows) for c in range(cols)
        ]
        return lax.ppermute(array, axes, pairs_list)

    def along(array, step):
        return move(array, 2 * step, 0)

    def to_core(array):
        return move(array, 1, 0)

    def in_plane(array):
        return [array] + [move(array, 0, d) for d in range(1, cols)]

    start = vectors.reshape(blocks, side, width)
    energy = energies.reshape(blocks, side, 1)
    two_owners = lay.owners == 2
    ids = jnp.stack([row_id // 2, row_id % 2, col_id]).astype(jnp.int32)
    listed = jnp.concatenate([tile_codes, tile_count[:, None]], axis=1)
    n_listed = listed.shape[1]
    digits = jnp.concatenate([listed[0] >> 8, listed[0] & 255]).astype(jnp.bfloat16)
    depth = 16 * -(-2 * n_listed // (16 * width * blocks))
    digits = jnp.pad(digits, (0, blocks * depth * width - 2 * n_listed)).reshape(blocks, depth, width)
    joined = jnp.concatenate([intersections, start.astype(jnp.bfloat16), digits], axis=1)

    near_coarse = [along(coarse, e) for e in range(1, near)]
    partner = [along(joined, near)] if two_owners else []
    inputs = in_plane(joined)
    inputs, partner, late_joined = lax.optimization_barrier((inputs, partner, joined))
    if two_owners:
        sent = partner[0][:, pairs + side :].reshape(-1)[: 2 * n_listed].astype(jnp.int32)
        listed = jnp.concatenate([listed, ((sent[:n_listed] << 8) + sent[n_listed:])[None]], axis=0)
    plan = make_plan(lay, ids, listed, fine_coarse, coarse_slot)
    for part in partner:
        inputs = inputs + in_plane(part)
    turned = turn_own(lay, late_joined)
    inputs[-1], near_coarse = lax.optimization_barrier((inputs[-1], near_coarse))
    turned, near_coarse, plan = lax.optimization_barrier((turned, near_coarse, plan))
    blocks_coarse = []
    for part in [coarse] + near_coarse:
        blocks_coarse += [part, to_core(part)]
    turned, blocks_coarse = lax.optimization_barrier((turned, blocks_coarse))
    lines = [along(turned, d) for d in lay.line_steps()]
    for part in partner:
        turned = turn_both(lay, part, turned)
    projected = [
        project(lay, g, plan, inputs[g * cols : (g + 1) * cols], blocks_coarse) for g in range(lay.owners)
    ]
    lines, turned, projected = lax.optimization_barrier((lines, turned, projected))
    lefts = [turned] + lines
    lefts = lefts + [to_core(part) for part in lefts]
    own_sum, other_sum, tiles = make_tiles(lay, plan, inputs, lefts, projected)

    def over_core(own_part, other_part):
        return (own_part + to_core(other_part)).reshape(lay.places, blocks, side, width)

    def shifted_part(field):
        return energy * field - spectrum_center * field

    merged = over_core(own_sum, other_sum)
    if two_owners:
        sums = jnp.stack([merged[0] + shifted_part(start), merged[near]])
        for e in range(1, near):
            sent = jnp.stack([merged[e], merged[e ^ near]]).astype(jnp.bfloat16)
            sums = sums + along(sent, e).astype(jnp.float32)
        sums = sums + along(sums.astype(jnp.bfloat16), near)[::-1].astype(jnp.float32)
    else:
        sums = merged + shifted_part(start)[None]

    firsts = sums / spectrum_half
    first = firsts[0]
    own_sum, other_sum = apply_tiles(lay, plan, tiles, in_plane(firsts.astype(jnp.bfloat16)))
    merged = over_core(own_sum, other_sum)
    last = merged[0]
    for d in range(1, lay.places):
        last = last + along(merged[d].astype(jnp.bfloat16), d).astype(jnp.float32)
    second = 2.0 * ((shifted_part(first) + last) / spectrum_half) - start
    return first.reshape(vectors.shape), second.reshape(vectors.shape)


def solution(mesh):
    in_specs = (
        P(axes, None),
        P(axes),
        P(axes, None, None),
        P("col", "row", None, None),
        P(),
        P(),
        P(axes, None),
        P(axes),
    )
    out_specs = (P(axes, None), P(axes, None))
    return jax.shard_map(
        on_device, mesh=mesh, in_specs=in_specs, out_specs=out_specs, check_vma=False
    )
```

```python
import functools

import jax
import jax.numpy as jnp
from jax import lax
from jax.experimental import pallas as pl
from jax.experimental.pallas import tpu as pltpu
from jax.sharding import PartitionSpec as P

spectrum_center = 2.0
spectrum_half = 3.0
axes = ("row", "col")
chunk_groups = 8
mib = 1 << 20


class Layout:
    def __init__(self, rows, cols, blocks, pairs, side, width, points, slots_dev, tile_max, unroll):
        self.rows, self.cols, self.blocks = rows, cols, blocks
        self.pairs, self.side, self.width = pairs, side, width
        self.points, self.slots_dev, self.tile_max = points, slots_dev, tile_max
        self.places = rows // 2
        self.near = max(self.places // 2, 1)
        self.owners = 2 if self.places > 1 else 1
        self.spread = cols * blocks
        self.inputs = self.owners * self.spread
        self.outputs = rows * blocks
        self.slots = 2 * self.near * slots_dev
        self.unroll = unroll
        self.vmem = 60 * mib
        most = self.owners * tile_max + self.inputs * (unroll - 1) + unroll
        self.groups = -(-most // (unroll * chunk_groups)) * chunk_groups

    def line_steps(self):
        return [d for d in range(1, self.places) if d != self.near]


def plan_kernel(lay, ids, listed, fine, stored, slot_of, valid, sizes, group_input, entries, fill):
    place, core, col = ids[0], ids[1], ids[2]
    half = lax.div(place, lay.near)
    blank = lay.outputs * lay.points

    for owner in range(lay.owners):

        def examine(i, found):
            p = owner * lay.spread + i
            from_col = lax.bitwise_xor(lax.div(i, lay.blocks), col)
            from_place = lax.bitwise_xor(place, owner * lay.near)
            block = ((from_place * 2 + core) * lay.cols + from_col) * lay.blocks + lax.rem(i, lay.blocks)
            position = stored[fine[block]]
            at_row = lax.div(position, lay.slots_dev)
            at_place, at_core = lax.div(at_row, 2), lax.rem(at_row, 2)
            slot = (lax.bitwise_xor(at_place, place) * 2 + lax.bitwise_xor(at_core, core)) * lay.slots_dev
            slot = slot + lax.rem(position, lay.slots_dev)
            here = lax.div(at_place, lay.near) == half
            slot_of[p] = jnp.where(here, slot, -1)
            valid[owner * (lay.spread + 1) + found] = i
            fill[p] = 0
            return found + here.astype(jnp.int32)

        sizes[1 + owner] = lax.fori_loop(0, lay.spread, examine, 0)

    def input_of(owner, code):
        j = lax.rem(code, lay.spread)
        from_col = lax.bitwise_xor(lax.div(j, lay.blocks), col)
        return owner * lay.spread + from_col * lay.blocks + lax.rem(j, lay.blocks)

    for owner in range(lay.owners):

        def count(i, carry):
            p = input_of(owner, listed[owner, i])
            fill[p] = fill[p] + 1
            return carry

        lax.fori_loop(0, listed[owner, lay.tile_max], count, 0)

    group_input[0] = 0

    def place_groups(p, start):
        used = jnp.where(slot_of[p] >= 0, fill[p], 0)
        fill[p] = start * lay.unroll
        end = start + lax.div(used + (lay.unroll - 1), lay.unroll)

        def name(group, carry):
            group_input[group] = p
            return carry

        lax.fori_loop(start, end, name, 0)
        return end

    total = 1
    for owner in range(lay.owners):
        if owner > 0:
            sizes[lay.owners + owner] = total
        total = lax.fori_loop(owner * lay.spread, (owner + 1) * lay.spread, place_groups, total)
    sizes[0] = total

    def clear(i, carry):
        entries[i] = blank
        return carry

    lax.fori_loop(0, total * lay.unroll, clear, 0)

    for owner in range(lay.owners):

        def put(i, carry):
            code = listed[owner, i]
            p = input_of(owner, code)

            @pl.when(slot_of[p] >= 0)
            def _():
                out = lax.div(code, lay.spread)
                at_row = lax.div(out, lay.blocks)
                within = lax.rem(out, lay.blocks)
                far = lax.bitwise_xor(lax.div(at_row, 2), place)
                other = lax.bitwise_xor(lax.rem(at_row, 2), core)
                q = (other * lay.places + far) * lay.blocks + within
                a = fine[(at_row * lay.cols + col) * lay.blocks + within] - col * lay.points
                spot = fill[p]
                entries[spot] = q * lay.points + a
                fill[p] = spot + 1

            return carry

        lax.fori_loop(0, listed[owner, lay.tile_max], put, 0)


def make_plan(lay, ids, listed, fine, stored):
    smem = pl.BlockSpec(memory_space=pltpu.SMEM)
    lengths = (
        lay.inputs,
        lay.owners * (lay.spread + 1),
        2 * lay.owners,
        lay.groups,
        lay.groups * lay.unroll,
    )
    return pl.pallas_call(
        functools.partial(plan_kernel, lay),
        out_shape=tuple(jax.ShapeDtypeStruct((n,), jnp.int32) for n in lengths),
        in_specs=[smem] * 4,
        out_specs=(smem,) * 5,
        scratch_shapes=[pltpu.SMEM((lay.inputs,), jnp.int32)],
        cost_estimate=pl.CostEstimate(flops=0, bytes_accessed=20_000_000, transcendentals=0),
    )(ids, listed, fine, stored)


def add_products(lay, group, group_input, entries, tiles, rounded, total):
    held = tiles[pl.ds(group * lay.unroll, lay.unroll)].reshape(lay.unroll * lay.side, lay.side)
    products = jnp.dot(held, rounded[group_input[group]], preferred_element_type=jnp.float32)
    for i in range(lay.unroll):
        q = lax.div(entries[group * lay.unroll + i], lay.points)
        total[q] = total[q] + products[i * lay.side : (i + 1) * lay.side]


def turn_own_kernel(lay, given, turned):
    for t in range(lay.blocks):
        turned[t] = given[t, 0 : lay.pairs, :].T


def turn_own(lay, joined):
    vmem = pl.BlockSpec(memory_space=pltpu.VMEM)
    return pl.pallas_call(
        functools.partial(turn_own_kernel, lay),
        out_shape=jax.ShapeDtypeStruct((lay.blocks, lay.side, lay.pairs), jnp.bfloat16),
        in_specs=[vmem],
        out_specs=vmem,
        compiler_params=pltpu.CompilerParams(vmem_limit_bytes=16 * mib),
        cost_estimate=pl.CostEstimate(flops=1_000_000, bytes_accessed=5_000_000, transcendentals=0),
    )(joined)


def turn_both_kernel(lay, given, own, out):
    out[0 : lay.blocks] = own[...]
    for t in range(lay.blocks):
        out[lay.blocks + t] = given[t, 0 : lay.pairs, :].T


def turn_both(lay, partner, own):
    vmem = pl.BlockSpec(memory_space=pltpu.VMEM)
    return pl.pallas_call(
        functools.partial(turn_both_kernel, lay),
        out_shape=jax.ShapeDtypeStruct((2 * lay.blocks, lay.side, lay.pairs), jnp.bfloat16),
        in_specs=[vmem] * 2,
        out_specs=vmem,
        compiler_params=pltpu.CompilerParams(vmem_limit_bytes=16 * mib),
        cost_estimate=pl.CostEstimate(flops=1_000_000, bytes_accessed=5_000_000, transcendentals=0),
    )(partner, own)


def project_kernel(lay, owner, slot_of, valid, sizes, *refs):
    refs = list(refs)
    given_in = [refs.pop(0) for _ in range(lay.cols)]
    given_coarse = [refs.pop(0) for _ in range(2 * lay.near)]
    out, right, blocks, projected, sems, out_sems = refs
    copies = []

    def fetch(source, target):
        copies.append(pltpu.make_async_copy(source, target, sems.at[len(copies)]))
        copies[-1].start()

    for i in range(2 * lay.near):
        for a in range(lay.points):
            fetch(given_coarse[i].at[a], blocks.at[a, pl.ds(i * lay.slots_dev, lay.slots_dev)])
    for i in range(lay.cols):
        fetch(given_in[i].at[:, pl.ds(0, lay.pairs)], right.at[pl.ds(i * lay.blocks, lay.blocks)])
    for copy in copies:
        copy.wait()
    found = sizes[1 + owner]

    def visit(step, carry):
        for lane in range(2):
            i = valid[owner * (lay.spread + 1) + jnp.minimum(2 * step + lane, found - 1)]
            slot = slot_of[owner * lay.spread + i]
            for a in range(lay.points):
                projected[i, :, a * lay.side : (a + 1) * lay.side] = jnp.dot(
                    blocks[a, slot], right[i], preferred_element_type=jnp.float32
                ).astype(jnp.bfloat16)
        return carry

    lax.fori_loop(0, lax.div(found + 1, 2), visit, 0)

    def store(i):
        return pltpu.make_async_copy(projected.at[i], out.at[i], out_sems.at[i])

    for i in range(lay.spread):

        @pl.when(slot_of[owner * lay.spread + i] >= 0)
        def _():
            store(i).start()

    for i in range(lay.spread):

        @pl.when(slot_of[owner * lay.spread + i] >= 0)
        def _():
            store(i).wait()


def project(lay, owner, plan, inputs, coarse):
    smem = pl.BlockSpec(memory_space=pltpu.SMEM)
    hbm = pl.BlockSpec(memory_space=pl.ANY)
    shape = (lay.spread, lay.pairs, lay.points * lay.side)
    return pl.pallas_call(
        functools.partial(project_kernel, lay, owner),
        out_shape=jax.ShapeDtypeStruct(shape, jnp.bfloat16),
        in_specs=[smem] * 3 + [hbm] * (len(inputs) + len(coarse)),
        out_specs=hbm,
        scratch_shapes=[
            pltpu.VMEM((lay.spread, lay.pairs, lay.side), jnp.bfloat16),
            pltpu.VMEM((lay.points, lay.slots, lay.pairs, lay.pairs), jnp.bfloat16),
            pltpu.VMEM(shape, jnp.bfloat16),
            pltpu.SemaphoreType.DMA((len(inputs) + len(coarse) * lay.points,)),
            pltpu.SemaphoreType.DMA((lay.spread,)),
        ],
        compiler_params=pltpu.CompilerParams(vmem_limit_bytes=lay.vmem),
        cost_estimate=pl.CostEstimate(flops=1_000_000_000, bytes_accessed=16_000_000, transcendentals=0),
    )(*plan[:3], *inputs, *coarse)


def tiles_kernel(lay, slot_of, sizes, group_input, entries, *refs):
    lines = lay.line_steps()
    refs = list(refs)
    given_in = [refs.pop(0) for _ in range(lay.owners * lay.cols)]
    given_out = [refs.pop(0) for _ in range(2 * (1 + len(lines)))]
    given_projected = [refs.pop(0) for _ in range(lay.owners)]
    own_sum, other_sum, tiles_out = refs[:3]
    left, projected, rounded, tiles, total, sent, sems, sum_sems, in_sems, out_sems = refs[3:]
    copies = []

    def fetch(source, target):
        copies.append(pltpu.make_async_copy(source, target, sems.at[len(copies)]))
        copies[-1].start()

    def load(p):
        source = given_projected[p // lay.spread].at[p % lay.spread]
        return pltpu.make_async_copy(source, projected.at[p], in_sems.at[p])

    for k in range(2):
        held = given_out[k * (1 + len(lines)) :]
        for g in range(lay.owners):
            spot = (k * lay.places + g * lay.near) * lay.blocks
            fetch(held[0].at[pl.ds(g * lay.blocks, lay.blocks)], left.at[pl.ds(spot, lay.blocks)])
        for i, d in enumerate(lines):
            spot = (k * lay.places + d) * lay.blocks
            fetch(held[1 + i], left.at[pl.ds(spot, lay.blocks)])
    for i, ref in enumerate(given_in):
        part = pl.ds(i * lay.blocks, lay.blocks)
        fetch(ref.at[:, pl.ds(lay.pairs, lay.side)], rounded.at[part])
    for p in range(lay.inputs):

        @pl.when(slot_of[p] >= 0)
        def _():
            load(p).start()

    total[...] = jnp.zeros_like(total)
    for copy in copies:
        copy.wait()
    used = sizes[0]

    for owner in range(lay.owners):
        for p in range(owner * lay.spread, (owner + 1) * lay.spread):

            @pl.when(slot_of[p] >= 0)
            def _():
                load(p).wait()

        def group_step(group, carry):
            block = projected[group_input[group]]
            numbers = [entries[group * lay.unroll + i] for i in range(lay.unroll)]
            places = [jnp.minimum(lax.div(n, lay.points), lay.outputs - 1) for n in numbers]
            lefts = jnp.concatenate([left[q] for q in places], axis=0)
            both = jnp.dot(lefts, block, preferred_element_type=jnp.float32)
            for i in range(lay.unroll):
                mine = both[i * lay.side : (i + 1) * lay.side]
                tile = mine[:, : lay.side]
                for b in range(1, lay.points):
                    at_b = mine[:, b * lay.side : (b + 1) * lay.side]
                    tile = jnp.where(lax.rem(numbers[i], lay.points) == b, at_b, tile)
                tiles[group * lay.unroll + i] = tile.astype(jnp.bfloat16)
            add_products(lay, group - 1, group_input, entries, tiles, rounded, total)
            return carry

        first = 1 if owner == 0 else sizes[lay.owners + owner]
        last = used if owner == lay.owners - 1 else sizes[lay.owners + owner + 1]
        lax.fori_loop(first, last, group_step, 0)

    span = chunk_groups * lay.unroll

    def store(chunk):
        part = pl.ds(chunk * span, span)
        return pltpu.make_async_copy(tiles.at[part], tiles_out.at[part], out_sems.at[chunk])

    for chunk in range(lay.groups // chunk_groups):

        @pl.when(used > chunk * chunk_groups)
        def _():
            store(chunk).start()

    add_products(lay, used - 1, group_input, entries, tiles, rounded, total)
    give_sums(lay, total, sent, own_sum, other_sum, sum_sems)
    for chunk in range(lay.groups // chunk_groups):

        @pl.when(used > chunk * chunk_groups)
        def _():
            store(chunk).wait()


def give_sums(lay, total, sent, own_sum, other_sum, sems):
    own = lay.places * lay.blocks
    for_own = pltpu.make_async_copy(total.at[pl.ds(0, own)], own_sum, sems.at[0])
    for_own.start()
    sent[...] = total[own : 2 * own].astype(jnp.bfloat16)
    for_other = pltpu.make_async_copy(sent, other_sum, sems.at[1])
    for_other.start()
    for_own.wait()
    for_other.wait()


def make_tiles(lay, plan, inputs, outputs, projected):
    smem = pl.BlockSpec(memory_space=pltpu.SMEM)
    hbm = pl.BlockSpec(memory_space=pl.ANY)
    own = lay.places * lay.blocks
    sums = jax.ShapeDtypeStruct((own, lay.side, lay.width), jnp.float32)
    sent = jax.ShapeDtypeStruct((own, lay.side, lay.width), jnp.bfloat16)
    tiles = (lay.groups * lay.unroll, lay.side, lay.side)
    return pl.pallas_call(
        functools.partial(tiles_kernel, lay),
        out_shape=(sums, sent, jax.ShapeDtypeStruct(tiles, jnp.bfloat16)),
        in_specs=[smem] * 4 + [hbm] * (len(inputs) + len(outputs) + len(projected)),
        out_specs=(hbm,) * 3,
        scratch_shapes=[
            pltpu.VMEM((lay.outputs, lay.side, lay.pairs), jnp.bfloat16),
            pltpu.VMEM((lay.inputs, lay.pairs, lay.points * lay.side), jnp.bfloat16),
            pltpu.VMEM((lay.inputs, lay.side, lay.width), jnp.bfloat16),
            pltpu.VMEM(tiles, jnp.bfloat16),
            pltpu.VMEM((lay.outputs + 1, lay.side, lay.width), jnp.float32),
            pltpu.VMEM((own, lay.side, lay.width), jnp.bfloat16),
            pltpu.SemaphoreType.DMA((len(inputs) + 2 * lay.places,)),
            pltpu.SemaphoreType.DMA((2,)),
            pltpu.SemaphoreType.DMA((lay.inputs,)),
            pltpu.SemaphoreType.DMA((lay.groups // chunk_groups,)),
        ],
        compiler_params=pltpu.CompilerParams(vmem_limit_bytes=lay.vmem),
        cost_estimate=pl.CostEstimate(flops=4_000_000_000, bytes_accessed=30_000_000, transcendentals=0),
    )(plan[0], *plan[2:], *inputs, *outputs, *projected)


def apply_kernel(lay, sizes, group_input, entries, tiles_in, *refs):
    given_vec = refs[: lay.cols]
    own_sum, other_sum = refs[lay.cols : lay.cols + 2]
    rounded, tiles, total, sent, sems, sum_sems, out_sems = refs[lay.cols + 2 :]
    used = sizes[0]
    span = chunk_groups * lay.unroll

    def load(chunk):
        part = pl.ds(chunk * span, span)
        return pltpu.make_async_copy(tiles_in.at[part], tiles.at[part], out_sems.at[chunk])

    for chunk in range(lay.groups // chunk_groups):

        @pl.when(used > chunk * chunk_groups)
        def _():
            load(chunk).start()

    copies = []
    for d in range(lay.cols):
        for g in range(lay.owners):
            target = rounded.at[pl.ds((g * lay.cols + d) * lay.blocks, lay.blocks)]
            copies.append(pltpu.make_async_copy(given_vec[d].at[g], target, sems.at[len(copies)]))
            copies[-1].start()
    total[...] = jnp.zeros_like(total)
    for copy in copies:
        copy.wait()
    for chunk in range(lay.groups // chunk_groups):

        @pl.when(used > chunk * chunk_groups)
        def _():
            load(chunk).wait()

    def group_step(group, carry):
        add_products(lay, group, group_input, entries, tiles, rounded, total)
        return carry

    lax.fori_loop(1, used, group_step, 0)
    give_sums(lay, total, sent, own_sum, other_sum, sum_sems)


def apply_tiles(lay, plan, tiles, rounded):
    smem = pl.BlockSpec(memory_space=pltpu.SMEM)
    hbm = pl.BlockSpec(memory_space=pl.ANY)
    own = lay.places * lay.blocks
    sums = jax.ShapeDtypeStruct((own, lay.side, lay.width), jnp.float32)
    sent = jax.ShapeDtypeStruct((own, lay.side, lay.width), jnp.bfloat16)
    return pl.pallas_call(
        functools.partial(apply_kernel, lay),
        out_shape=(sums, sent),
        in_specs=[smem] * 3 + [hbm] * (1 + len(rounded)),
        out_specs=(hbm, hbm),
        scratch_shapes=[
            pltpu.VMEM((lay.inputs, lay.side, lay.width), jnp.bfloat16),
            pltpu.VMEM(tiles.shape, jnp.bfloat16),
            pltpu.VMEM((lay.outputs + 1, lay.side, lay.width), jnp.float32),
            pltpu.VMEM((own, lay.side, lay.width), jnp.bfloat16),
            pltpu.SemaphoreType.DMA((len(rounded) * lay.owners,)),
            pltpu.SemaphoreType.DMA((2,)),
            pltpu.SemaphoreType.DMA((lay.groups // chunk_groups,)),
        ],
        compiler_params=pltpu.CompilerParams(vmem_limit_bytes=lay.vmem),
        cost_estimate=pl.CostEstimate(flops=400_000_000, bytes_accessed=4_000_000, transcendentals=0),
    )(*plan[2:], tiles, *rounded)


def on_device(
    vectors, energies, intersections, coarse, fine_coarse, coarse_slot, tile_codes, tile_count
):
    rows = lax.axis_size("row")
    cols = lax.axis_size("col")
    row_id = lax.axis_index("row")
    col_id = lax.axis_index("col")
    blocks, pairs, side = intersections.shape
    width = vectors.shape[1]
    points, slots_dev = coarse.shape[:2]
    lay = Layout(rows, cols, blocks, pairs, side, width, points, slots_dev, tile_codes.shape[1], 4)
    if lay.groups * lay.unroll * side * side * 2 > 16 * mib:
        lay = Layout(rows, cols, blocks, pairs, side, width, points, slots_dev, tile_codes.shape[1], 1)
    near = lay.near

    def move(array, row_step, col_step):
        pairs_list = [
            (r * cols + c, (r ^ row_step) * cols + (c ^ col_step)) for r in range(rows) for c in range(cols)
        ]
        return lax.ppermute(array, axes, pairs_list)

    def along(array, step):
        return move(array, 2 * step, 0)

    def to_core(array):
        return move(array, 1, 0)

    def in_plane(array):
        return [array] + [move(array, 0, d) for d in range(1, cols)]

    start = vectors.reshape(blocks, side, width)
    energy = energies.reshape(blocks, side, 1)
    two_owners = lay.owners == 2
    ids = jnp.stack([row_id // 2, row_id % 2, col_id]).astype(jnp.int32)
    listed = jnp.concatenate([tile_codes, tile_count[:, None]], axis=1)
    n_listed = listed.shape[1]
    digits = jnp.concatenate([listed[0] >> 8, listed[0] & 255]).astype(jnp.bfloat16)
    depth = 16 * -(-2 * n_listed // (16 * width * blocks))
    digits = jnp.pad(digits, (0, blocks * depth * width - 2 * n_listed)).reshape(blocks, depth, width)
    joined = jnp.concatenate([intersections, start.astype(jnp.bfloat16), digits], axis=1)

    inputs = in_plane(joined)
    partner = [along(joined, near)] if two_owners else []
    near_coarse = [along(coarse, e) for e in range(1, near)]
    held = (partner, inputs, near_coarse, joined)
    partner, inputs, near_coarse, late_joined = lax.optimization_barrier(held)
    if two_owners:
        sent = partner[0][:, pairs + side :].reshape(-1)[: 2 * n_listed].astype(jnp.int32)
        listed = jnp.concatenate([listed, ((sent[:n_listed] << 8) + sent[n_listed:])[None]], axis=0)
    plan = make_plan(lay, ids, listed, fine_coarse, coarse_slot)
    for part in partner:
        inputs = inputs + in_plane(part)
    turned = turn_own(lay, late_joined)
    blocks_coarse = []
    for part in [coarse] + near_coarse:
        blocks_coarse += [part, to_core(part)]
    turned, blocks_coarse = lax.optimization_barrier((turned, blocks_coarse))
    lines = [along(turned, d) for d in lay.line_steps()]
    for part in partner:
        turned = turn_both(lay, part, turned)
    projected = [
        project(lay, g, plan, inputs[g * cols : (g + 1) * cols], blocks_coarse) for g in range(lay.owners)
    ]
    lines, turned, projected = lax.optimization_barrier((lines, turned, projected))
    lefts = [turned] + lines
    lefts = lefts + [to_core(part) for part in lefts]
    own_sum, other_sum, tiles = make_tiles(lay, plan, inputs, lefts, projected)

    def over_core(own_part, other_part):
        return (own_part + to_core(other_part).astype(jnp.float32)).reshape(lay.places, blocks, side, width)

    def shifted_part(field):
        return energy * field - spectrum_center * field

    merged = over_core(own_sum, other_sum)
    if two_owners:
        sums = jnp.stack([merged[0] + shifted_part(start), merged[near]])
        for e in range(1, near):
            sent = jnp.stack([merged[e], merged[e ^ near]]).astype(jnp.bfloat16)
            sums = sums + along(sent, e).astype(jnp.float32)
        sums = sums + along(sums.astype(jnp.bfloat16), near)[::-1].astype(jnp.float32)
    else:
        sums = merged + shifted_part(start)[None]

    firsts = sums / spectrum_half
    first = firsts[0]
    own_sum, other_sum = apply_tiles(lay, plan, tiles, in_plane(firsts.astype(jnp.bfloat16)))
    merged = over_core(own_sum, other_sum)
    last = merged[0]
    for d in range(1, lay.places):
        last = last + along(merged[d].astype(jnp.bfloat16), d).astype(jnp.float32)
    second = 2.0 * ((shifted_part(first) + last) / spectrum_half) - start
    return first.reshape(vectors.shape), second.reshape(vectors.shape)


def solution(mesh):
    in_specs = (
        P(axes, None),
        P(axes),
        P(axes, None, None),
        P("col", "row", None, None),
        P(),
        P(),
        P(axes, None),
        P(axes),
    )
    out_specs = (P(axes, None), P(axes, None))
    return jax.shard_map(
        on_device, mesh=mesh, in_specs=in_specs, out_specs=out_specs, check_vma=False
    )
```

```python
import functools

import jax
import jax.numpy as jnp
from jax import lax
from jax.experimental import pallas as pl
from jax.experimental.pallas import tpu as pltpu
from jax.sharding import PartitionSpec as P

spectrum_center = 2.0
spectrum_half = 3.0
axes = ("row", "col")
chunk_groups = 8
mib = 1 << 20


class Layout:
    def __init__(self, rows, cols, blocks, pairs, side, width, points, slots_dev, tile_max, unroll):
        self.rows, self.cols, self.blocks = rows, cols, blocks
        self.pairs, self.side, self.width = pairs, side, width
        self.points, self.slots_dev, self.tile_max = points, slots_dev, tile_max
        self.places = rows // 2
        self.near = max(self.places // 2, 1)
        self.owners = 2 if self.places > 1 else 1
        self.spread = cols * blocks
        self.inputs = self.owners * self.spread
        self.outputs = rows * blocks
        self.slots = 2 * self.near * slots_dev
        self.unroll = unroll
        self.vmem = 60 * mib
        most = self.owners * tile_max + self.inputs * (unroll - 1) + unroll
        self.groups = -(-most // (unroll * chunk_groups)) * chunk_groups

    def line_steps(self):
        return [d for d in range(1, self.places) if d != self.near]


def plan_kernel(lay, ids, listed, fine, stored, slot_of, valid, sizes, group_input, entries, fill):
    place, core, col = ids[0], ids[1], ids[2]
    half = lax.div(place, lay.near)
    blank = lay.outputs * lay.points

    for owner in range(lay.owners):

        def examine(i, found):
            p = owner * lay.spread + i
            from_col = lax.bitwise_xor(lax.div(i, lay.blocks), col)
            from_place = lax.bitwise_xor(place, owner * lay.near)
            block = ((from_place * 2 + core) * lay.cols + from_col) * lay.blocks + lax.rem(i, lay.blocks)
            position = stored[fine[block]]
            at_row = lax.div(position, lay.slots_dev)
            at_place, at_core = lax.div(at_row, 2), lax.rem(at_row, 2)
            slot = (lax.bitwise_xor(at_place, place) * 2 + lax.bitwise_xor(at_core, core)) * lay.slots_dev
            slot = slot + lax.rem(position, lay.slots_dev)
            here = lax.div(at_place, lay.near) == half
            slot_of[p] = jnp.where(here, slot, -1)
            valid[owner * (lay.spread + 1) + found] = i
            fill[p] = 0
            return found + here.astype(jnp.int32)

        sizes[1 + owner] = lax.fori_loop(0, lay.spread, examine, 0)

    def input_of(owner, code):
        j = lax.rem(code, lay.spread)
        from_col = lax.bitwise_xor(lax.div(j, lay.blocks), col)
        return owner * lay.spread + from_col * lay.blocks + lax.rem(j, lay.blocks)

    for owner in range(lay.owners):

        def count(i, carry):
            p = input_of(owner, listed[owner, i])
            fill[p] = fill[p] + 1
            return carry

        lax.fori_loop(0, listed[owner, lay.tile_max], count, 0)

    group_input[0] = 0

    def place_groups(p, start):
        used = jnp.where(slot_of[p] >= 0, fill[p], 0)
        fill[p] = start * lay.unroll
        end = start + lax.div(used + (lay.unroll - 1), lay.unroll)

        def name(group, carry):
            group_input[group] = p
            return carry

        lax.fori_loop(start, end, name, 0)
        return end

    total = 1
    for owner in range(lay.owners):
        if owner > 0:
            sizes[lay.owners + owner] = total
        total = lax.fori_loop(owner * lay.spread, (owner + 1) * lay.spread, place_groups, total)
    sizes[0] = total

    def clear(i, carry):
        entries[i] = blank
        return carry

    lax.fori_loop(0, total * lay.unroll, clear, 0)

    for owner in range(lay.owners):

        def put(i, carry):
            code = listed[owner, i]
            p = input_of(owner, code)

            @pl.when(slot_of[p] >= 0)
            def _():
                out = lax.div(code, lay.spread)
                at_row = lax.div(out, lay.blocks)
                within = lax.rem(out, lay.blocks)
                far = lax.bitwise_xor(lax.div(at_row, 2), place)
                other = lax.bitwise_xor(lax.rem(at_row, 2), core)
                q = (other * lay.places + far) * lay.blocks + within
                a = fine[(at_row * lay.cols + col) * lay.blocks + within] - col * lay.points
                spot = fill[p]
                entries[spot] = q * lay.points + a
                fill[p] = spot + 1

            return carry

        lax.fori_loop(0, listed[owner, lay.tile_max], put, 0)


def make_plan(lay, ids, listed, fine, stored):
    smem = pl.BlockSpec(memory_space=pltpu.SMEM)
    lengths = (
        lay.inputs,
        lay.owners * (lay.spread + 1),
        2 * lay.owners,
        lay.groups,
        lay.groups * lay.unroll,
    )
    return pl.pallas_call(
        functools.partial(plan_kernel, lay),
        out_shape=tuple(jax.ShapeDtypeStruct((n,), jnp.int32) for n in lengths),
        in_specs=[smem] * 4,
        out_specs=(smem,) * 5,
        scratch_shapes=[pltpu.SMEM((lay.inputs,), jnp.int32)],
        cost_estimate=pl.CostEstimate(flops=0, bytes_accessed=20_000_000, transcendentals=0),
    )(ids, listed, fine, stored)


def add_products(lay, group, group_input, entries, tiles, rounded, total):
    held = tiles[pl.ds(group * lay.unroll, lay.unroll)].reshape(lay.unroll * lay.side, lay.side)
    products = jnp.dot(held, rounded[group_input[group]], preferred_element_type=jnp.float32)
    for i in range(lay.unroll):
        q = lax.div(entries[group * lay.unroll + i], lay.points)
        total[q] = total[q] + products[i * lay.side : (i + 1) * lay.side]


def turn_own_kernel(lay, given, turned):
    for t in range(lay.blocks):
        turned[t] = given[t, 0 : lay.pairs, :].T


def turn_own(lay, joined):
    vmem = pl.BlockSpec(memory_space=pltpu.VMEM)
    return pl.pallas_call(
        functools.partial(turn_own_kernel, lay),
        out_shape=jax.ShapeDtypeStruct((lay.blocks, lay.side, lay.pairs), jnp.bfloat16),
        in_specs=[vmem],
        out_specs=vmem,
        compiler_params=pltpu.CompilerParams(vmem_limit_bytes=16 * mib),
        cost_estimate=pl.CostEstimate(flops=1_000_000, bytes_accessed=5_000_000, transcendentals=0),
    )(joined)


def turn_both_kernel(lay, given, own, out):
    out[0 : lay.blocks] = own[...]
    for t in range(lay.blocks):
        out[lay.blocks + t] = given[t, 0 : lay.pairs, :].T


def turn_both(lay, partner, own):
    vmem = pl.BlockSpec(memory_space=pltpu.VMEM)
    return pl.pallas_call(
        functools.partial(turn_both_kernel, lay),
        out_shape=jax.ShapeDtypeStruct((2 * lay.blocks, lay.side, lay.pairs), jnp.bfloat16),
        in_specs=[vmem] * 2,
        out_specs=vmem,
        compiler_params=pltpu.CompilerParams(vmem_limit_bytes=16 * mib),
        cost_estimate=pl.CostEstimate(flops=1_000_000, bytes_accessed=5_000_000, transcendentals=0),
    )(partner, own)


def project_kernel(lay, owner, slot_of, valid, sizes, *refs):
    refs = list(refs)
    given_in = [refs.pop(0) for _ in range(lay.cols)]
    given_coarse = [refs.pop(0) for _ in range(2 * lay.near)]
    out, right, blocks, projected, sems, out_sems = refs
    copies = []

    def fetch(source, target):
        copies.append(pltpu.make_async_copy(source, target, sems.at[len(copies)]))
        copies[-1].start()

    for i in range(2 * lay.near):
        for a in range(lay.points):
            fetch(given_coarse[i].at[a], blocks.at[a, pl.ds(i * lay.slots_dev, lay.slots_dev)])
    for i in range(lay.cols):
        fetch(given_in[i].at[:, pl.ds(0, lay.pairs)], right.at[pl.ds(i * lay.blocks, lay.blocks)])
    for copy in copies:
        copy.wait()
    found = sizes[1 + owner]

    def visit(step, carry):
        for lane in range(2):
            i = valid[owner * (lay.spread + 1) + jnp.minimum(2 * step + lane, found - 1)]
            slot = slot_of[owner * lay.spread + i]
            for a in range(lay.points):
                projected[i, :, a * lay.side : (a + 1) * lay.side] = jnp.dot(
                    blocks[a, slot], right[i], preferred_element_type=jnp.float32
                ).astype(jnp.bfloat16)
        return carry

    lax.fori_loop(0, lax.div(found + 1, 2), visit, 0)

    def store(i):
        return pltpu.make_async_copy(projected.at[i], out.at[i], out_sems.at[i])

    for i in range(lay.spread):

        @pl.when(slot_of[owner * lay.spread + i] >= 0)
        def _():
            store(i).start()

    for i in range(lay.spread):

        @pl.when(slot_of[owner * lay.spread + i] >= 0)
        def _():
            store(i).wait()


def project(lay, owner, plan, inputs, coarse):
    smem = pl.BlockSpec(memory_space=pltpu.SMEM)
    hbm = pl.BlockSpec(memory_space=pl.ANY)
    shape = (lay.spread, lay.pairs, lay.points * lay.side)
    return pl.pallas_call(
        functools.partial(project_kernel, lay, owner),
        out_shape=jax.ShapeDtypeStruct(shape, jnp.bfloat16),
        in_specs=[smem] * 3 + [hbm] * (len(inputs) + len(coarse)),
        out_specs=hbm,
        scratch_shapes=[
            pltpu.VMEM((lay.spread, lay.pairs, lay.side), jnp.bfloat16),
            pltpu.VMEM((lay.points, lay.slots, lay.pairs, lay.pairs), jnp.bfloat16),
            pltpu.VMEM(shape, jnp.bfloat16),
            pltpu.SemaphoreType.DMA((len(inputs) + len(coarse) * lay.points,)),
            pltpu.SemaphoreType.DMA((lay.spread,)),
        ],
        compiler_params=pltpu.CompilerParams(vmem_limit_bytes=lay.vmem),
        cost_estimate=pl.CostEstimate(flops=1_000_000_000, bytes_accessed=16_000_000, transcendentals=0),
    )(*plan[:3], *inputs, *coarse)


def tiles_kernel(lay, slot_of, sizes, group_input, entries, *refs):
    lines = lay.line_steps()
    refs = list(refs)
    given_in = [refs.pop(0) for _ in range(lay.owners * lay.cols)]
    given_out = [refs.pop(0) for _ in range(2 * (1 + len(lines)))]
    given_projected = [refs.pop(0) for _ in range(lay.owners)]
    own_sum, other_sum, tiles_out = refs[:3]
    left, projected, rounded, tiles, total, sent, sems, sum_sems, in_sems, out_sems = refs[3:]
    copies = []

    def fetch(source, target):
        copies.append(pltpu.make_async_copy(source, target, sems.at[len(copies)]))
        copies[-1].start()

    def load(p):
        source = given_projected[p // lay.spread].at[p % lay.spread]
        return pltpu.make_async_copy(source, projected.at[p], in_sems.at[p])

    for k in range(2):
        held = given_out[k * (1 + len(lines)) :]
        for g in range(lay.owners):
            spot = (k * lay.places + g * lay.near) * lay.blocks
            fetch(held[0].at[pl.ds(g * lay.blocks, lay.blocks)], left.at[pl.ds(spot, lay.blocks)])
        for i, d in enumerate(lines):
            spot = (k * lay.places + d) * lay.blocks
            fetch(held[1 + i], left.at[pl.ds(spot, lay.blocks)])
    for i, ref in enumerate(given_in):
        part = pl.ds(i * lay.blocks, lay.blocks)
        fetch(ref.at[:, pl.ds(lay.pairs, lay.side)], rounded.at[part])
    for p in range(lay.inputs):

        @pl.when(slot_of[p] >= 0)
        def _():
            load(p).start()

    total[...] = jnp.zeros_like(total)
    for copy in copies:
        copy.wait()
    used = sizes[0]

    for owner in range(lay.owners):
        for p in range(owner * lay.spread, (owner + 1) * lay.spread):

            @pl.when(slot_of[p] >= 0)
            def _():
                load(p).wait()

        def group_step(group, carry):
            block = projected[group_input[group]]
            numbers = [entries[group * lay.unroll + i] for i in range(lay.unroll)]
            places = [jnp.minimum(lax.div(n, lay.points), lay.outputs - 1) for n in numbers]
            lefts = jnp.concatenate([left[q] for q in places], axis=0)
            both = jnp.dot(lefts, block, preferred_element_type=jnp.float32)
            for i in range(lay.unroll):
                mine = both[i * lay.side : (i + 1) * lay.side]
                tile = mine[:, : lay.side]
                for b in range(1, lay.points):
                    at_b = mine[:, b * lay.side : (b + 1) * lay.side]
                    tile = jnp.where(lax.rem(numbers[i], lay.points) == b, at_b, tile)
                tiles[group * lay.unroll + i] = tile.astype(jnp.bfloat16)
            add_products(lay, group - 1, group_input, entries, tiles, rounded, total)
            return carry

        first = 1 if owner == 0 else sizes[lay.owners + owner]
        last = used if owner == lay.owners - 1 else sizes[lay.owners + owner + 1]
        lax.fori_loop(first, last, group_step, 0)

    span = chunk_groups * lay.unroll

    def store(chunk):
        part = pl.ds(chunk * span, span)
        return pltpu.make_async_copy(tiles.at[part], tiles_out.at[part], out_sems.at[chunk])

    for chunk in range(lay.groups // chunk_groups):

        @pl.when(used > chunk * chunk_groups)
        def _():
            store(chunk).start()

    add_products(lay, used - 1, group_input, entries, tiles, rounded, total)
    give_sums(lay, total, sent, own_sum, other_sum, sum_sems)
    for chunk in range(lay.groups // chunk_groups):

        @pl.when(used > chunk * chunk_groups)
        def _():
            store(chunk).wait()


def give_sums(lay, total, sent, own_sum, other_sum, sems):
    own = lay.places * lay.blocks
    for_own = pltpu.make_async_copy(total.at[pl.ds(0, own)], own_sum, sems.at[0])
    for_own.start()
    sent[...] = total[own : 2 * own].astype(jnp.bfloat16)
    for_other = pltpu.make_async_copy(sent, other_sum, sems.at[1])
    for_other.start()
    for_own.wait()
    for_other.wait()


def make_tiles(lay, plan, inputs, outputs, projected):
    smem = pl.BlockSpec(memory_space=pltpu.SMEM)
    hbm = pl.BlockSpec(memory_space=pl.ANY)
    own = lay.places * lay.blocks
    sums = jax.ShapeDtypeStruct((own, lay.side, lay.width), jnp.float32)
    sent = jax.ShapeDtypeStruct((own, lay.side, lay.width), jnp.bfloat16)
    tiles = (lay.groups * lay.unroll, lay.side, lay.side)
    return pl.pallas_call(
        functools.partial(tiles_kernel, lay),
        out_shape=(sums, sent, jax.ShapeDtypeStruct(tiles, jnp.bfloat16)),
        in_specs=[smem] * 4 + [hbm] * (len(inputs) + len(outputs) + len(projected)),
        out_specs=(hbm,) * 3,
        scratch_shapes=[
            pltpu.VMEM((lay.outputs, lay.side, lay.pairs), jnp.bfloat16),
            pltpu.VMEM((lay.inputs, lay.pairs, lay.points * lay.side), jnp.bfloat16),
            pltpu.VMEM((lay.inputs, lay.side, lay.width), jnp.bfloat16),
            pltpu.VMEM(tiles, jnp.bfloat16),
            pltpu.VMEM((lay.outputs + 1, lay.side, lay.width), jnp.float32),
            pltpu.VMEM((own, lay.side, lay.width), jnp.bfloat16),
            pltpu.SemaphoreType.DMA((len(inputs) + 2 * lay.places,)),
            pltpu.SemaphoreType.DMA((2,)),
            pltpu.SemaphoreType.DMA((lay.inputs,)),
            pltpu.SemaphoreType.DMA((lay.groups // chunk_groups,)),
        ],
        compiler_params=pltpu.CompilerParams(vmem_limit_bytes=lay.vmem),
        cost_estimate=pl.CostEstimate(flops=4_000_000_000, bytes_accessed=30_000_000, transcendentals=0),
    )(plan[0], *plan[2:], *inputs, *outputs, *projected)


def apply_kernel(lay, sizes, group_input, entries, tiles_in, *refs):
    given_vec = refs[: lay.cols]
    own_sum, other_sum = refs[lay.cols : lay.cols + 2]
    rounded, tiles, total, sent, sems, sum_sems, out_sems = refs[lay.cols + 2 :]
    used = sizes[0]
    span = chunk_groups * lay.unroll

    def load(chunk):
        part = pl.ds(chunk * span, span)
        return pltpu.make_async_copy(tiles_in.at[part], tiles.at[part], out_sems.at[chunk])

    for chunk in range(lay.groups // chunk_groups):

        @pl.when(used > chunk * chunk_groups)
        def _():
            load(chunk).start()

    copies = []
    for d in range(lay.cols):
        for g in range(lay.owners):
            target = rounded.at[pl.ds((g * lay.cols + d) * lay.blocks, lay.blocks)]
            copies.append(pltpu.make_async_copy(given_vec[d].at[g], target, sems.at[len(copies)]))
            copies[-1].start()
    total[...] = jnp.zeros_like(total)
    for copy in copies:
        copy.wait()
    for chunk in range(lay.groups // chunk_groups):

        @pl.when(used > chunk * chunk_groups)
        def _():
            load(chunk).wait()

    def group_step(group, carry):
        add_products(lay, group, group_input, entries, tiles, rounded, total)
        return carry

    lax.fori_loop(1, used, group_step, 0)
    give_sums(lay, total, sent, own_sum, other_sum, sum_sems)


def apply_tiles(lay, plan, tiles, rounded):
    smem = pl.BlockSpec(memory_space=pltpu.SMEM)
    hbm = pl.BlockSpec(memory_space=pl.ANY)
    own = lay.places * lay.blocks
    sums = jax.ShapeDtypeStruct((own, lay.side, lay.width), jnp.float32)
    sent = jax.ShapeDtypeStruct((own, lay.side, lay.width), jnp.bfloat16)
    return pl.pallas_call(
        functools.partial(apply_kernel, lay),
        out_shape=(sums, sent),
        in_specs=[smem] * 3 + [hbm] * (1 + len(rounded)),
        out_specs=(hbm, hbm),
        scratch_shapes=[
            pltpu.VMEM((lay.inputs, lay.side, lay.width), jnp.bfloat16),
            pltpu.VMEM(tiles.shape, jnp.bfloat16),
            pltpu.VMEM((lay.outputs + 1, lay.side, lay.width), jnp.float32),
            pltpu.VMEM((own, lay.side, lay.width), jnp.bfloat16),
            pltpu.SemaphoreType.DMA((len(rounded) * lay.owners,)),
            pltpu.SemaphoreType.DMA((2,)),
            pltpu.SemaphoreType.DMA((lay.groups // chunk_groups,)),
        ],
        compiler_params=pltpu.CompilerParams(vmem_limit_bytes=lay.vmem),
        cost_estimate=pl.CostEstimate(flops=400_000_000, bytes_accessed=4_000_000, transcendentals=0),
    )(*plan[2:], tiles, *rounded)


def on_device(
    vectors, energies, intersections, coarse, fine_coarse, coarse_slot, tile_codes, tile_count
):
    rows = lax.axis_size("row")
    cols = lax.axis_size("col")
    row_id = lax.axis_index("row")
    col_id = lax.axis_index("col")
    blocks, pairs, side = intersections.shape
    width = vectors.shape[1]
    points, slots_dev = coarse.shape[:2]
    lay = Layout(rows, cols, blocks, pairs, side, width, points, slots_dev, tile_codes.shape[1], 4)
    if lay.groups * lay.unroll * side * side * 2 > 16 * mib:
        lay = Layout(rows, cols, blocks, pairs, side, width, points, slots_dev, tile_codes.shape[1], 1)
    near = lay.near

    def move(array, row_step, col_step):
        pairs_list = [
            (r * cols + c, (r ^ row_step) * cols + (c ^ col_step)) for r in range(rows) for c in range(cols)
        ]
        return lax.ppermute(array, axes, pairs_list)

    def along(array, step):
        return move(array, 2 * step, 0)

    def to_core(array):
        return move(array, 1, 0)

    def in_plane(array):
        return [array] + [move(array, 0, d) for d in range(1, cols)]

    start = vectors.reshape(blocks, side, width)
    energy = energies.reshape(blocks, side, 1)
    two_owners = lay.owners == 2
    ids = jnp.stack([row_id // 2, row_id % 2, col_id]).astype(jnp.int32)
    listed = jnp.concatenate([tile_codes, tile_count[:, None]], axis=1)
    n_listed = listed.shape[1]
    digits = jnp.concatenate([listed[0] >> 8, listed[0] & 255]).astype(jnp.bfloat16)
    depth = 16 * -(-2 * n_listed // (16 * width * blocks))
    digits = jnp.pad(digits, (0, blocks * depth * width - 2 * n_listed)).reshape(blocks, depth, width)
    joined = jnp.concatenate([intersections, start.astype(jnp.bfloat16), digits], axis=1)

    inputs = in_plane(joined)
    partner = [along(joined, near)] if two_owners else []
    near_coarse = [along(coarse, e) for e in range(1, near)]
    held = (partner, inputs, near_coarse, joined)
    partner, inputs, near_coarse, late_joined = lax.optimization_barrier(held)
    if two_owners:
        sent = partner[0][:, pairs + side :].reshape(-1)[: 2 * n_listed].astype(jnp.int32)
        listed = jnp.concatenate([listed, ((sent[:n_listed] << 8) + sent[n_listed:])[None]], axis=0)
    plan = make_plan(lay, ids, listed, fine_coarse, coarse_slot)
    for part in partner:
        inputs = inputs + in_plane(part)
    turned = turn_own(lay, late_joined)
    blocks_coarse = []
    for part in [coarse] + near_coarse:
        blocks_coarse += [part, to_core(part)]
    turned, blocks_coarse = lax.optimization_barrier((turned, blocks_coarse))
    lines = [along(turned, d) for d in lay.line_steps()]
    for part in partner:
        turned = turn_both(lay, part, turned)
    projected = [project(lay, 0, plan, inputs[:cols], blocks_coarse)]
    held = (inputs, lines, turned, projected)
    inputs, lines, turned, projected = lax.optimization_barrier(held)
    lefts = [turned] + lines
    lefts = lefts + [to_core(part) for part in lefts]
    if two_owners:
        projected.append(project(lay, 1, plan, inputs[cols:], blocks_coarse))
    own_sum, other_sum, tiles = make_tiles(lay, plan, inputs, lefts, projected)

    def over_core(own_part, other_part):
        return (own_part + to_core(other_part).astype(jnp.float32)).reshape(lay.places, blocks, side, width)

    def shifted_part(field):
        return energy * field - spectrum_center * field

    merged = over_core(own_sum, other_sum)
    if two_owners:
        sums = jnp.stack([merged[0] + shifted_part(start), merged[near]])
        for e in range(1, near):
            sent = jnp.stack([merged[e], merged[e ^ near]]).astype(jnp.bfloat16)
            sums = sums + along(sent, e).astype(jnp.float32)
        sums = sums + along(sums.astype(jnp.bfloat16), near)[::-1].astype(jnp.float32)
    else:
        sums = merged + shifted_part(start)[None]

    firsts = sums / spectrum_half
    first = firsts[0]
    own_sum, other_sum = apply_tiles(lay, plan, tiles, in_plane(firsts.astype(jnp.bfloat16)))
    merged = over_core(own_sum, other_sum)
    last = merged[0]
    for d in range(1, lay.places):
        last = last + along(merged[d].astype(jnp.bfloat16), d).astype(jnp.float32)
    second = 2.0 * ((shifted_part(first) + last) / spectrum_half) - start
    return first.reshape(vectors.shape), second.reshape(vectors.shape)


def solution(mesh):
    in_specs = (
        P(axes, None),
        P(axes),
        P(axes, None, None),
        P("col", "row", None, None),
        P(),
        P(),
        P(axes, None),
        P(axes),
    )
    out_specs = (P(axes, None), P(axes, None))
    return jax.shard_map(
        on_device, mesh=mesh, in_specs=in_specs, out_specs=out_specs, check_vma=False
    )
```

```python
import functools

import jax
import jax.numpy as jnp
from jax import lax
from jax.experimental import pallas as pl
from jax.experimental.pallas import tpu as pltpu
from jax.sharding import PartitionSpec as P

spectrum_center = 2.0
spectrum_half = 3.0
axes = ("row", "col")
chunk_groups = 8
mib = 1 << 20


class Layout:
    def __init__(self, rows, cols, blocks, pairs, side, width, points, slots_dev, tile_max, unroll):
        self.rows, self.cols, self.blocks = rows, cols, blocks
        self.pairs, self.side, self.width = pairs, side, width
        self.points, self.slots_dev, self.tile_max = points, slots_dev, tile_max
        self.places = rows // 2
        self.near = max(self.places // 2, 1)
        self.owners = 2 if self.places > 1 else 1
        self.spread = cols * blocks
        self.inputs = self.owners * self.spread
        self.outputs = rows * blocks
        self.slots = 2 * self.near * slots_dev
        self.unroll = unroll
        self.vmem = 60 * mib
        self.vmem_sums = (50 if unroll > 1 else 60) * mib
        most = self.owners * tile_max + self.inputs * (unroll - 1) + unroll
        self.groups = -(-most // (unroll * chunk_groups)) * chunk_groups

    def line_steps(self):
        return [d for d in range(1, self.places) if d != self.near]


def plan_kernel(lay, ids, listed, fine, stored, slot_of, valid, sizes, group_input, entries, fill):
    place, core, col = ids[0], ids[1], ids[2]
    half = lax.div(place, lay.near)
    blank = lay.outputs * lay.points

    for owner in range(lay.owners):

        def examine(i, found):
            p = owner * lay.spread + i
            from_col = lax.bitwise_xor(lax.div(i, lay.blocks), col)
            from_place = lax.bitwise_xor(place, owner * lay.near)
            block = ((from_place * 2 + core) * lay.cols + from_col) * lay.blocks + lax.rem(i, lay.blocks)
            position = stored[fine[block]]
            at_row = lax.div(position, lay.slots_dev)
            at_place, at_core = lax.div(at_row, 2), lax.rem(at_row, 2)
            slot = (lax.bitwise_xor(at_place, place) * 2 + lax.bitwise_xor(at_core, core)) * lay.slots_dev
            slot = slot + lax.rem(position, lay.slots_dev)
            here = lax.div(at_place, lay.near) == half
            slot_of[p] = jnp.where(here, slot, -1)
            valid[owner * (lay.spread + 1) + found] = i
            fill[p] = 0
            return found + here.astype(jnp.int32)

        sizes[1 + owner] = lax.fori_loop(0, lay.spread, examine, 0)

    def input_of(owner, code):
        j = lax.rem(code, lay.spread)
        from_col = lax.bitwise_xor(lax.div(j, lay.blocks), col)
        return owner * lay.spread + from_col * lay.blocks + lax.rem(j, lay.blocks)

    for owner in range(lay.owners):

        def count(i, carry):
            p = input_of(owner, listed[owner, i])
            fill[p] = fill[p] + 1
            return carry

        lax.fori_loop(0, listed[owner, lay.tile_max], count, 0)

    group_input[0] = 0

    def place_groups(p, start):
        used = jnp.where(slot_of[p] >= 0, fill[p], 0)
        fill[p] = start * lay.unroll
        end = start + lax.div(used + (lay.unroll - 1), lay.unroll)

        def name(group, carry):
            group_input[group] = p
            return carry

        lax.fori_loop(start, end, name, 0)
        return end

    total = 1
    for owner in range(lay.owners):
        if owner > 0:
            sizes[lay.owners + owner] = total
        total = lax.fori_loop(owner * lay.spread, (owner + 1) * lay.spread, place_groups, total)
    sizes[0] = total

    def clear(i, carry):
        entries[i] = blank
        return carry

    lax.fori_loop(0, total * lay.unroll, clear, 0)

    for owner in range(lay.owners):

        def put(i, carry):
            code = listed[owner, i]
            p = input_of(owner, code)

            @pl.when(slot_of[p] >= 0)
            def _():
                out = lax.div(code, lay.spread)
                at_row = lax.div(out, lay.blocks)
                within = lax.rem(out, lay.blocks)
                far = lax.bitwise_xor(lax.div(at_row, 2), place)
                other = lax.bitwise_xor(lax.rem(at_row, 2), core)
                q = (other * lay.places + far) * lay.blocks + within
                a = fine[(at_row * lay.cols + col) * lay.blocks + within] - col * lay.points
                spot = fill[p]
                entries[spot] = q * lay.points + a
                fill[p] = spot + 1

            return carry

        lax.fori_loop(0, listed[owner, lay.tile_max], put, 0)


def make_plan(lay, ids, listed, fine, stored):
    smem = pl.BlockSpec(memory_space=pltpu.SMEM)
    lengths = (
        lay.inputs,
        lay.owners * (lay.spread + 1),
        2 * lay.owners,
        lay.groups,
        lay.groups * lay.unroll,
    )
    return pl.pallas_call(
        functools.partial(plan_kernel, lay),
        out_shape=tuple(jax.ShapeDtypeStruct((n,), jnp.int32) for n in lengths),
        in_specs=[smem] * 4,
        out_specs=(smem,) * 5,
        scratch_shapes=[pltpu.SMEM((lay.inputs,), jnp.int32)],
        cost_estimate=pl.CostEstimate(flops=0, bytes_accessed=20_000_000, transcendentals=0),
    )(ids, listed, fine, stored)


def add_products(lay, group, group_input, entries, tiles, rounded, total):
    held = tiles[pl.ds(group * lay.unroll, lay.unroll)].reshape(lay.unroll * lay.side, lay.side)
    products = jnp.dot(held, rounded[group_input[group]], preferred_element_type=jnp.float32)
    for i in range(lay.unroll):
        q = lax.div(entries[group * lay.unroll + i], lay.points)
        total[q] = total[q] + products[i * lay.side : (i + 1) * lay.side]


def turn_own_kernel(lay, given, turned):
    for t in range(lay.blocks):
        turned[t] = given[t, 0 : lay.pairs, :].T


def turn_own(lay, joined):
    vmem = pl.BlockSpec(memory_space=pltpu.VMEM)
    return pl.pallas_call(
        functools.partial(turn_own_kernel, lay),
        out_shape=jax.ShapeDtypeStruct((lay.blocks, lay.side, lay.pairs), jnp.bfloat16),
        in_specs=[vmem],
        out_specs=vmem,
        compiler_params=pltpu.CompilerParams(vmem_limit_bytes=16 * mib),
        cost_estimate=pl.CostEstimate(flops=1_000_000, bytes_accessed=5_000_000, transcendentals=0),
    )(joined)


def turn_both_kernel(lay, given, own, out):
    out[0 : lay.blocks] = own[...]
    for t in range(lay.blocks):
        out[lay.blocks + t] = given[t, 0 : lay.pairs, :].T


def turn_both(lay, partner, own):
    vmem = pl.BlockSpec(memory_space=pltpu.VMEM)
    return pl.pallas_call(
        functools.partial(turn_both_kernel, lay),
        out_shape=jax.ShapeDtypeStruct((2 * lay.blocks, lay.side, lay.pairs), jnp.bfloat16),
        in_specs=[vmem] * 2,
        out_specs=vmem,
        compiler_params=pltpu.CompilerParams(vmem_limit_bytes=16 * mib),
        cost_estimate=pl.CostEstimate(flops=1_000_000, bytes_accessed=5_000_000, transcendentals=0),
    )(partner, own)


def project_kernel(lay, owner, slot_of, valid, sizes, *refs):
    refs = list(refs)
    given_in = [refs.pop(0) for _ in range(lay.cols)]
    given_coarse = [refs.pop(0) for _ in range(2 * lay.near)]
    out, right, blocks, projected, sems, out_sems = refs
    copies = []

    def fetch(source, target):
        copies.append(pltpu.make_async_copy(source, target, sems.at[len(copies)]))
        copies[-1].start()

    for i in range(2 * lay.near):
        for a in range(lay.points):
            fetch(given_coarse[i].at[a], blocks.at[a, pl.ds(i * lay.slots_dev, lay.slots_dev)])
    for i in range(lay.cols):
        fetch(given_in[i].at[:, pl.ds(0, lay.pairs)], right.at[pl.ds(i * lay.blocks, lay.blocks)])
    for copy in copies:
        copy.wait()
    found = sizes[1 + owner]

    def visit(step, carry):
        for lane in range(2):
            i = valid[owner * (lay.spread + 1) + jnp.minimum(2 * step + lane, found - 1)]
            slot = slot_of[owner * lay.spread + i]
            for a in range(lay.points):
                projected[i, :, a * lay.side : (a + 1) * lay.side] = jnp.dot(
                    blocks[a, slot], right[i], preferred_element_type=jnp.float32
                ).astype(jnp.bfloat16)
        return carry

    lax.fori_loop(0, lax.div(found + 1, 2), visit, 0)

    def store(i):
        return pltpu.make_async_copy(projected.at[i], out.at[i], out_sems.at[i])

    for i in range(lay.spread):

        @pl.when(slot_of[owner * lay.spread + i] >= 0)
        def _():
            store(i).start()

    for i in range(lay.spread):

        @pl.when(slot_of[owner * lay.spread + i] >= 0)
        def _():
            store(i).wait()


def project(lay, owner, plan, inputs, coarse):
    smem = pl.BlockSpec(memory_space=pltpu.SMEM)
    hbm = pl.BlockSpec(memory_space=pl.ANY)
    shape = (lay.spread, lay.pairs, lay.points * lay.side)
    return pl.pallas_call(
        functools.partial(project_kernel, lay, owner),
        out_shape=jax.ShapeDtypeStruct(shape, jnp.bfloat16),
        in_specs=[smem] * 3 + [hbm] * (len(inputs) + len(coarse)),
        out_specs=hbm,
        scratch_shapes=[
            pltpu.VMEM((lay.spread, lay.pairs, lay.side), jnp.bfloat16),
            pltpu.VMEM((lay.points, lay.slots, lay.pairs, lay.pairs), jnp.bfloat16),
            pltpu.VMEM(shape, jnp.bfloat16),
            pltpu.SemaphoreType.DMA((len(inputs) + len(coarse) * lay.points,)),
            pltpu.SemaphoreType.DMA((lay.spread,)),
        ],
        compiler_params=pltpu.CompilerParams(vmem_limit_bytes=lay.vmem),
        cost_estimate=pl.CostEstimate(flops=1_000_000_000, bytes_accessed=16_000_000, transcendentals=0),
    )(*plan[:3], *inputs, *coarse)


def tiles_kernel(lay, slot_of, sizes, group_input, entries, *refs):
    lines = lay.line_steps()
    refs = list(refs)
    given_in = [refs.pop(0) for _ in range(lay.owners * lay.cols)]
    given_out = [refs.pop(0) for _ in range(2 * (1 + len(lines)))]
    given_projected = [refs.pop(0) for _ in range(lay.owners)]
    own_sum, other_sum, tiles_out = refs[:3]
    left, projected, rounded, tiles, total, sems, in_sems, out_sems = refs[3:]
    copies = []

    def fetch(source, target):
        copies.append(pltpu.make_async_copy(source, target, sems.at[len(copies)]))
        copies[-1].start()

    def load(p):
        source = given_projected[p // lay.spread].at[p % lay.spread]
        return pltpu.make_async_copy(source, projected.at[p], in_sems.at[p])

    for k in range(2):
        held = given_out[k * (1 + len(lines)) :]
        for g in range(lay.owners):
            spot = (k * lay.places + g * lay.near) * lay.blocks
            fetch(held[0].at[pl.ds(g * lay.blocks, lay.blocks)], left.at[pl.ds(spot, lay.blocks)])
        for i, d in enumerate(lines):
            spot = (k * lay.places + d) * lay.blocks
            fetch(held[1 + i], left.at[pl.ds(spot, lay.blocks)])
    for i, ref in enumerate(given_in):
        part = pl.ds(i * lay.blocks, lay.blocks)
        fetch(ref.at[:, pl.ds(lay.pairs, lay.side)], rounded.at[part])
    for p in range(lay.inputs):

        @pl.when(slot_of[p] >= 0)
        def _():
            load(p).start()

    total[...] = jnp.zeros_like(total)
    for copy in copies:
        copy.wait()
    used = sizes[0]

    for owner in range(lay.owners):
        for p in range(owner * lay.spread, (owner + 1) * lay.spread):

            @pl.when(slot_of[p] >= 0)
            def _():
                load(p).wait()

        def group_step(group, carry):
            block = projected[group_input[group]]
            numbers = [entries[group * lay.unroll + i] for i in range(lay.unroll)]
            places = [jnp.minimum(lax.div(n, lay.points), lay.outputs - 1) for n in numbers]
            lefts = jnp.concatenate([left[q] for q in places], axis=0)
            both = jnp.dot(lefts, block, preferred_element_type=jnp.float32)
            for i in range(lay.unroll):
                mine = both[i * lay.side : (i + 1) * lay.side]
                tile = mine[:, : lay.side]
                for b in range(1, lay.points):
                    at_b = mine[:, b * lay.side : (b + 1) * lay.side]
                    tile = jnp.where(lax.rem(numbers[i], lay.points) == b, at_b, tile)
                tiles[group * lay.unroll + i] = tile.astype(jnp.bfloat16)
            add_products(lay, group - 1, group_input, entries, tiles, rounded, total)
            return carry

        first = 1 if owner == 0 else sizes[lay.owners + owner]
        last = used if owner == lay.owners - 1 else sizes[lay.owners + owner + 1]
        lax.fori_loop(first, last, group_step, 0)

    span = chunk_groups * lay.unroll

    def store(chunk):
        part = pl.ds(chunk * span, span)
        return pltpu.make_async_copy(tiles.at[part], tiles_out.at[part], out_sems.at[chunk])

    for chunk in range(lay.groups // chunk_groups):

        @pl.when(used > chunk * chunk_groups)
        def _():
            store(chunk).start()

    add_products(lay, used - 1, group_input, entries, tiles, rounded, total)
    give_sums(lay, total, own_sum, other_sum)
    for chunk in range(lay.groups // chunk_groups):

        @pl.when(used > chunk * chunk_groups)
        def _():
            store(chunk).wait()


def give_sums(lay, total, own_sum, other_sum):
    own = lay.places * lay.blocks
    own_sum[...] = total[0:own]
    other_sum[...] = total[own : 2 * own].astype(jnp.bfloat16)


def make_tiles(lay, plan, inputs, outputs, projected):
    smem = pl.BlockSpec(memory_space=pltpu.SMEM)
    hbm = pl.BlockSpec(memory_space=pl.ANY)
    vmem = pl.BlockSpec(memory_space=pltpu.VMEM)
    own = lay.places * lay.blocks
    sums = jax.ShapeDtypeStruct((own, lay.side, lay.width), jnp.float32)
    sent = jax.ShapeDtypeStruct((own, lay.side, lay.width), jnp.bfloat16)
    tiles = (lay.groups * lay.unroll, lay.side, lay.side)
    return pl.pallas_call(
        functools.partial(tiles_kernel, lay),
        out_shape=(sums, sent, jax.ShapeDtypeStruct(tiles, jnp.bfloat16)),
        in_specs=[smem] * 4 + [hbm] * (len(inputs) + len(outputs) + len(projected)),
        out_specs=(vmem, vmem, hbm),
        scratch_shapes=[
            pltpu.VMEM((lay.outputs, lay.side, lay.pairs), jnp.bfloat16),
            pltpu.VMEM((lay.inputs, lay.pairs, lay.points * lay.side), jnp.bfloat16),
            pltpu.VMEM((lay.inputs, lay.side, lay.width), jnp.bfloat16),
            pltpu.VMEM(tiles, jnp.bfloat16),
            pltpu.VMEM((lay.outputs + 1, lay.side, lay.width), jnp.float32),
            pltpu.SemaphoreType.DMA((len(inputs) + 2 * lay.places,)),
            pltpu.SemaphoreType.DMA((lay.inputs,)),
            pltpu.SemaphoreType.DMA((lay.groups // chunk_groups,)),
        ],
        compiler_params=pltpu.CompilerParams(vmem_limit_bytes=lay.vmem_sums),
        cost_estimate=pl.CostEstimate(flops=4_000_000_000, bytes_accessed=30_000_000, transcendentals=0),
    )(plan[0], *plan[2:], *inputs, *outputs, *projected)


def apply_kernel(lay, sizes, group_input, entries, tiles_in, *refs):
    given_vec = refs[: lay.cols]
    own_sum, other_sum = refs[lay.cols : lay.cols + 2]
    rounded, tiles, total, sems, out_sems = refs[lay.cols + 2 :]
    used = sizes[0]
    span = chunk_groups * lay.unroll

    def load(chunk):
        part = pl.ds(chunk * span, span)
        return pltpu.make_async_copy(tiles_in.at[part], tiles.at[part], out_sems.at[chunk])

    for chunk in range(lay.groups // chunk_groups):

        @pl.when(used > chunk * chunk_groups)
        def _():
            load(chunk).start()

    copies = []
    for d in range(lay.cols):
        for g in range(lay.owners):
            target = rounded.at[pl.ds((g * lay.cols + d) * lay.blocks, lay.blocks)]
            copies.append(pltpu.make_async_copy(given_vec[d].at[g], target, sems.at[len(copies)]))
            copies[-1].start()
    total[...] = jnp.zeros_like(total)
    for copy in copies:
        copy.wait()
    for chunk in range(lay.groups // chunk_groups):

        @pl.when(used > chunk * chunk_groups)
        def _():
            load(chunk).wait()

    def group_step(group, carry):
        add_products(lay, group, group_input, entries, tiles, rounded, total)
        return carry

    lax.fori_loop(1, used, group_step, 0)
    give_sums(lay, total, own_sum, other_sum)


def apply_tiles(lay, plan, tiles, rounded):
    smem = pl.BlockSpec(memory_space=pltpu.SMEM)
    hbm = pl.BlockSpec(memory_space=pl.ANY)
    vmem = pl.BlockSpec(memory_space=pltpu.VMEM)
    own = lay.places * lay.blocks
    sums = jax.ShapeDtypeStruct((own, lay.side, lay.width), jnp.float32)
    sent = jax.ShapeDtypeStruct((own, lay.side, lay.width), jnp.bfloat16)
    return pl.pallas_call(
        functools.partial(apply_kernel, lay),
        out_shape=(sums, sent),
        in_specs=[smem] * 3 + [hbm] * (1 + len(rounded)),
        out_specs=(vmem, vmem),
        scratch_shapes=[
            pltpu.VMEM((lay.inputs, lay.side, lay.width), jnp.bfloat16),
            pltpu.VMEM(tiles.shape, jnp.bfloat16),
            pltpu.VMEM((lay.outputs + 1, lay.side, lay.width), jnp.float32),
            pltpu.SemaphoreType.DMA((len(rounded) * lay.owners,)),
            pltpu.SemaphoreType.DMA((lay.groups // chunk_groups,)),
        ],
        compiler_params=pltpu.CompilerParams(vmem_limit_bytes=lay.vmem_sums),
        cost_estimate=pl.CostEstimate(flops=400_000_000, bytes_accessed=4_000_000, transcendentals=0),
    )(*plan[2:], tiles, *rounded)


def on_device(
    vectors, energies, intersections, coarse, fine_coarse, coarse_slot, tile_codes, tile_count
):
    rows = lax.axis_size("row")
    cols = lax.axis_size("col")
    row_id = lax.axis_index("row")
    col_id = lax.axis_index("col")
    blocks, pairs, side = intersections.shape
    width = vectors.shape[1]
    points, slots_dev = coarse.shape[:2]
    lay = Layout(rows, cols, blocks, pairs, side, width, points, slots_dev, tile_codes.shape[1], 4)
    if lay.groups * lay.unroll * side * side * 2 > 16 * mib:
        lay = Layout(rows, cols, blocks, pairs, side, width, points, slots_dev, tile_codes.shape[1], 1)
    near = lay.near

    def move(array, row_step, col_step):
        pairs_list = [
            (r * cols + c, (r ^ row_step) * cols + (c ^ col_step)) for r in range(rows) for c in range(cols)
        ]
        return lax.ppermute(array, axes, pairs_list)

    def along(array, step):
        return move(array, 2 * step, 0)

    def to_core(array):
        return move(array, 1, 0)

    def in_plane(array):
        return [array] + [move(array, 0, d) for d in range(1, cols)]

    start = vectors.reshape(blocks, side, width)
    energy = energies.reshape(blocks, side, 1)
    two_owners = lay.owners == 2
    ids = jnp.stack([row_id // 2, row_id % 2, col_id]).astype(jnp.int32)
    listed = jnp.concatenate([tile_codes, tile_count[:, None]], axis=1)
    n_listed = listed.shape[1]
    digits = jnp.concatenate([listed[0] >> 8, listed[0] & 255]).astype(jnp.bfloat16)
    depth = 16 * -(-2 * n_listed // (16 * width * blocks))
    digits = jnp.pad(digits, (0, blocks * depth * width - 2 * n_listed)).reshape(blocks, depth, width)
    joined = jnp.concatenate([intersections, start.astype(jnp.bfloat16), digits], axis=1)

    inputs = in_plane(joined)
    partner = [along(joined, near)] if two_owners else []
    near_coarse = [along(coarse, e) for e in range(1, near)]
    held = (partner, inputs, near_coarse, joined)
    partner, inputs, near_coarse, late_joined = lax.optimization_barrier(held)
    if two_owners:
        sent = partner[0][:, pairs + side :].reshape(-1)[: 2 * n_listed].astype(jnp.int32)
        listed = jnp.concatenate([listed, ((sent[:n_listed] << 8) + sent[n_listed:])[None]], axis=0)
    plan = make_plan(lay, ids, listed, fine_coarse, coarse_slot)
    for part in partner:
        inputs = inputs + in_plane(part)
    turned = turn_own(lay, late_joined)
    blocks_coarse = []
    for part in [coarse] + near_coarse:
        blocks_coarse += [part, to_core(part)]
    turned, blocks_coarse = lax.optimization_barrier((turned, blocks_coarse))
    lines = [along(turned, d) for d in lay.line_steps()]
    for part in partner:
        turned = turn_both(lay, part, turned)
    projected = [project(lay, 0, plan, inputs[:cols], blocks_coarse)]
    held = (inputs, lines, turned, projected)
    inputs, lines, turned, projected = lax.optimization_barrier(held)
    lefts = [turned] + lines
    lefts = lefts + [to_core(part) for part in lefts]
    if two_owners:
        projected.append(project(lay, 1, plan, inputs[cols:], blocks_coarse))
    own_sum, other_sum, tiles = make_tiles(lay, plan, inputs, lefts, projected)

    def over_core(own_part, other_part):
        return (own_part + to_core(other_part).astype(jnp.float32)).reshape(lay.places, blocks, side, width)

    def shifted_part(field):
        return energy * field - spectrum_center * field

    merged = over_core(own_sum, other_sum)
    if two_owners:
        sums = jnp.stack([merged[0] + shifted_part(start), merged[near]])
        for e in range(1, near):
            sent = jnp.stack([merged[e], merged[e ^ near]]).astype(jnp.bfloat16)
            sums = sums + along(sent, e).astype(jnp.float32)
        sums = sums + along(sums.astype(jnp.bfloat16), near)[::-1].astype(jnp.float32)
    else:
        sums = merged + shifted_part(start)[None]

    firsts = sums / spectrum_half
    first = firsts[0]
    own_sum, other_sum = apply_tiles(lay, plan, tiles, in_plane(firsts.astype(jnp.bfloat16)))
    merged = over_core(own_sum, other_sum)
    last = merged[0]
    for d in range(1, lay.places):
        last = last + along(merged[d].astype(jnp.bfloat16), d).astype(jnp.float32)
    second = 2.0 * ((shifted_part(first) + last) / spectrum_half) - start
    return first.reshape(vectors.shape), second.reshape(vectors.shape)


def solution(mesh):
    in_specs = (
        P(axes, None),
        P(axes),
        P(axes, None, None),
        P("col", "row", None, None),
        P(),
        P(),
        P(axes, None),
        P(axes),
    )
    out_specs = (P(axes, None), P(axes, None))
    return jax.shard_map(
        on_device, mesh=mesh, in_specs=in_specs, out_specs=out_specs, check_vma=False
    )
```

```python
import functools

import jax
import jax.numpy as jnp
from jax import lax
from jax.experimental import pallas as pl
from jax.experimental.pallas import tpu as pltpu
from jax.sharding import PartitionSpec as P

spectrum_center = 2.0
spectrum_half = 3.0
axes = ("row", "col")
chunk_groups = 8
mib = 1 << 20


class Layout:
    def __init__(self, rows, cols, blocks, pairs, side, width, points, slots_dev, tile_max, unroll):
        self.rows, self.cols, self.blocks = rows, cols, blocks
        self.pairs, self.side, self.width = pairs, side, width
        self.points, self.slots_dev, self.tile_max = points, slots_dev, tile_max
        self.places = rows // 2
        self.near = max(self.places // 2, 1)
        self.owners = 2 if self.places > 1 else 1
        self.spread = cols * blocks
        self.inputs = self.owners * self.spread
        self.outputs = rows * blocks
        self.slots = 2 * self.near * slots_dev
        self.unroll = unroll
        self.vmem = 60 * mib
        self.vmem_sums = (50 if unroll > 1 else 60) * mib
        most = self.owners * tile_max + self.inputs * (unroll - 1) + (3 + self.owners) * unroll
        self.groups = -(-most // (unroll * chunk_groups)) * chunk_groups

    def line_steps(self):
        return [d for d in range(1, self.places) if d != self.near]


def plan_kernel(lay, ids, listed, fine, stored, slot_of, valid, sizes, group_input, entries, fill):
    place, core, col = ids[0], ids[1], ids[2]
    half = lax.div(place, lay.near)
    blank = lay.outputs * lay.points

    for owner in range(lay.owners):

        def examine(i, found):
            p = owner * lay.spread + i
            from_col = lax.bitwise_xor(lax.div(i, lay.blocks), col)
            from_place = lax.bitwise_xor(place, owner * lay.near)
            block = ((from_place * 2 + core) * lay.cols + from_col) * lay.blocks + lax.rem(i, lay.blocks)
            position = stored[fine[block]]
            at_row = lax.div(position, lay.slots_dev)
            at_place, at_core = lax.div(at_row, 2), lax.rem(at_row, 2)
            slot = (lax.bitwise_xor(at_place, place) * 2 + lax.bitwise_xor(at_core, core)) * lay.slots_dev
            slot = slot + lax.rem(position, lay.slots_dev)
            here = lax.div(at_place, lay.near) == half
            slot_of[p] = jnp.where(here, slot, -1)
            valid[owner * (lay.spread + 1) + found] = i
            fill[p] = 0
            return found + here.astype(jnp.int32)

        sizes[1 + owner] = lax.fori_loop(0, lay.spread, examine, 0)

    def input_of(owner, code):
        j = lax.rem(code, lay.spread)
        from_col = lax.bitwise_xor(lax.div(j, lay.blocks), col)
        return owner * lay.spread + from_col * lay.blocks + lax.rem(j, lay.blocks)

    for owner in range(lay.owners):

        def count(i, carry):
            p = input_of(owner, listed[owner, i])
            fill[p] = fill[p] + 1
            return carry

        lax.fori_loop(0, listed[owner, lay.tile_max], count, 0)

    group_input[0] = 0
    group_input[1] = 0

    def place_groups(p, start):
        used = jnp.where(slot_of[p] >= 0, fill[p], 0)
        fill[p] = start * lay.unroll
        end = start + lax.div(used + (lay.unroll - 1), lay.unroll)

        def name(group, carry):
            group_input[group] = p
            return carry

        lax.fori_loop(start, end, name, 0)
        return end

    total = 2
    for owner in range(lay.owners):
        if owner > 0:
            sizes[lay.owners + owner] = total
        total = lax.fori_loop(owner * lay.spread, (owner + 1) * lay.spread, place_groups, total)
        group_input[total] = owner * lay.spread
        total = total + lax.rem(total, 2)
    sizes[0] = total

    def clear(i, carry):
        entries[i] = blank
        return carry

    lax.fori_loop(0, total * lay.unroll, clear, 0)

    for owner in range(lay.owners):

        def put(i, carry):
            code = listed[owner, i]
            p = input_of(owner, code)

            @pl.when(slot_of[p] >= 0)
            def _():
                out = lax.div(code, lay.spread)
                at_row = lax.div(out, lay.blocks)
                within = lax.rem(out, lay.blocks)
                far = lax.bitwise_xor(lax.div(at_row, 2), place)
                other = lax.bitwise_xor(lax.rem(at_row, 2), core)
                q = (other * lay.places + far) * lay.blocks + within
                a = fine[(at_row * lay.cols + col) * lay.blocks + within] - col * lay.points
                spot = fill[p]
                entries[spot] = q * lay.points + a
                fill[p] = spot + 1

            return carry

        lax.fori_loop(0, listed[owner, lay.tile_max], put, 0)


def make_plan(lay, ids, listed, fine, stored):
    smem = pl.BlockSpec(memory_space=pltpu.SMEM)
    lengths = (
        lay.inputs,
        lay.owners * (lay.spread + 1),
        2 * lay.owners,
        lay.groups,
        lay.groups * lay.unroll,
    )
    return pl.pallas_call(
        functools.partial(plan_kernel, lay),
        out_shape=tuple(jax.ShapeDtypeStruct((n,), jnp.int32) for n in lengths),
        in_specs=[smem] * 4,
        out_specs=(smem,) * 5,
        scratch_shapes=[pltpu.SMEM((lay.inputs,), jnp.int32)],
        cost_estimate=pl.CostEstimate(flops=0, bytes_accessed=20_000_000, transcendentals=0),
    )(ids, listed, fine, stored)


def add_products(lay, group, group_input, entries, tiles, rounded, total):
    held = tiles[pl.ds(group * lay.unroll, lay.unroll)].reshape(lay.unroll * lay.side, lay.side)
    products = jnp.dot(held, rounded[group_input[group]], preferred_element_type=jnp.float32)
    for i in range(lay.unroll):
        q = lax.div(entries[group * lay.unroll + i], lay.points)
        total[q] = total[q] + products[i * lay.side : (i + 1) * lay.side]


def turn_own_kernel(lay, given, turned):
    for t in range(lay.blocks):
        turned[t] = given[t, 0 : lay.pairs, :].T


def turn_own(lay, joined):
    vmem = pl.BlockSpec(memory_space=pltpu.VMEM)
    return pl.pallas_call(
        functools.partial(turn_own_kernel, lay),
        out_shape=jax.ShapeDtypeStruct((lay.blocks, lay.side, lay.pairs), jnp.bfloat16),
        in_specs=[vmem],
        out_specs=vmem,
        compiler_params=pltpu.CompilerParams(vmem_limit_bytes=16 * mib),
        cost_estimate=pl.CostEstimate(flops=1_000_000, bytes_accessed=5_000_000, transcendentals=0),
    )(joined)


def turn_both_kernel(lay, given, own, out):
    out[0 : lay.blocks] = own[...]
    for t in range(lay.blocks):
        out[lay.blocks + t] = given[t, 0 : lay.pairs, :].T


def turn_both(lay, partner, own):
    vmem = pl.BlockSpec(memory_space=pltpu.VMEM)
    return pl.pallas_call(
        functools.partial(turn_both_kernel, lay),
        out_shape=jax.ShapeDtypeStruct((2 * lay.blocks, lay.side, lay.pairs), jnp.bfloat16),
        in_specs=[vmem] * 2,
        out_specs=vmem,
        compiler_params=pltpu.CompilerParams(vmem_limit_bytes=16 * mib),
        cost_estimate=pl.CostEstimate(flops=1_000_000, bytes_accessed=5_000_000, transcendentals=0),
    )(partner, own)


def project_kernel(lay, owner, slot_of, valid, sizes, *refs):
    refs = list(refs)
    given_in = [refs.pop(0) for _ in range(lay.cols)]
    given_coarse = [refs.pop(0) for _ in range(2 * lay.near)]
    out, right, blocks, projected, sems, out_sems = refs
    copies = []

    def fetch(source, target):
        copies.append(pltpu.make_async_copy(source, target, sems.at[len(copies)]))
        copies[-1].start()

    for i in range(2 * lay.near):
        for a in range(lay.points):
            fetch(given_coarse[i].at[a], blocks.at[a, pl.ds(i * lay.slots_dev, lay.slots_dev)])
    for i in range(lay.cols):
        fetch(given_in[i].at[:, pl.ds(0, lay.pairs)], right.at[pl.ds(i * lay.blocks, lay.blocks)])
    for copy in copies:
        copy.wait()
    found = sizes[1 + owner]

    def visit(step, carry):
        for lane in range(2):
            i = valid[owner * (lay.spread + 1) + jnp.minimum(2 * step + lane, found - 1)]
            slot = slot_of[owner * lay.spread + i]
            for a in range(lay.points):
                projected[i, :, a * lay.side : (a + 1) * lay.side] = jnp.dot(
                    blocks[a, slot], right[i], preferred_element_type=jnp.float32
                ).astype(jnp.bfloat16)
        return carry

    lax.fori_loop(0, lax.div(found + 1, 2), visit, 0)

    def store(i):
        return pltpu.make_async_copy(projected.at[i], out.at[i], out_sems.at[i])

    for i in range(lay.spread):

        @pl.when(slot_of[owner * lay.spread + i] >= 0)
        def _():
            store(i).start()

    for i in range(lay.spread):

        @pl.when(slot_of[owner * lay.spread + i] >= 0)
        def _():
            store(i).wait()


def project(lay, owner, plan, inputs, coarse):
    smem = pl.BlockSpec(memory_space=pltpu.SMEM)
    hbm = pl.BlockSpec(memory_space=pl.ANY)
    shape = (lay.spread, lay.pairs, lay.points * lay.side)
    return pl.pallas_call(
        functools.partial(project_kernel, lay, owner),
        out_shape=jax.ShapeDtypeStruct(shape, jnp.bfloat16),
        in_specs=[smem] * 3 + [hbm] * (len(inputs) + len(coarse)),
        out_specs=hbm,
        scratch_shapes=[
            pltpu.VMEM((lay.spread, lay.pairs, lay.side), jnp.bfloat16),
            pltpu.VMEM((lay.points, lay.slots, lay.pairs, lay.pairs), jnp.bfloat16),
            pltpu.VMEM(shape, jnp.bfloat16),
            pltpu.SemaphoreType.DMA((len(inputs) + len(coarse) * lay.points,)),
            pltpu.SemaphoreType.DMA((lay.spread,)),
        ],
        compiler_params=pltpu.CompilerParams(vmem_limit_bytes=lay.vmem),
        cost_estimate=pl.CostEstimate(flops=1_000_000_000, bytes_accessed=16_000_000, transcendentals=0),
    )(*plan[:3], *inputs, *coarse)


def tiles_kernel(lay, slot_of, sizes, group_input, entries, *refs):
    lines = lay.line_steps()
    refs = list(refs)
    given_in = [refs.pop(0) for _ in range(lay.owners * lay.cols)]
    given_out = [refs.pop(0) for _ in range(2 * (1 + len(lines)))]
    given_projected = [refs.pop(0) for _ in range(lay.owners)]
    own_sum, other_sum, tiles_out = refs[:3]
    left, projected, rounded, tiles, total, sems, in_sems, out_sems = refs[3:]
    copies = []

    def fetch(source, target):
        copies.append(pltpu.make_async_copy(source, target, sems.at[len(copies)]))
        copies[-1].start()

    def load(p):
        source = given_projected[p // lay.spread].at[p % lay.spread]
        return pltpu.make_async_copy(source, projected.at[p], in_sems.at[p])

    for k in range(2):
        held = given_out[k * (1 + len(lines)) :]
        for g in range(lay.owners):
            spot = (k * lay.places + g * lay.near) * lay.blocks
            fetch(held[0].at[pl.ds(g * lay.blocks, lay.blocks)], left.at[pl.ds(spot, lay.blocks)])
        for i, d in enumerate(lines):
            spot = (k * lay.places + d) * lay.blocks
            fetch(held[1 + i], left.at[pl.ds(spot, lay.blocks)])
    for i, ref in enumerate(given_in):
        part = pl.ds(i * lay.blocks, lay.blocks)
        fetch(ref.at[:, pl.ds(lay.pairs, lay.side)], rounded.at[part])
    for p in range(lay.inputs):

        @pl.when(slot_of[p] >= 0)
        def _():
            load(p).start()

    total[...] = jnp.zeros_like(total)
    for copy in copies:
        copy.wait()
    used = sizes[0]

    for owner in range(lay.owners):
        for p in range(owner * lay.spread, (owner + 1) * lay.spread):

            @pl.when(slot_of[p] >= 0)
            def _():
                load(p).wait()

        def make_group(group):
            block = projected[group_input[group]]
            numbers = [entries[group * lay.unroll + i] for i in range(lay.unroll)]
            places = [jnp.minimum(lax.div(n, lay.points), lay.outputs - 1) for n in numbers]
            lefts = jnp.concatenate([left[q] for q in places], axis=0)
            both = jnp.dot(lefts, block, preferred_element_type=jnp.float32)
            for i in range(lay.unroll):
                mine = both[i * lay.side : (i + 1) * lay.side]
                tile = mine[:, : lay.side]
                for b in range(1, lay.points):
                    at_b = mine[:, b * lay.side : (b + 1) * lay.side]
                    tile = jnp.where(lax.rem(numbers[i], lay.points) == b, at_b, tile)
                tiles[group * lay.unroll + i] = tile.astype(jnp.bfloat16)

        def pair_step(pair, carry):
            for lane in range(2):
                add_products(lay, 2 * pair - 2 + lane, group_input, entries, tiles, rounded, total)
            for lane in range(2):
                make_group(2 * pair + lane)
            return carry

        first = 1 if owner == 0 else lax.div(sizes[lay.owners + owner], 2)
        last = used if owner == lay.owners - 1 else sizes[lay.owners + owner + 1]
        lax.fori_loop(first, lax.div(last, 2), pair_step, 0)

    span = chunk_groups * lay.unroll

    def store(chunk):
        part = pl.ds(chunk * span, span)
        return pltpu.make_async_copy(tiles.at[part], tiles_out.at[part], out_sems.at[chunk])

    for chunk in range(lay.groups // chunk_groups):

        @pl.when(used > chunk * chunk_groups)
        def _():
            store(chunk).start()

    for lane in range(2):
        add_products(lay, used - 2 + lane, group_input, entries, tiles, rounded, total)
    give_sums(lay, total, own_sum, other_sum)
    for chunk in range(lay.groups // chunk_groups):

        @pl.when(used > chunk * chunk_groups)
        def _():
            store(chunk).wait()


def give_sums(lay, total, own_sum, other_sum):
    own = lay.places * lay.blocks
    own_sum[...] = total[0:own]
    other_sum[...] = total[own : 2 * own].astype(jnp.bfloat16)


def make_tiles(lay, plan, inputs, outputs, projected):
    smem = pl.BlockSpec(memory_space=pltpu.SMEM)
    hbm = pl.BlockSpec(memory_space=pl.ANY)
    vmem = pl.BlockSpec(memory_space=pltpu.VMEM)
    own = lay.places * lay.blocks
    sums = jax.ShapeDtypeStruct((own, lay.side, lay.width), jnp.float32)
    sent = jax.ShapeDtypeStruct((own, lay.side, lay.width), jnp.bfloat16)
    tiles = (lay.groups * lay.unroll, lay.side, lay.side)
    return pl.pallas_call(
        functools.partial(tiles_kernel, lay),
        out_shape=(sums, sent, jax.ShapeDtypeStruct(tiles, jnp.bfloat16)),
        in_specs=[smem] * 4 + [hbm] * (len(inputs) + len(outputs) + len(projected)),
        out_specs=(vmem, vmem, hbm),
        scratch_shapes=[
            pltpu.VMEM((lay.outputs, lay.side, lay.pairs), jnp.bfloat16),
            pltpu.VMEM((lay.inputs, lay.pairs, lay.points * lay.side), jnp.bfloat16),
            pltpu.VMEM((lay.inputs, lay.side, lay.width), jnp.bfloat16),
            pltpu.VMEM(tiles, jnp.bfloat16),
            pltpu.VMEM((lay.outputs + 1, lay.side, lay.width), jnp.float32),
            pltpu.SemaphoreType.DMA((len(inputs) + 2 * lay.places,)),
            pltpu.SemaphoreType.DMA((lay.inputs,)),
            pltpu.SemaphoreType.DMA((lay.groups // chunk_groups,)),
        ],
        compiler_params=pltpu.CompilerParams(vmem_limit_bytes=lay.vmem_sums),
        cost_estimate=pl.CostEstimate(flops=4_000_000_000, bytes_accessed=30_000_000, transcendentals=0),
    )(plan[0], *plan[2:], *inputs, *outputs, *projected)


def apply_kernel(lay, sizes, group_input, entries, tiles_in, *refs):
    given_vec = refs[: lay.cols]
    own_sum, other_sum = refs[lay.cols : lay.cols + 2]
    rounded, tiles, total, sems, out_sems = refs[lay.cols + 2 :]
    used = sizes[0]
    span = chunk_groups * lay.unroll

    def load(chunk):
        part = pl.ds(chunk * span, span)
        return pltpu.make_async_copy(tiles_in.at[part], tiles.at[part], out_sems.at[chunk])

    for chunk in range(lay.groups // chunk_groups):

        @pl.when(used > chunk * chunk_groups)
        def _():
            load(chunk).start()

    copies = []
    for d in range(lay.cols):
        for g in range(lay.owners):
            target = rounded.at[pl.ds((g * lay.cols + d) * lay.blocks, lay.blocks)]
            copies.append(pltpu.make_async_copy(given_vec[d].at[g], target, sems.at[len(copies)]))
            copies[-1].start()
    total[...] = jnp.zeros_like(total)
    for copy in copies:
        copy.wait()
    for chunk in range(lay.groups // chunk_groups):

        @pl.when(used > chunk * chunk_groups)
        def _():
            load(chunk).wait()

    def pair_step(pair, carry):
        for lane in range(2):
            add_products(lay, 2 * pair + lane, group_input, entries, tiles, rounded, total)
        return carry

    lax.fori_loop(1, lax.div(used, 2), pair_step, 0)
    give_sums(lay, total, own_sum, other_sum)


def apply_tiles(lay, plan, tiles, rounded):
    smem = pl.BlockSpec(memory_space=pltpu.SMEM)
    hbm = pl.BlockSpec(memory_space=pl.ANY)
    vmem = pl.BlockSpec(memory_space=pltpu.VMEM)
    own = lay.places * lay.blocks
    sums = jax.ShapeDtypeStruct((own, lay.side, lay.width), jnp.float32)
    sent = jax.ShapeDtypeStruct((own, lay.side, lay.width), jnp.bfloat16)
    return pl.pallas_call(
        functools.partial(apply_kernel, lay),
        out_shape=(sums, sent),
        in_specs=[smem] * 3 + [hbm] * (1 + len(rounded)),
        out_specs=(vmem, vmem),
        scratch_shapes=[
            pltpu.VMEM((lay.inputs, lay.side, lay.width), jnp.bfloat16),
            pltpu.VMEM(tiles.shape, jnp.bfloat16),
            pltpu.VMEM((lay.outputs + 1, lay.side, lay.width), jnp.float32),
            pltpu.SemaphoreType.DMA((len(rounded) * lay.owners,)),
            pltpu.SemaphoreType.DMA((lay.groups // chunk_groups,)),
        ],
        compiler_params=pltpu.CompilerParams(vmem_limit_bytes=lay.vmem_sums),
        cost_estimate=pl.CostEstimate(flops=400_000_000, bytes_accessed=4_000_000, transcendentals=0),
    )(*plan[2:], tiles, *rounded)


def on_device(
    vectors, energies, intersections, coarse, fine_coarse, coarse_slot, tile_codes, tile_count
):
    rows = lax.axis_size("row")
    cols = lax.axis_size("col")
    row_id = lax.axis_index("row")
    col_id = lax.axis_index("col")
    blocks, pairs, side = intersections.shape
    width = vectors.shape[1]
    points, slots_dev = coarse.shape[:2]
    lay = Layout(rows, cols, blocks, pairs, side, width, points, slots_dev, tile_codes.shape[1], 4)
    if lay.groups * lay.unroll * side * side * 2 > 16 * mib:
        lay = Layout(rows, cols, blocks, pairs, side, width, points, slots_dev, tile_codes.shape[1], 1)
    near = lay.near

    def move(array, row_step, col_step):
        pairs_list = [
            (r * cols + c, (r ^ row_step) * cols + (c ^ col_step)) for r in range(rows) for c in range(cols)
        ]
        return lax.ppermute(array, axes, pairs_list)

    def along(array, step):
        return move(array, 2 * step, 0)

    def to_core(array):
        return move(array, 1, 0)

    def in_plane(array):
        return [array] + [move(array, 0, d) for d in range(1, cols)]

    start = vectors.reshape(blocks, side, width)
    energy = energies.reshape(blocks, side, 1)
    two_owners = lay.owners == 2
    ids = jnp.stack([row_id // 2, row_id % 2, col_id]).astype(jnp.int32)
    listed = jnp.concatenate([tile_codes, tile_count[:, None]], axis=1)
    n_listed = listed.shape[1]
    digits = jnp.concatenate([listed[0] >> 8, listed[0] & 255]).astype(jnp.bfloat16)
    depth = 16 * -(-2 * n_listed // (16 * width * blocks))
    digits = jnp.pad(digits, (0, blocks * depth * width - 2 * n_listed)).reshape(blocks, depth, width)
    joined = jnp.concatenate([intersections, start.astype(jnp.bfloat16), digits], axis=1)

    inputs = in_plane(joined)
    partner = [along(joined, near)] if two_owners else []
    near_coarse = [along(coarse, e) for e in range(1, near)]
    held = (partner, inputs, near_coarse, joined)
    partner, inputs, near_coarse, late_joined = lax.optimization_barrier(held)
    if two_owners:
        sent = partner[0][:, pairs + side :].reshape(-1)[: 2 * n_listed].astype(jnp.int32)
        listed = jnp.concatenate([listed, ((sent[:n_listed] << 8) + sent[n_listed:])[None]], axis=0)
    plan = make_plan(lay, ids, listed, fine_coarse, coarse_slot)
    for part in partner:
        inputs = inputs + in_plane(part)
    turned = turn_own(lay, late_joined)
    blocks_coarse = []
    for part in [coarse] + near_coarse:
        blocks_coarse += [part, to_core(part)]
    turned, blocks_coarse = lax.optimization_barrier((turned, blocks_coarse))
    lines = [along(turned, d) for d in lay.line_steps()]
    for part in partner:
        turned = turn_both(lay, part, turned)
    projected = [project(lay, 0, plan, inputs[:cols], blocks_coarse)]
    held = (inputs, lines, turned, projected)
    inputs, lines, turned, projected = lax.optimization_barrier(held)
    lefts = [turned] + lines
    lefts = lefts + [to_core(part) for part in lefts]
    if two_owners:
        projected.append(project(lay, 1, plan, inputs[cols:], blocks_coarse))
    own_sum, other_sum, tiles = make_tiles(lay, plan, inputs, lefts, projected)

    def over_core(own_part, other_part):
        return (own_part + to_core(other_part).astype(jnp.float32)).reshape(lay.places, blocks, side, width)

    def shifted_part(field):
        return energy * field - spectrum_center * field

    merged = over_core(own_sum, other_sum)
    if two_owners:
        sums = jnp.stack([merged[0] + shifted_part(start), merged[near]])
        for e in range(1, near):
            sent = jnp.stack([merged[e], merged[e ^ near]]).astype(jnp.bfloat16)
            sums = sums + along(sent, e).astype(jnp.float32)
        sums = sums + along(sums.astype(jnp.bfloat16), near)[::-1].astype(jnp.float32)
    else:
        sums = merged + shifted_part(start)[None]

    firsts = sums / spectrum_half
    first = firsts[0]
    own_sum, other_sum = apply_tiles(lay, plan, tiles, in_plane(firsts.astype(jnp.bfloat16)))
    merged = over_core(own_sum, other_sum)
    last = merged[0]
    for d in range(1, lay.places):
        last = last + along(merged[d].astype(jnp.bfloat16), d).astype(jnp.float32)
    second = 2.0 * ((shifted_part(first) + last) / spectrum_half) - start
    return first.reshape(vectors.shape), second.reshape(vectors.shape)


def solution(mesh):
    in_specs = (
        P(axes, None),
        P(axes),
        P(axes, None, None),
        P("col", "row", None, None),
        P(),
        P(),
        P(axes, None),
        P(axes),
    )
    out_specs = (P(axes, None), P(axes, None))
    return jax.shard_map(
        on_device, mesh=mesh, in_specs=in_specs, out_specs=out_specs, check_vma=False
    )
```

```python
import functools

import jax
import jax.numpy as jnp
from jax import lax
from jax.experimental import pallas as pl
from jax.experimental.pallas import tpu as pltpu
from jax.sharding import PartitionSpec as P

spectrum_center = 2.0
spectrum_half = 3.0
axes = ("row", "col")
chunk_groups = 8
batch = 4
mib = 1 << 20


class Layout:
    def __init__(self, rows, cols, blocks, pairs, side, width, points, slots_dev, tile_max, unroll):
        self.rows, self.cols, self.blocks = rows, cols, blocks
        self.pairs, self.side, self.width = pairs, side, width
        self.points, self.slots_dev, self.tile_max = points, slots_dev, tile_max
        self.places = rows // 2
        self.near = max(self.places // 2, 1)
        self.owners = 2 if self.places > 1 else 1
        self.spread = cols * blocks
        self.inputs = self.owners * self.spread
        self.outputs = rows * blocks
        self.slots = 2 * self.near * slots_dev
        self.unroll = unroll
        self.vmem = 60 * mib
        self.vmem_sums = (50 if unroll > 1 else 60) * mib
        most = self.owners * tile_max + self.inputs * (unroll - 1) + (2 * batch + self.owners * (batch - 1)) * unroll
        self.groups = -(-most // (unroll * chunk_groups)) * chunk_groups

    def line_steps(self):
        return [d for d in range(1, self.places) if d != self.near]


def plan_kernel(lay, ids, listed, fine, stored, slot_of, valid, sizes, group_input, entries, fill):
    place, core, col = ids[0], ids[1], ids[2]
    half = lax.div(place, lay.near)
    blank = lay.outputs * lay.points

    for owner in range(lay.owners):

        def examine(i, found):
            p = owner * lay.spread + i
            from_col = lax.bitwise_xor(lax.div(i, lay.blocks), col)
            from_place = lax.bitwise_xor(place, owner * lay.near)
            block = ((from_place * 2 + core) * lay.cols + from_col) * lay.blocks + lax.rem(i, lay.blocks)
            position = stored[fine[block]]
            at_row = lax.div(position, lay.slots_dev)
            at_place, at_core = lax.div(at_row, 2), lax.rem(at_row, 2)
            slot = (lax.bitwise_xor(at_place, place) * 2 + lax.bitwise_xor(at_core, core)) * lay.slots_dev
            slot = slot + lax.rem(position, lay.slots_dev)
            here = lax.div(at_place, lay.near) == half
            slot_of[p] = jnp.where(here, slot, -1)
            valid[owner * (lay.spread + 1) + found] = i
            fill[p] = 0
            return found + here.astype(jnp.int32)

        sizes[1 + owner] = lax.fori_loop(0, lay.spread, examine, 0)

    def input_of(owner, code):
        j = lax.rem(code, lay.spread)
        from_col = lax.bitwise_xor(lax.div(j, lay.blocks), col)
        return owner * lay.spread + from_col * lay.blocks + lax.rem(j, lay.blocks)

    for owner in range(lay.owners):

        def count(i, carry):
            p = input_of(owner, listed[owner, i])
            fill[p] = fill[p] + 1
            return carry

        lax.fori_loop(0, listed[owner, lay.tile_max], count, 0)

    for lane in range(batch):
        group_input[lane] = 0

    def place_groups(p, start):
        used = jnp.where(slot_of[p] >= 0, fill[p], 0)
        fill[p] = start * lay.unroll
        end = start + lax.div(used + (lay.unroll - 1), lay.unroll)

        def name(group, carry):
            group_input[group] = p
            return carry

        lax.fori_loop(start, end, name, 0)
        return end

    total = batch
    for owner in range(lay.owners):
        if owner > 0:
            sizes[lay.owners + owner] = total
        total = lax.fori_loop(owner * lay.spread, (owner + 1) * lay.spread, place_groups, total)
        for lane in range(batch - 1):
            group_input[total + lane] = owner * lay.spread
        total = lax.div(total + batch - 1, batch) * batch
    sizes[0] = total

    def clear(i, carry):
        entries[i] = blank
        return carry

    lax.fori_loop(0, total * lay.unroll, clear, 0)

    for owner in range(lay.owners):

        def put(i, carry):
            code = listed[owner, i]
            p = input_of(owner, code)

            @pl.when(slot_of[p] >= 0)
            def _():
                out = lax.div(code, lay.spread)
                at_row = lax.div(out, lay.blocks)
                within = lax.rem(out, lay.blocks)
                far = lax.bitwise_xor(lax.div(at_row, 2), place)
                other = lax.bitwise_xor(lax.rem(at_row, 2), core)
                q = (other * lay.places + far) * lay.blocks + within
                a = fine[(at_row * lay.cols + col) * lay.blocks + within] - col * lay.points
                spot = fill[p]
                entries[spot] = q * lay.points + a
                fill[p] = spot + 1

            return carry

        lax.fori_loop(0, listed[owner, lay.tile_max], put, 0)


def make_plan(lay, ids, listed, fine, stored):
    smem = pl.BlockSpec(memory_space=pltpu.SMEM)
    lengths = (
        lay.inputs,
        lay.owners * (lay.spread + 1),
        2 * lay.owners,
        lay.groups,
        lay.groups * lay.unroll,
    )
    return pl.pallas_call(
        functools.partial(plan_kernel, lay),
        out_shape=tuple(jax.ShapeDtypeStruct((n,), jnp.int32) for n in lengths),
        in_specs=[smem] * 4,
        out_specs=(smem,) * 5,
        scratch_shapes=[pltpu.SMEM((lay.inputs,), jnp.int32)],
        cost_estimate=pl.CostEstimate(flops=0, bytes_accessed=20_000_000, transcendentals=0),
    )(ids, listed, fine, stored)


def add_products(lay, group, group_input, entries, tiles, rounded, total):
    held = tiles[pl.ds(group * lay.unroll, lay.unroll)].reshape(lay.unroll * lay.side, lay.side)
    products = jnp.dot(held, rounded[group_input[group]], preferred_element_type=jnp.float32)
    for i in range(lay.unroll):
        q = lax.div(entries[group * lay.unroll + i], lay.points)
        total[q] = total[q] + products[i * lay.side : (i + 1) * lay.side]


def turn_own_kernel(lay, given, turned):
    for t in range(lay.blocks):
        turned[t] = given[t, 0 : lay.pairs, :].T


def turn_own(lay, joined):
    vmem = pl.BlockSpec(memory_space=pltpu.VMEM)
    return pl.pallas_call(
        functools.partial(turn_own_kernel, lay),
        out_shape=jax.ShapeDtypeStruct((lay.blocks, lay.side, lay.pairs), jnp.bfloat16),
        in_specs=[vmem],
        out_specs=vmem,
        compiler_params=pltpu.CompilerParams(vmem_limit_bytes=16 * mib),
        cost_estimate=pl.CostEstimate(flops=1_000_000, bytes_accessed=5_000_000, transcendentals=0),
    )(joined)


def turn_both_kernel(lay, given, own, out):
    out[0 : lay.blocks] = own[...]
    for t in range(lay.blocks):
        out[lay.blocks + t] = given[t, 0 : lay.pairs, :].T


def turn_both(lay, partner, own):
    vmem = pl.BlockSpec(memory_space=pltpu.VMEM)
    return pl.pallas_call(
        functools.partial(turn_both_kernel, lay),
        out_shape=jax.ShapeDtypeStruct((2 * lay.blocks, lay.side, lay.pairs), jnp.bfloat16),
        in_specs=[vmem] * 2,
        out_specs=vmem,
        compiler_params=pltpu.CompilerParams(vmem_limit_bytes=16 * mib),
        cost_estimate=pl.CostEstimate(flops=1_000_000, bytes_accessed=5_000_000, transcendentals=0),
    )(partner, own)


def project_kernel(lay, owner, slot_of, valid, sizes, *refs):
    refs = list(refs)
    given_in = [refs.pop(0) for _ in range(lay.cols)]
    given_coarse = [refs.pop(0) for _ in range(2 * lay.near)]
    out, right, blocks, projected, sems, out_sems = refs
    copies = []

    def fetch(source, target):
        copies.append(pltpu.make_async_copy(source, target, sems.at[len(copies)]))
        copies[-1].start()

    for i in range(2 * lay.near):
        for a in range(lay.points):
            fetch(given_coarse[i].at[a], blocks.at[a, pl.ds(i * lay.slots_dev, lay.slots_dev)])
    for i in range(lay.cols):
        fetch(given_in[i].at[:, pl.ds(0, lay.pairs)], right.at[pl.ds(i * lay.blocks, lay.blocks)])
    for copy in copies:
        copy.wait()
    found = sizes[1 + owner]

    def visit(step, carry):
        for lane in range(2):
            i = valid[owner * (lay.spread + 1) + jnp.minimum(2 * step + lane, found - 1)]
            slot = slot_of[owner * lay.spread + i]
            for a in range(lay.points):
                projected[i, :, a * lay.side : (a + 1) * lay.side] = jnp.dot(
                    blocks[a, slot], right[i], preferred_element_type=jnp.float32
                ).astype(jnp.bfloat16)
        return carry

    lax.fori_loop(0, lax.div(found + 1, 2), visit, 0)

    def store(i):
        return pltpu.make_async_copy(projected.at[i], out.at[i], out_sems.at[i])

    for i in range(lay.spread):

        @pl.when(slot_of[owner * lay.spread + i] >= 0)
        def _():
            store(i).start()

    for i in range(lay.spread):

        @pl.when(slot_of[owner * lay.spread + i] >= 0)
        def _():
            store(i).wait()


def project(lay, owner, plan, inputs, coarse):
    smem = pl.BlockSpec(memory_space=pltpu.SMEM)
    hbm = pl.BlockSpec(memory_space=pl.ANY)
    shape = (lay.spread, lay.pairs, lay.points * lay.side)
    return pl.pallas_call(
        functools.partial(project_kernel, lay, owner),
        out_shape=jax.ShapeDtypeStruct(shape, jnp.bfloat16),
        in_specs=[smem] * 3 + [hbm] * (len(inputs) + len(coarse)),
        out_specs=hbm,
        scratch_shapes=[
            pltpu.VMEM((lay.spread, lay.pairs, lay.side), jnp.bfloat16),
            pltpu.VMEM((lay.points, lay.slots, lay.pairs, lay.pairs), jnp.bfloat16),
            pltpu.VMEM(shape, jnp.bfloat16),
            pltpu.SemaphoreType.DMA((len(inputs) + len(coarse) * lay.points,)),
            pltpu.SemaphoreType.DMA((lay.spread,)),
        ],
        compiler_params=pltpu.CompilerParams(vmem_limit_bytes=lay.vmem),
        cost_estimate=pl.CostEstimate(flops=1_000_000_000, bytes_accessed=16_000_000, transcendentals=0),
    )(*plan[:3], *inputs, *coarse)


def tiles_kernel(lay, slot_of, sizes, group_input, entries, *refs):
    lines = lay.line_steps()
    refs = list(refs)
    given_in = [refs.pop(0) for _ in range(lay.owners * lay.cols)]
    given_out = [refs.pop(0) for _ in range(2 * (1 + len(lines)))]
    given_projected = [refs.pop(0) for _ in range(lay.owners)]
    own_sum, other_sum, tiles_out = refs[:3]
    left, projected, rounded, tiles, total, sems, in_sems, out_sems = refs[3:]
    copies = []

    def fetch(source, target):
        copies.append(pltpu.make_async_copy(source, target, sems.at[len(copies)]))
        copies[-1].start()

    def load(p):
        source = given_projected[p // lay.spread].at[p % lay.spread]
        return pltpu.make_async_copy(source, projected.at[p], in_sems.at[p])

    for k in range(2):
        held = given_out[k * (1 + len(lines)) :]
        for g in range(lay.owners):
            spot = (k * lay.places + g * lay.near) * lay.blocks
            fetch(held[0].at[pl.ds(g * lay.blocks, lay.blocks)], left.at[pl.ds(spot, lay.blocks)])
        for i, d in enumerate(lines):
            spot = (k * lay.places + d) * lay.blocks
            fetch(held[1 + i], left.at[pl.ds(spot, lay.blocks)])
    for i, ref in enumerate(given_in):
        part = pl.ds(i * lay.blocks, lay.blocks)
        fetch(ref.at[:, pl.ds(lay.pairs, lay.side)], rounded.at[part])
    for p in range(lay.inputs):

        @pl.when(slot_of[p] >= 0)
        def _():
            load(p).start()

    total[...] = jnp.zeros_like(total)
    for copy in copies:
        copy.wait()
    used = sizes[0]

    for owner in range(lay.owners):
        for p in range(owner * lay.spread, (owner + 1) * lay.spread):

            @pl.when(slot_of[p] >= 0)
            def _():
                load(p).wait()

        def make_group(group):
            block = projected[group_input[group]]
            numbers = [entries[group * lay.unroll + i] for i in range(lay.unroll)]
            places = [jnp.minimum(lax.div(n, lay.points), lay.outputs - 1) for n in numbers]
            lefts = jnp.concatenate([left[q] for q in places], axis=0)
            both = jnp.dot(lefts, block, preferred_element_type=jnp.float32)
            for i in range(lay.unroll):
                mine = both[i * lay.side : (i + 1) * lay.side]
                tile = mine[:, : lay.side]
                for b in range(1, lay.points):
                    at_b = mine[:, b * lay.side : (b + 1) * lay.side]
                    tile = jnp.where(lax.rem(numbers[i], lay.points) == b, at_b, tile)
                tiles[group * lay.unroll + i] = tile.astype(jnp.bfloat16)

        def batch_step(step, carry):
            for lane in range(batch):
                add_products(lay, batch * (step - 1) + lane, group_input, entries, tiles, rounded, total)
            for lane in range(batch):
                make_group(batch * step + lane)
            return carry

        first = 1 if owner == 0 else lax.div(sizes[lay.owners + owner], batch)
        last = used if owner == lay.owners - 1 else sizes[lay.owners + owner + 1]
        lax.fori_loop(first, lax.div(last, batch), batch_step, 0)

    span = chunk_groups * lay.unroll

    def store(chunk):
        part = pl.ds(chunk * span, span)
        return pltpu.make_async_copy(tiles.at[part], tiles_out.at[part], out_sems.at[chunk])

    for chunk in range(lay.groups // chunk_groups):

        @pl.when(used > chunk * chunk_groups)
        def _():
            store(chunk).start()

    for lane in range(batch):
        add_products(lay, used - batch + lane, group_input, entries, tiles, rounded, total)
    give_sums(lay, total, own_sum, other_sum)
    for chunk in range(lay.groups // chunk_groups):

        @pl.when(used > chunk * chunk_groups)
        def _():
            store(chunk).wait()


def give_sums(lay, total, own_sum, other_sum):
    own = lay.places * lay.blocks
    own_sum[...] = total[0:own]
    other_sum[...] = total[own : 2 * own].astype(jnp.bfloat16)


def make_tiles(lay, plan, inputs, outputs, projected):
    smem = pl.BlockSpec(memory_space=pltpu.SMEM)
    hbm = pl.BlockSpec(memory_space=pl.ANY)
    vmem = pl.BlockSpec(memory_space=pltpu.VMEM)
    own = lay.places * lay.blocks
    sums = jax.ShapeDtypeStruct((own, lay.side, lay.width), jnp.float32)
    sent = jax.ShapeDtypeStruct((own, lay.side, lay.width), jnp.bfloat16)
    tiles = (lay.groups * lay.unroll, lay.side, lay.side)
    return pl.pallas_call(
        functools.partial(tiles_kernel, lay),
        out_shape=(sums, sent, jax.ShapeDtypeStruct(tiles, jnp.bfloat16)),
        in_specs=[smem] * 4 + [hbm] * (len(inputs) + len(outputs) + len(projected)),
        out_specs=(vmem, vmem, hbm),
        scratch_shapes=[
            pltpu.VMEM((lay.outputs, lay.side, lay.pairs), jnp.bfloat16),
            pltpu.VMEM((lay.inputs, lay.pairs, lay.points * lay.side), jnp.bfloat16),
            pltpu.VMEM((lay.inputs, lay.side, lay.width), jnp.bfloat16),
            pltpu.VMEM(tiles, jnp.bfloat16),
            pltpu.VMEM((lay.outputs + 1, lay.side, lay.width), jnp.float32),
            pltpu.SemaphoreType.DMA((len(inputs) + 2 * lay.places,)),
            pltpu.SemaphoreType.DMA((lay.inputs,)),
            pltpu.SemaphoreType.DMA((lay.groups // chunk_groups,)),
        ],
        compiler_params=pltpu.CompilerParams(vmem_limit_bytes=lay.vmem_sums),
        cost_estimate=pl.CostEstimate(flops=4_000_000_000, bytes_accessed=30_000_000, transcendentals=0),
    )(plan[0], *plan[2:], *inputs, *outputs, *projected)


def apply_kernel(lay, sizes, group_input, entries, tiles_in, *refs):
    given_vec = refs[: lay.cols]
    own_sum, other_sum = refs[lay.cols : lay.cols + 2]
    rounded, tiles, total, sems, out_sems = refs[lay.cols + 2 :]
    used = sizes[0]
    span = chunk_groups * lay.unroll

    def load(chunk):
        part = pl.ds(chunk * span, span)
        return pltpu.make_async_copy(tiles_in.at[part], tiles.at[part], out_sems.at[chunk])

    for chunk in range(lay.groups // chunk_groups):

        @pl.when(used > chunk * chunk_groups)
        def _():
            load(chunk).start()

    copies = []
    for d in range(lay.cols):
        for g in range(lay.owners):
            target = rounded.at[pl.ds((g * lay.cols + d) * lay.blocks, lay.blocks)]
            copies.append(pltpu.make_async_copy(given_vec[d].at[g], target, sems.at[len(copies)]))
            copies[-1].start()
    total[...] = jnp.zeros_like(total)
    for copy in copies:
        copy.wait()
    for chunk in range(lay.groups // chunk_groups):

        @pl.when(used > chunk * chunk_groups)
        def _():
            load(chunk).wait()

    def batch_step(step, carry):
        for lane in range(batch):
            add_products(lay, batch * step + lane, group_input, entries, tiles, rounded, total)
        return carry

    lax.fori_loop(1, lax.div(used, batch), batch_step, 0)
    give_sums(lay, total, own_sum, other_sum)


def apply_tiles(lay, plan, tiles, rounded):
    smem = pl.BlockSpec(memory_space=pltpu.SMEM)
    hbm = pl.BlockSpec(memory_space=pl.ANY)
    vmem = pl.BlockSpec(memory_space=pltpu.VMEM)
    own = lay.places * lay.blocks
    sums = jax.ShapeDtypeStruct((own, lay.side, lay.width), jnp.float32)
    sent = jax.ShapeDtypeStruct((own, lay.side, lay.width), jnp.bfloat16)
    return pl.pallas_call(
        functools.partial(apply_kernel, lay),
        out_shape=(sums, sent),
        in_specs=[smem] * 3 + [hbm] * (1 + len(rounded)),
        out_specs=(vmem, vmem),
        scratch_shapes=[
            pltpu.VMEM((lay.inputs, lay.side, lay.width), jnp.bfloat16),
            pltpu.VMEM(tiles.shape, jnp.bfloat16),
            pltpu.VMEM((lay.outputs + 1, lay.side, lay.width), jnp.float32),
            pltpu.SemaphoreType.DMA((len(rounded) * lay.owners,)),
            pltpu.SemaphoreType.DMA((lay.groups // chunk_groups,)),
        ],
        compiler_params=pltpu.CompilerParams(vmem_limit_bytes=lay.vmem_sums),
        cost_estimate=pl.CostEstimate(flops=400_000_000, bytes_accessed=4_000_000, transcendentals=0),
    )(*plan[2:], tiles, *rounded)


def on_device(
    vectors, energies, intersections, coarse, fine_coarse, coarse_slot, tile_codes, tile_count
):
    rows = lax.axis_size("row")
    cols = lax.axis_size("col")
    row_id = lax.axis_index("row")
    col_id = lax.axis_index("col")
    blocks, pairs, side = intersections.shape
    width = vectors.shape[1]
    points, slots_dev = coarse.shape[:2]
    lay = Layout(rows, cols, blocks, pairs, side, width, points, slots_dev, tile_codes.shape[1], 4)
    if lay.groups * lay.unroll * side * side * 2 > 16 * mib:
        lay = Layout(rows, cols, blocks, pairs, side, width, points, slots_dev, tile_codes.shape[1], 1)
    near = lay.near

    def move(array, row_step, col_step):
        pairs_list = [
            (r * cols + c, (r ^ row_step) * cols + (c ^ col_step)) for r in range(rows) for c in range(cols)
        ]
        return lax.ppermute(array, axes, pairs_list)

    def along(array, step):
        return move(array, 2 * step, 0)

    def to_core(array):
        return move(array, 1, 0)

    def in_plane(array):
        return [array] + [move(array, 0, d) for d in range(1, cols)]

    start = vectors.reshape(blocks, side, width)
    energy = energies.reshape(blocks, side, 1)
    two_owners = lay.owners == 2
    ids = jnp.stack([row_id // 2, row_id % 2, col_id]).astype(jnp.int32)
    listed = jnp.concatenate([tile_codes, tile_count[:, None]], axis=1)
    n_listed = listed.shape[1]
    digits = jnp.concatenate([listed[0] >> 8, listed[0] & 255]).astype(jnp.bfloat16)
    depth = 16 * -(-2 * n_listed // (16 * width * blocks))
    digits = jnp.pad(digits, (0, blocks * depth * width - 2 * n_listed)).reshape(blocks, depth, width)
    joined = jnp.concatenate([intersections, start.astype(jnp.bfloat16), digits], axis=1)

    inputs = in_plane(joined)
    partner = [along(joined, near)] if two_owners else []
    near_coarse = [along(coarse, e) for e in range(1, near)]
    held = (partner, inputs, near_coarse, joined)
    partner, inputs, near_coarse, late_joined = lax.optimization_barrier(held)
    if two_owners:
        sent = partner[0][:, pairs + side :].reshape(-1)[: 2 * n_listed].astype(jnp.int32)
        listed = jnp.concatenate([listed, ((sent[:n_listed] << 8) + sent[n_listed:])[None]], axis=0)
    plan = make_plan(lay, ids, listed, fine_coarse, coarse_slot)
    for part in partner:
        inputs = inputs + in_plane(part)
    turned = turn_own(lay, late_joined)
    blocks_coarse = []
    for part in [coarse] + near_coarse:
        blocks_coarse += [part, to_core(part)]
    turned, blocks_coarse = lax.optimization_barrier((turned, blocks_coarse))
    lines = [along(turned, d) for d in lay.line_steps()]
    for part in partner:
        turned = turn_both(lay, part, turned)
    projected = [project(lay, 0, plan, inputs[:cols], blocks_coarse)]
    held = (inputs, lines, turned, projected)
    inputs, lines, turned, projected = lax.optimization_barrier(held)
    lefts = [turned] + lines
    lefts = lefts + [to_core(part) for part in lefts]
    if two_owners:
        projected.append(project(lay, 1, plan, inputs[cols:], blocks_coarse))
    own_sum, other_sum, tiles = make_tiles(lay, plan, inputs, lefts, projected)

    def over_core(own_part, other_part):
        return (own_part + to_core(other_part).astype(jnp.float32)).reshape(lay.places, blocks, side, width)

    def shifted_part(field):
        return energy * field - spectrum_center * field

    merged = over_core(own_sum, other_sum)
    if two_owners:
        sums = jnp.stack([merged[0] + shifted_part(start), merged[near]])
        for e in range(1, near):
            sent = jnp.stack([merged[e], merged[e ^ near]]).astype(jnp.bfloat16)
            sums = sums + along(sent, e).astype(jnp.float32)
        sums = sums + along(sums.astype(jnp.bfloat16), near)[::-1].astype(jnp.float32)
    else:
        sums = merged + shifted_part(start)[None]

    firsts = sums / spectrum_half
    first = firsts[0]
    own_sum, other_sum = apply_tiles(lay, plan, tiles, in_plane(firsts.astype(jnp.bfloat16)))
    merged = over_core(own_sum, other_sum)
    last = merged[0]
    for d in range(1, lay.places):
        last = last + along(merged[d].astype(jnp.bfloat16), d).astype(jnp.float32)
    second = 2.0 * ((shifted_part(first) + last) / spectrum_half) - start
    return first.reshape(vectors.shape), second.reshape(vectors.shape)


def solution(mesh):
    in_specs = (
        P(axes, None),
        P(axes),
        P(axes, None, None),
        P("col", "row", None, None),
        P(),
        P(),
        P(axes, None),
        P(axes),
    )
    out_specs = (P(axes, None), P(axes, None))
    return jax.shard_map(
        on_device, mesh=mesh, in_specs=in_specs, out_specs=out_specs, check_vma=False
    )
```
